32 devices in a mesh: dp: 4 (over y, x), expert: 8 (over z, core).
Axes of the slice: x: 2, y: 2, z: 4, core: 2. Of those that a mesh axis runs over, the one named last changes fastest.
Arguments:
- tokens: bfloat16 [8192, 768], P(('dp', 'expert')), may hold values from -6 to 6
- cotangent: bfloat16 [8192, 768], P(('dp', 'expert')), may hold values from -6 to 6
- routes: int32 [8192, 1], P(('dp', 'expert')), may hold values from 0 to 7; in each aligned block of 256 rows (0 to 255, 256 to 511, ...) at most 64 rows name the same one
- buckets: int32 [511], replicated, may hold values from 0 to 31
- norm_attn: float32 [768], replicated, may hold values from 0.1 to 1.9
- norm_ffn: float32 [768], replicated, may hold values from 0.1 to 1.9
- rel_table: float32 [32, 12], replicated, may hold values from -6 to 6
- query_weight: bfloat16 [768, 768], P(('dp', 'expert')), may hold values from -0.078125 to 0.078125
- key_weight: bfloat16 [768, 768], P(('dp', 'expert')), may hold values from -0.078125 to 0.078125
- value_weight: bfloat16 [768, 768], P(('dp', 'expert')), may hold values from -0.21875 to 0.21875
- out_weight: bfloat16 [768, 768], P(('dp', 'expert')), may hold values from -1.75 to 1.75
- router_weight: bfloat16 [768, 8], P(('dp', 'expert')), may hold values from -0.109375 to 0.109375
- expert_in: bfloat16 [8, 768, 3072], P('expert'), may hold values from -0.21875 to 0.21875
- expert_out: bfloat16 [8, 3072, 768], P('expert'), may hold values from -3.359375 to 3.359375
Outputs:
- output: bfloat16 [8192, 768], P(('dp', 'expert'))
- input_grad: float32 [8192, 768], P(('dp', 'expert'))
- grad_norm_attn: float32 [768], replicated
- grad_norm_ffn: float32 [768], replicated
- grad_rel: float32 [32, 12], replicated
- grad_query: float32 [768, 768], P(('dp', 'expert'))
- grad_key: float32 [768, 768], P(('dp', 'expert'))
- grad_value: float32 [768, 768], P(('dp', 'expert'))
- grad_out: float32 [768, 768], P(('dp', 'expert'))
- grad_router: float32 [768, 8], P(('dp', 'expert'))
- grad_expert_in: float32 [8, 768, 3072], P('expert', None, 'dp')
- grad_expert_out: float32 [8, 3072, 768], P('expert', 'dp')
The draws below stay inside these ranges and needn't reach their ends.
Inputs may be any that keep to these rules, and one draw needn't show every extreme that they name: `routes`: within the 256 rows of one device no expert is named by more than 64 rows, and in every draw some expert is named by exactly 64 rows of some device.
All inputs are finite; a program needn't handle non-finite values.
Results may differ from the reference program's by a relative error of at most 0.017.
Values may be sent and summed in bfloat16 or wider, within the bound.
No kernel may reach another device: no remote copies, remote signals or barrier semaphores. Data moves between devices by JAX's collectives and lax.ppermute only.
A program may use at most 192 MiB of HBM per device.

```python
import math
import jax
import jax.numpy as jnp
import numpy as np
from jax import lax

D = 768
HEADS = 12
HEAD = 64
FF = 3072
BUCKETS = 32
TOK_DEV = 256
EXPERTS = 8
CAP = 64
TOKENS = 8192
DEVICES = 32


def place_ends(array, own_key, low, top_value):
    longest = array.shape.index(max(array.shape))
    spots = []
    for shift in (0, 1):
        where = [jax.random.randint(jax.random.fold_in(own_key, axis), (), 0, length) for axis, length in enumerate(array.shape)]
        where[longest] = (where[longest] + shift) % array.shape[longest]
        spots.append(tuple(where))
    return array.at[spots[0]].set(low).at[spots[1]].set(top_value)


def raised(values, key, source, target, shards_of, factor):
    owner, partner = [(jnp.arange(values.shape[position]) // (values.shape[position] // shards_of)).reshape([-1 if axis == position else 1 for axis in range(values.ndim)]) for position in (source, target)]
    chosen = jax.random.permutation(key, shards_of)[partner]
    strong = (owner == chosen) | (owner == (partner + shards_of // 2) % shards_of)
    return jnp.where(strong, factor * values, values)


def levels(key, extent, shards, least, largest):
    def one(dim, parts):
        steps = jax.random.uniform(jax.random.fold_in(jax.random.fold_in(key, 6), dim), (parts,), jnp.float32, least / len(shards), largest / len(shards))
        return jnp.repeat(jnp.exp(steps), extent[dim] // parts).reshape((-1,) + (1,) * (len(extent) - dim - 1))

    loudness = one(*shards[0])
    for cut in shards[1:]:
        loudness = loudness * one(*cut)
    return loudness


def assign_block(key, own, number, rows, count, top, most, lean):
    order = jax.random.permutation(key, count)
    crowded, common = shares(count, rows * top, most, lean, True), shares(count, rows * top, most, lean, False)
    places = jnp.arange(count)

    def named(tallies, offset_by):
        used = int((tallies > 0).sum())
        fixed = max(1, used // 4)
        passed = fixed + (places - fixed + offset_by * (used - fixed)) % max(1, count - fixed)
        return jnp.zeros((count,), jnp.int32).at[order[jnp.where(places < fixed, places, passed)]].set(jnp.asarray(tallies, jnp.int32))

    tallies = jnp.where(number % 4 == 0, named(crowded, number // 4), named(common, number - number // 4 - 1))
    mixed = jax.random.permutation(jax.random.fold_in(own, 3), count)
    source_of, receiver = mixed[0:count // 2 * 2:2], mixed[1:count // 2 * 2:2]
    margin = jnp.minimum(tallies[source_of] - 1, most - tallies[receiver]) // 2
    margin = jnp.where((source_of == order[0]) | (receiver == order[0]) | (tallies[receiver] == 0), 0, jnp.maximum(margin, 0))
    passed = jax.random.randint(jax.random.fold_in(own, 4), (count // 2,), 0, 1 << 20) % (margin + 1)
    tallies = tallies.at[source_of].add(-passed).at[receiver].add(passed)
    items = jnp.searchsorted(jnp.cumsum(tallies), jnp.arange(rows * top), side="right").astype(jnp.int32)
    table = items.reshape(top, rows).T
    table = table[jax.random.permutation(jax.random.fold_in(own, 1), rows)]
    offset_by = jax.random.randint(jax.random.fold_in(own, 2), (rows, 1), 0, top)
    return jnp.take_along_axis(table, (jnp.arange(top)[None, :] + offset_by) % top, axis=1)


def shares(number_of, total, limit, lean, full):
    weights = [(1 << 20) // math.isqrt(grade ** lean) + 1 for grade in range(1, number_of + 1)]
    largest = limit if full else min(limit, max(-(-total // number_of), total * weights[0] // sum(weights)))
    least = 1 if total - largest >= number_of - 1 else 0
    given, surplus = [largest] + [least] * (number_of - 1), total - largest - least * (number_of - 1)
    while surplus > 0:
        candidates = [i for i in range(1, number_of) if given[i] < largest] or [i for i in range(1, number_of) if given[i] < limit]
        mass, remaining = sum([weights[i] for i in candidates]), surplus
        for i in candidates:
            addition = min(limit - given[i], max(1, remaining * weights[i] // mass), surplus)
            given[i] = given[i] + addition
            surplus = surplus - addition
    return np.array(given)


def normal_values(own_key, dims, spread, reach, shards=(), kind=jnp.bfloat16):
    loudness = levels(own_key, dims, shards, -0.22, 0.18) if shards else 1.0
    result = jax.random.normal(own_key, dims, jnp.float32) * spread * loudness
    return jnp.minimum(jnp.maximum(result, -reach), reach).astype(kind)


def bell_draw_with(rng, extent, spread, bound, cuts, heavy, kind=jnp.bfloat16):
    entries = spread * jax.random.normal(rng, extent, jnp.float32)
    if cuts:
        entries = entries * levels(rng, extent, cuts, -0.22, 0.18)
    return jnp.clip(raised(entries, jax.random.fold_in(rng, 3), *heavy), -bound, bound).astype(kind)


def setup_inputs(seed: int = 0) -> dict:
    key_list = jax.random.split(jax.random.key(seed), 15)
    tokens = bell_draw_with(key_list[0], (TOKENS, D), 1.0, 6.0, ((0, 32),), (0, 1, 32, 2.75))
    cotangent = normal_values(key_list[1], (TOKENS, D), 1.0, 6.0, ((0, 32),))
    routes_keys = jax.random.split(jax.random.fold_in(key_list[2], 1), TOKENS // TOK_DEV)
    routes_turns = jax.random.permutation(jax.random.fold_in(key_list[2], 3), TOKENS // TOK_DEV)
    routes = jax.vmap(lambda own, number: assign_block(jax.random.fold_in(key_list[2], 2), own, number, TOK_DEV, EXPERTS, 1, CAP, 2))(routes_keys, routes_turns).reshape((TOKENS, 1))
    buckets = place_ends(jax.random.randint(key_list[3], (2 * TOK_DEV - 1,), 0, BUCKETS), jax.random.fold_in(key_list[3], 1), 0, BUCKETS - 1).astype(jnp.int32)
    norm_attn = jnp.clip(1.0 + 0.18 * jax.random.normal(key_list[4], (D,), jnp.float32), 0.1, 1.9)
    norm_ffn = jnp.clip(1.0 + 0.18 * jax.random.normal(key_list[5], (D,), jnp.float32), 0.1, 1.9)
    rel_table = normal_values(key_list[6], (BUCKETS, HEADS), 1.0, 6.0, (), jnp.float32)
    query_weight = normal_values(key_list[7], (D, D), (8 * D) ** -0.5, 0.078125, ((0, 32),))
    key_weight = normal_values(key_list[8], (D, D), (8 * D) ** -0.5, 0.078125, ((0, 32),))
    value_weight = normal_values(key_list[9], (D, D), D ** -0.5, 0.21875, ((0, 32),))
    out_weight = normal_values(key_list[10], (D, D), (D // 64) ** -0.5, 1.75, ((0, 32),))
    router_weight = normal_values(key_list[11], (D, EXPERTS), (4 * D) ** -0.5, 0.109375, ((0, 32),))
    expert_in = normal_values(key_list[12], (EXPERTS, D, FF), D ** -0.5, 0.21875, ((0, 8),))
    expert_out = normal_values(key_list[13], (EXPERTS, FF, D), (0.07 * EXPERTS), 3.359375, ((0, 8),))
    return dict(tokens=tokens, cotangent=cotangent, routes=routes, buckets=buckets, norm_attn=norm_attn, norm_ffn=norm_ffn, rel_table=rel_table, query_weight=query_weight, key_weight=key_weight, value_weight=value_weight, out_weight=out_weight, router_weight=router_weight, expert_in=expert_in, expert_out=expert_out)


PRECISE = lax.Precision.HIGHEST
EPSILON = 1e-06

@jax.custom_vjp
def low(v):
    return lax.optimization_barrier(v.astype(jnp.bfloat16)).astype(jnp.float32)

@jax.custom_vjp
def low_back(v):
    return v

def low_keep(v):
    return (low(v), None)

def low_pass(kept, grad):
    return (grad,)

def back_keep(v):
    return (v, None)

def back_low(kept, grad):
    return (low(grad),)
low.defvjp(low_keep, low_pass)
low_back.defvjp(back_keep, back_low)

def rms_norm(values_in, gain_in):
    return values_in * lax.rsqrt(lax.optimization_barrier(jnp.mean(values_in * values_in, axis=-1, keepdims=True)) + EPSILON) * gain_in

def gelu_tanh(values_in):
    return jax.nn.gelu(values_in, approximate=True)

def relative_bias(rel_table, buckets):
    onehot = (buckets[:, None] == jnp.arange(BUCKETS, dtype=jnp.int32)[None, :]).astype(jnp.float32)
    bias_along = jnp.dot(onehot, rel_table, precision=PRECISE)
    places = jnp.arange(TOK_DEV, dtype=jnp.int32)
    offset = places[None, :] - places[:, None] + (TOK_DEV - 1)
    return jnp.transpose(bias_along[offset], (2, 0, 1))

def attend(sequence, query_weight, key_weight, value_weight, bias_table):
    queries = low_back(low(jnp.dot(sequence, query_weight, precision=PRECISE))).reshape(TOK_DEV, HEADS, HEAD)
    keys_all = low_back(low(jnp.dot(sequence, key_weight, precision=PRECISE))).reshape(TOK_DEV, HEADS, HEAD)
    values = low_back(low(jnp.dot(sequence, value_weight, precision=PRECISE))).reshape(TOK_DEV, HEADS, HEAD)
    scores = low_back(jnp.einsum('qhd,khd->hqk', queries, keys_all, precision=PRECISE) + bias_table)
    router_probs = jax.nn.softmax(scores, axis=-1)
    mixed_rows = jnp.einsum('hqk,khd->qhd', low(router_probs), values, precision=PRECISE)
    return low_back(low(mixed_rows.reshape(TOK_DEV, D)))

def expert_ffn(row_block, weight_in, weight_out):
    pre_act = low_back(jnp.dot(row_block, weight_in, precision=PRECISE))
    hidden = low(gelu_tanh(pre_act))
    return low_back(low(jnp.dot(hidden, weight_out, precision=PRECISE)))

def slot_tables(routes):
    blocks = routes[:, 0].reshape(DEVICES, TOK_DEV)
    onehot = (blocks[:, :, None] == jnp.arange(EXPERTS, dtype=jnp.int32)[None, None, :]).astype(jnp.int32)
    slot_rank = lax.optimization_barrier(jnp.sum((jnp.cumsum(onehot, axis=1) - 1) * onehot, axis=2)).astype(jnp.int32)
    owners = jnp.broadcast_to(jnp.arange(DEVICES, dtype=jnp.int32)[:, None], blocks.shape)
    local_index = jnp.broadcast_to(jnp.arange(TOK_DEV, dtype=jnp.int32)[None, :], blocks.shape)
    slot_table = jnp.full((EXPERTS, DEVICES, CAP), TOKENS, jnp.int32)
    slot_table = slot_table.at[blocks, owners, slot_rank].set(owners * TOK_DEV + local_index)
    flat_slot = ((blocks * DEVICES + owners) * CAP + slot_rank).astype(jnp.int32)
    return (slot_table.reshape(EXPERTS, DEVICES * CAP), flat_slot.reshape(TOKENS))

def reference(tokens, cotangent, routes, buckets, norm_attn, norm_ffn, rel_table, query_weight, key_weight, value_weight, out_weight, router_weight, expert_in, expert_out):
    slot_table, flat_slot = slot_tables(routes)
    group_size = math.gcd(DEVICES, max(1, 4096 // TOK_DEV))

    def forward(inputs, gain_attn, gain_ffn, rel_values, weight_query, weight_key, weight_value, weight_proj, weight_router, weight_first, weight_second):
        bias_table = relative_bias(rel_values, buckets)
        normed = low(rms_norm(inputs, gain_attn))

        def one_group(seq_block):

            def one_sequence(sequence):
                return attend(sequence, weight_query, weight_key, weight_value, bias_table)
            mixed_rows = jax.vmap(one_sequence)(seq_block)
            return low_back(jnp.einsum('gtd,de->gte', mixed_rows, weight_proj, precision=PRECISE))
        attn_out = lax.map(jax.checkpoint(one_group), normed.reshape(DEVICES // group_size, group_size, TOK_DEV, D))
        middle = inputs + attn_out.reshape(TOKENS, D)
        ffn_in = low(rms_norm(middle, gain_ffn))
        logits = low_back(jnp.dot(ffn_in, weight_router, precision=PRECISE))
        router_probs = jax.nn.softmax(logits, axis=-1)
        gate_prob = jnp.take_along_axis(router_probs, routes, axis=1)[:, 0]
        expert_rows = low_back(ffn_in)
        padded = jnp.concatenate([expert_rows, jnp.zeros((1, D), expert_rows.dtype)], axis=0)

        def one_expert(operands):
            indices, weight_in, weight_out = operands
            return expert_ffn(padded[indices], weight_in, weight_out)
        results = lax.map(jax.checkpoint(one_expert), (slot_table, weight_first, weight_second))
        returned = results.reshape(EXPERTS * DEVICES * CAP, D)[flat_slot]
        return middle + gate_prob[:, None] * returned
    floats = (tokens.astype(jnp.float32), norm_attn.astype(jnp.float32), norm_ffn.astype(jnp.float32), rel_table.astype(jnp.float32), query_weight.astype(jnp.float32), key_weight.astype(jnp.float32), value_weight.astype(jnp.float32), out_weight.astype(jnp.float32), router_weight.astype(jnp.float32), expert_in.astype(jnp.float32), expert_out.astype(jnp.float32))
    output, pullback = jax.vjp(forward, *floats)
    gradients = pullback(cotangent.astype(jnp.float32))
    return (output.astype(jnp.bfloat16), gradients[0], gradients[1], gradients[2], gradients[3], gradients[4], gradients[5], gradients[6], gradients[7], gradients[8], gradients[9], gradients[10])
```

```python
import functools

import jax
import jax.numpy as jnp
from jax import lax
from jax.experimental import pallas as pl
from jax.experimental.pallas import tpu as pltpu
from jax.sharding import PartitionSpec as P

PRECISE = lax.Precision.HIGHEST
EPSILON = 1e-06
BF = jnp.bfloat16
F32 = jnp.float32
VMEM_BYTES = 56 * 1024 * 1024
GROUP = 256


def mm(a, b):
    return jnp.dot(a, b, preferred_element_type=F32)


def mm_nt(a, b):
    return lax.dot_general(a, b, (((1,), (1,)), ((), ())), preferred_element_type=F32)


def mm_tn(a, b):
    return lax.dot_general(a, b, (((0,), (0,)), ((), ())), preferred_element_type=F32)


def full(shape):
    return pl.BlockSpec(shape, lambda *_: (0,) * len(shape))


def cols(rows, width):
    return pl.BlockSpec((rows, width), lambda g, *_: (0, g))


def shape_of(shape, dtype):
    return jax.ShapeDtypeStruct(shape, dtype)


def params():
    return pltpu.CompilerParams(vmem_limit_bytes=VMEM_BYTES)


def cost(flops, nbytes):
    return pl.CostEstimate(flops=int(flops), bytes_accessed=int(nbytes), transcendentals=0)


def gelu_parts(v):
    square = v * v
    bent = jnp.tanh(0.7978845608 * v * (1.0 + 0.044715 * square))
    half = 0.5 * (1.0 + bent)
    slope = half + 0.5 * v * (1.0 - bent * bent) * (0.7978845608 * (1.0 + 0.134145 * square))
    return v * half, slope


def routed(rows, router, own):
    logits = mm(rows, router)
    exponent = jnp.exp(logits - jnp.max(logits, axis=-1, keepdims=True))
    router_probs = exponent / jnp.sum(exponent, axis=-1, keepdims=True)
    picked = (lax.broadcasted_iota(jnp.int32, logits.shape, 1) == own).astype(F32)
    gate = jnp.sum(router_probs * picked, axis=-1, keepdims=True)
    return router_probs, picked, gate


def route_kernel(room, nz, where_ref, routes_ref, dy_ref, order_ref, slots_t_ref, keep_ref, send_ref, perm_ref):
    tokens = routes_ref.shape[0]
    slots = slots_t_ref.shape[1]
    z, c = where_ref[0], where_ref[1]
    expert = routes_ref[...]
    lanes = lax.broadcasted_iota(jnp.int32, (tokens, 128), 1)
    picked = (lanes == expert).astype(F32)
    lower = (
        lax.broadcasted_iota(jnp.int32, (tokens, tokens), 0)
        >= lax.broadcasted_iota(jnp.int32, (tokens, tokens), 1)
    ).astype(BF)
    counts = mm(lower, picked.astype(BF))
    rank = jnp.sum(picked * (counts - 1.0), axis=1, keepdims=True).astype(jnp.int32)
    to_z, to_c = expert >> 1, expert & 1
    ahead = jnp.where(to_z >= z, to_z - z, to_z - z + nz)
    other = jnp.where(to_c == c, 0, 1)
    slot = (other * nz + ahead) * room + rank
    slots_t = (lax.broadcasted_iota(jnp.int32, (tokens, slots), 1) == slot).astype(F32).astype(BF)
    slots_t_ref[...] = slots_t
    dy_rows = mm_tn(slots_t, dy_ref[...]).astype(BF)
    keep_ref[...] = dy_rows[: slots // 2]
    send_ref[...] = dy_rows[slots // 2 :]
    width = perm_ref.shape[0]
    perm_ref[...] = (
        (lax.broadcasted_iota(jnp.int32, (width, width), 0) == order_ref[...]).astype(F32).astype(BF)
    )


def bias_kernel(along_ref, bias_ref):
    rows = bias_ref.shape[1]
    span = along_ref.shape[2]
    line = jnp.broadcast_to(along_ref[0], (rows, span))
    bias_ref[0] = pltpu.roll(line, span - rows + 1, 1, stride=1, stride_axis=0)[:, :rows]


def fill_x_first(pieces, out_ref):
    half = pieces[0].shape[0]
    for number, piece in enumerate(pieces):
        out_ref[number * half : (number + 1) * half, :] = piece[...]


def fill_y_first(pieces, out_ref):
    half = pieces[0].shape[0]
    part = half // 2
    for side in range(2):
        own, other = pieces[2 * side], pieces[2 * side + 1]
        base = side * 2 * half
        out_ref[base : base + part, :] = own[:part, :]
        out_ref[base + part : base + half, :] = other[:part, :]
        out_ref[base + half : base + half + part, :] = own[part:, :]
        out_ref[base + half + part : base + 2 * half, :] = other[part:, :]


def scores_kernel(head, *refs):
    x_ref, gain_ref, perm_ref, bias_ref = refs[:4]
    wq_refs, wk_refs = refs[4:8], refs[8:12]
    normed_ref, q_ref, k_ref, probs_ref, wq, wk = refs[12:]

    @pl.when(pl.program_id(0) == 0)
    def _():
        x = x_ref[...].astype(F32)
        scale = lax.rsqrt(jnp.mean(x * x, axis=-1, keepdims=True) + EPSILON)
        normed = (x * scale * gain_ref[...]).astype(BF)
        normed_ref[...] = mm(normed, perm_ref[...]).astype(BF)

    fill_x_first(wq_refs, wq)
    fill_y_first(wk_refs, wk)
    normed = normed_ref[...]
    q = mm(normed, wq[...]).astype(BF)
    k = mm(normed, wk[...]).astype(BF)
    q_ref[...] = q
    k_ref[...] = k
    for h in range(q.shape[1] // head):
        part = slice(h * head, (h + 1) * head)
        scores = mm_nt(q[:, part], k[:, part]) + bias_ref[h]
        exponent = jnp.exp(scores - jnp.max(scores, axis=-1, keepdims=True))
        probs_ref[h] = exponent / jnp.sum(exponent, axis=-1, keepdims=True)


def mix_kernel(head, *refs):
    normed_ref, perm_ref, probs_ref, x_ref, gain_ref, slots_t_ref, routes_ref = refs[:7]
    wv_refs, wo_refs = refs[7:11], refs[11:15]
    v_ref, mixed_ref, middle_ref, router_ref, gate_ref, keep_ref, send_ref, wv, wo, mixed = refs[15:]
    step = pl.program_id(0)
    experts = router_ref.shape[1]

    fill_x_first(wv_refs, wv)
    v = mm(normed_ref[...], wv[...]).astype(BF)
    v_ref[...] = v
    width = v.shape[1]
    rows = [
        mm(probs_ref[h].astype(BF), v[:, h * head : (h + 1) * head]) for h in range(width // head)
    ]
    mixed[step] = jnp.concatenate(rows, axis=1).astype(BF)

    @pl.when(step == pl.num_programs(0) - 1)
    def _():
        fill_y_first(wo_refs, wo)
        perm = perm_ref[...]
        every = jnp.concatenate([mixed[g] for g in range(mixed.shape[0])], axis=1)
        mixed_in_order = mm(every, perm).astype(BF)
        mixed_ref[...] = mixed_in_order
        model = x_ref.shape[1]
        middle = x_ref[...].astype(F32) + mm(mixed_in_order, wo[:, :model])
        middle_ref[...] = middle
        scale = lax.rsqrt(jnp.mean(middle * middle, axis=-1, keepdims=True) + EPSILON)
        ffn_in = (middle * scale * gain_ref[...]).astype(BF)
        router = mm(perm, wo[:, model:]).astype(BF)[:, :experts]
        router_ref[...] = router
        gate_ref[...] = routed(ffn_in, router, routes_ref[...])[2]
        rows = mm_tn(slots_t_ref[...], ffn_in).astype(BF)
        half = rows.shape[0] // 2
        keep_ref[...] = rows[:half]
        send_ref[...] = rows[half:]


def expert_kernel(own_ref, rows_ref, dy_ref, router_ref, w1_ref, w2_ref, back_ref, result_ref, router_grad_ref, branch, probs_ref, gate_ref, result, back):
    step = pl.program_id(0)
    rows = rows_ref[...]
    own = own_ref[0]

    @pl.when(step == 0)
    def _():
        router_probs, _, gate = routed(rows, router_ref[...], own)
        probs_ref[...] = router_probs
        gate_ref[...] = gate
        branch[...] = (dy_ref[...].astype(F32) * gate).astype(BF)
        result[...] = jnp.zeros_like(result)
        back[...] = jnp.zeros_like(back)

    w1, w2 = w1_ref[0], w2_ref[0]
    hidden, slope = gelu_parts(mm(rows, w1))
    result[...] += mm(hidden.astype(BF), w2)
    pre_grad = (mm_nt(branch[...], w2) * slope).astype(BF)
    back[...] += mm_nt(pre_grad, w1)

    @pl.when(step == pl.num_programs(0) - 1)
    def _():
        returned = result[...].astype(BF)
        result_ref[...] = returned
        gate_grad = jnp.sum(dy_ref[...].astype(F32) * returned.astype(F32), axis=-1, keepdims=True)
        router_probs, gate = probs_ref[...], gate_ref[...]
        picked = (lax.broadcasted_iota(jnp.int32, router_probs.shape, 1) == own).astype(F32)
        logit_grad = (router_probs * (picked - gate) * gate_grad).astype(BF)
        router_grad_ref[...] = mm_tn(rows, logit_grad)
        back_ref[...] = (back[...] + mm_nt(logit_grad, router_ref[...])).astype(BF)


def expert_grad_kernel(pieces, place_ref, *refs):
    rows_refs, dy_refs = refs[:pieces], refs[pieces : 2 * pieces]
    own_ref, router_ref, w1_ref, w2_ref, g1_ref, g2_ref, rows_all, branch_all, hidden_all, pre_all = refs[2 * pieces :]
    del place_ref
    own = own_ref[0]
    chunk = 256
    base = 0
    for rows_ref, dy_ref in zip(rows_refs, dy_refs, strict=True):

        def body(i, _, rows_ref=rows_ref, dy_ref=dy_ref, base=base):
            here = pl.ds(i * chunk, chunk)
            there = pl.ds(base + i * chunk, chunk)
            rows = rows_ref[here, :]
            gate = routed(rows, router_ref[...], own)[2]
            branch = (dy_ref[here, :].astype(F32) * gate).astype(BF)
            hidden, slope = gelu_parts(mm(rows, w1_ref[0]))
            pre_grad = mm_nt(branch, w2_ref[0]) * slope
            rows_all[there, :] = rows
            branch_all[there, :] = branch
            hidden_all[there, :] = hidden.astype(BF)
            pre_all[there, :] = pre_grad.astype(BF)
            return 0

        lax.fori_loop(0, rows_ref.shape[0] // chunk, body, 0)
        base += rows_ref.shape[0]
    g1_ref[0] = mm_tn(rows_all[...], pre_all[...])
    g2_ref[0] = mm_tn(hidden_all[...], branch_all[...])


def middle_kernel(head, *refs):
    (keep_ref, send_ref, slots_t_ref, dy_ref, middle_ref, gain_ref, mixed_ref, normed_ref, perm_ref, probs_ref) = refs[:10]
    wo_refs = refs[10:14]
    (middle_grad_ref, gain_grad_ref, mixed_grad_ref, value_grad_ref, mine_ref, theirs_ref, wo, mixed_grad) = refs[14:]
    step = pl.program_id(0)
    half = keep_ref.shape[0]
    model = dy_ref.shape[1]

    @pl.when(step == 0)
    def _():
        fill_y_first(wo_refs, wo)
        back = jnp.concatenate([keep_ref[...], send_ref[...]], axis=0)
        ffn_grad = mm(slots_t_ref[...], back)
        middle = middle_ref[...]
        scale = lax.rsqrt(jnp.mean(middle * middle, axis=-1, keepdims=True) + EPSILON)
        gain_grad_ref[...] = jnp.sum(ffn_grad * middle * scale, axis=0, keepdims=True)
        scaled = ffn_grad * gain_ref[...]
        along = jnp.mean(scaled * middle, axis=-1, keepdims=True)
        middle_grad = dy_ref[...].astype(F32) + scale * scaled - middle * (scale * scale * scale * along)
        middle_grad_ref[...] = middle_grad
        attn_grad = middle_grad.astype(BF)
        in_order = mm_nt(attn_grad, wo[...]).astype(BF)
        every = mm_nt(in_order, perm_ref[...]).astype(BF)
        mixed_grad_ref[...] = every
        for g in range(mixed_grad.shape[0]):
            mixed_grad[g] = every[:, g * GROUP : (g + 1) * GROUP]
        out_grad = mm_tn(mixed_ref[...], attn_grad)
        own = out_grad.shape[0] // 2
        mine_ref[1] = out_grad[:own]
        theirs_ref[1] = out_grad[own:].astype(BF)

    grads = mixed_grad[step]
    parts = [
        mm_tn(probs_ref[h].astype(BF), grads[:, h * head : (h + 1) * head]) for h in range(GROUP // head)
    ]
    value_grad = jnp.concatenate(parts, axis=1).astype(BF)
    value_grad_ref[...] = value_grad
    weight_grad = mm_tn(normed_ref[...], value_grad)
    own = weight_grad.shape[0] // 2
    at = pl.ds(pl.multiple_of(step * GROUP, GROUP), GROUP)
    mine_ref[0, :, at] = weight_grad[:own]
    theirs_ref[0, :, at] = weight_grad[own:].astype(BF)


def score_grad_kernel(head, mixed_grad_ref, v_ref, q_ref, k_ref, probs_ref, normed_ref, dq_ref, dk_ref, along_ref, mine_ref, theirs_ref):
    rows = q_ref.shape[0]
    flip = (
        lax.broadcasted_iota(jnp.int32, (rows, rows), 0) + lax.broadcasted_iota(jnp.int32, (rows, rows), 1)
        == rows - 1
    ).astype(F32).astype(BF)
    q_parts, k_parts = [], []
    for h in range(GROUP // head):
        part = slice(h * head, (h + 1) * head)
        probs = probs_ref[h]
        prob_grad = mm_nt(mixed_grad_ref[:, part], v_ref[:, part])
        inner = jnp.sum(probs * prob_grad, axis=-1, keepdims=True)
        score_grad = (probs * (prob_grad - inner)).astype(BF)
        q_parts.append(mm(score_grad, k_ref[:, part]))
        k_parts.append(mm_tn(score_grad, q_ref[:, part]))
        flipped = mm(flip, score_grad)
        wide = jnp.concatenate([flipped, jnp.zeros_like(flipped)], axis=1)
        along_ref[h] = jnp.sum(pltpu.roll(wide, 0, 1, stride=1, stride_axis=0), axis=0, keepdims=True)
    dq = jnp.concatenate(q_parts, axis=1).astype(BF)
    dk = jnp.concatenate(k_parts, axis=1).astype(BF)
    dq_ref[...] = dq
    dk_ref[...] = dk
    normed = normed_ref[...]
    for number, grad in enumerate((dq, dk)):
        weight_grad = mm_tn(normed, grad)
        own = weight_grad.shape[0] // 2
        mine_ref[number] = weight_grad[:own]
        theirs_ref[number] = weight_grad[own:].astype(BF)


def input_kernel(*refs):
    dq_ref, dk_ref, dv_ref, x_ref, gain_ref, perm_ref, middle_grad_ref = refs[:7]
    wq_refs, wk_refs, wv_refs = refs[7:11], refs[11:15], refs[15:19]
    input_grad_ref, gain_grad_ref, weight = refs[19:]
    fill_x_first(wq_refs, weight)
    total = mm_nt(dq_ref[...], weight[...])
    fill_y_first(wk_refs, weight)
    total += mm_nt(dk_ref[...], weight[...])
    fill_x_first(wv_refs, weight)
    total += mm_nt(dv_ref[...], weight[...])
    perm = perm_ref[...]
    high = total.astype(BF)
    low = (total - high.astype(F32)).astype(BF)
    normed_grad = mm_nt(high, perm) + mm_nt(low, perm)
    x = x_ref[...].astype(F32)
    scale = lax.rsqrt(jnp.mean(x * x, axis=-1, keepdims=True) + EPSILON)
    gain_grad_ref[...] = jnp.sum(normed_grad * x * scale, axis=0, keepdims=True)
    scaled = normed_grad * gain_ref[...]
    along = jnp.mean(scaled * x, axis=-1, keepdims=True)
    input_grad_ref[...] = middle_grad_ref[...] + scale * scaled - x * (scale * scale * scale * along)


class Places:
    def __init__(self):
        self.experts = lax.axis_size("expert")
        self.nz = self.experts // 2
        self.dp = lax.axis_size("dp")
        self.near = self.nz <= 4
        me = lax.axis_index("expert")
        self.z, self.c = me // 2, me % 2
        self.row = lax.axis_index("dp")
        self.columns = [[2 * z + c for z in range(self.nz)] for c in range(2)]

    def core(self, v):
        return lax.ppermute(v, "expert", [(i, i ^ 1) for i in range(self.experts)])

    def x(self, v):
        return lax.ppermute(v, "dp", [(i, i ^ 1) for i in range(self.dp)])

    def y(self, v):
        return lax.ppermute(v, "dp", [(i, i ^ 2) for i in range(self.dp)])

    def shift(self, v, k):
        size = self.experts
        return lax.ppermute(v, "expert", [(i, (i + 2 * k) % size) for i in range(size)])

    def shifts(self):
        middle = self.nz // 2
        return [middle] + [k for k in range(1, self.nz) if k != middle]

    def gather_z(self, v):
        if self.near:
            got = {k: self.shift(v, k) for k in self.shifts()}
            return jnp.concatenate([v] + [got[k] for k in range(1, self.nz)], axis=0)
        return lax.all_gather(v, "expert", axis=0, tiled=True, axis_index_groups=self.columns)

    def z_order(self):
        steps = jnp.arange(self.nz, dtype=jnp.int32)
        return (self.z - steps) % self.nz if self.near else steps

    def scatter_z(self, v):
        if self.near:
            size = v.shape[0] // self.nz
            total = v[:size]
            low = v.astype(BF)
            for k in self.shifts():
                total = total + self.shift(low[k * size : (k + 1) * size], -k).astype(F32)
            return total
        blocks = v.astype(BF).reshape(self.nz, v.shape[0] // self.nz, v.shape[1])
        got = lax.all_to_all(
            blocks, "expert", split_axis=0, concat_axis=0, tiled=True, axis_index_groups=self.columns
        )
        return jnp.sum(got.astype(F32), axis=0)

    def send_out(self, keep, send):
        got = self.core(send)
        room = keep.shape[0] // self.nz
        both = jnp.concatenate(
            [v.reshape(self.nz, room, keep.shape[1]) for v in (keep, got)], axis=1
        )
        if self.near:
            moved = {k: self.shift(both[k], k) for k in self.shifts()}
            return jnp.concatenate([both[0]] + [moved[k] for k in range(1, self.nz)], axis=0)
        placed = jnp.roll(both, self.z, axis=0)
        moved = lax.all_to_all(
            placed, "expert", split_axis=0, concat_axis=0, tiled=True, axis_index_groups=self.columns
        )
        return moved.reshape(-1, keep.shape[1])

    def send_home(self, rows):
        blocks = rows.reshape(self.nz, rows.shape[0] // self.nz, rows.shape[1])
        if self.near:
            moved = {k: self.shift(blocks[k], -k) for k in self.shifts()}
            both = jnp.stack([blocks[0]] + [moved[k] for k in range(1, self.nz)], axis=0)
        else:
            moved = lax.all_to_all(
                blocks, "expert", split_axis=0, concat_axis=0, tiled=True, axis_index_groups=self.columns
            )
            both = jnp.roll(moved, -self.z, axis=0)
        room = both.shape[1] // 2
        keep, other = both[:, :room].reshape(-1, rows.shape[1]), both[:, room:].reshape(-1, rows.shape[1])
        return keep, self.core(other)

    def gather_two(self, first, second):
        width = first.shape[1]
        line = self.gather_z(jnp.concatenate([first, second], axis=1))
        a, b = line[:, :width], line[:, width:]
        ax, by = self.x(a), self.y(b)
        a2, b2 = jnp.concatenate([a, ax], axis=0), jnp.concatenate([b, by], axis=0)
        a3, b3 = self.y(a2), self.x(b2)
        return (a2, a3, self.core(a2), self.core(a3)), (b2, b3, self.core(b2), self.core(b3))

    def scatter_two(self, mine, theirs):
        total = mine + self.core(theirs).astype(F32)
        half = total.shape[1] // 2
        quarter = half // 2
        low = total.astype(BF)
        a = total[0, :half] + self.y(low[0, half:]).astype(F32)
        b_low = low[1].reshape(2, 2, quarter, -1)
        b = total[1].reshape(2, 2, quarter, -1)[:, 0] + self.x(b_low[:, 1]).astype(F32)
        a = a[:quarter] + self.x(a[quarter:].astype(BF)).astype(F32)
        b = b[0] + self.y(b[1].astype(BF)).astype(F32)
        both = self.scatter_z(jnp.concatenate([a, b], axis=1))
        return both[:, : a.shape[1]], both[:, a.shape[1] :]

    def gather_rows(self, v):
        half = v.shape[0] // 2
        a, b = v[:half], v[half:]
        ax, by = self.x(a), self.y(b)
        return [v, ax, by, self.y(jnp.concatenate([a, ax], axis=0)), self.x(jnp.concatenate([b, by], axis=0))]

    def sum_small(self, v):
        v = v + self.core(v)
        v = v + self.x(v)
        v = v + self.y(v)
        if not self.near:
            return lax.psum(v, "expert", axis_index_groups=self.columns)
        got = [self.shift(v, k) for k in self.shifts()]
        parts = jnp.stack([v] + [got[self.shifts().index(k)] for k in range(1, self.nz)], axis=0)
        parts = jnp.roll(parts[::-1], self.z + 1, axis=0)
        return jnp.sum(parts, axis=0)


def per_device(
    tokens,
    cotangent,
    routes,
    buckets,
    norm_attn,
    norm_ffn,
    rel_table,
    query_weight,
    key_weight,
    value_weight,
    out_weight,
    router_weight,
    expert_in,
    expert_out,
):
    at = Places()
    rows, model = tokens.shape
    head_count = rel_table.shape[1]
    head = model // head_count
    bucket_count = rel_table.shape[0]
    experts = router_weight.shape[1]
    shard = query_weight.shape[0]
    nz = at.nz
    room = max(2, 2 * rows // at.experts)
    slots = experts * room
    half = slots // 2
    groups = model // GROUP
    per_group = GROUP // head
    hidden = expert_in.shape[2]
    gain_attn, gain_ffn = norm_attn.reshape(1, model), norm_ffn.reshape(1, model)
    own = lax.axis_index("expert").astype(jnp.int32).reshape(1)
    smem = pl.BlockSpec(memory_space=pltpu.SMEM)

    core_of = at.c ^ jnp.arange(2, dtype=jnp.int32)
    row_of = at.row ^ jnp.arange(4, dtype=jnp.int32)
    device_of = (
        row_of[None, :, None] * at.experts + at.z_order()[None, None, :] * 2 + core_of[:, None, None]
    )
    order = (
        device_of[..., None] * shard + jnp.arange(shard, dtype=jnp.int32)
    ).reshape(1, model).astype(jnp.int32)

    qk_pieces = at.gather_two(query_weight, key_weight)
    padded_router = jnp.pad(router_weight, ((0, 0), (0, 128 - experts)))
    vo_pieces = at.gather_two(
        value_weight, jnp.concatenate([out_weight, padded_router], axis=1)
    )
    wq, wk = qk_pieces
    wv, wo = vo_pieces

    slots_t, dy_keep, dy_send, perm = pl.pallas_call(
        functools.partial(route_kernel, room, nz),
        out_shape=(
            shape_of((rows, slots), BF),
            shape_of((half, model), BF),
            shape_of((half, model), BF),
            shape_of((model, model), BF),
        ),
        in_specs=[smem] + [pl.BlockSpec(memory_space=pltpu.VMEM)] * 3,
        compiler_params=params(),
        cost_estimate=cost(2 * rows * slots * model, 4 * rows * model),
        name="route",
    )(jnp.stack([at.z, at.c]).astype(jnp.int32), routes, cotangent, order)
    dy_rows = at.send_out(dy_keep, dy_send)

    onehot_bucket = (buckets[:, None] == jnp.arange(bucket_count, dtype=jnp.int32)[None, :]).astype(F32)
    along = jnp.pad(jnp.dot(onehot_bucket, rel_table, precision=PRECISE).T, ((0, 0), (0, 1)))
    span = along.shape[1]
    bias = pl.pallas_call(
        bias_kernel,
        grid=(head_count,),
        out_shape=shape_of((head_count, rows, rows), F32),
        in_specs=[pl.BlockSpec((1, 1, span), lambda g: (g, 0, 0))],
        out_specs=pl.BlockSpec((1, rows, rows), lambda g: (g, 0, 0)),
        compiler_params=params(),
        cost_estimate=cost(1 << 20, 4 * head_count * rows * rows),
        name="bias",
    )(along.reshape(head_count, 1, span))

    quarter = wq[0].shape[0]
    head_block = pl.BlockSpec((per_group, rows, rows), lambda g: (g, 0, 0))
    normed, q, k, probs = pl.pallas_call(
        functools.partial(scores_kernel, head),
        grid=(groups,),
        out_shape=(
            shape_of((rows, model), BF),
            shape_of((rows, model), BF),
            shape_of((rows, model), BF),
            shape_of((head_count, rows, rows), F32),
        ),
        in_specs=[full((rows, model)), full((1, model)), full((model, model)), head_block]
        + [cols(quarter, GROUP)] * 8,
        out_specs=(full((rows, model)), cols(rows, GROUP), cols(rows, GROUP), head_block),
        scratch_shapes=[pltpu.VMEM((model, GROUP), BF), pltpu.VMEM((model, GROUP), BF)],
        compiler_params=params(),
        cost_estimate=cost(6 * rows * model * model, 12 * model * model),
        name="scores",
    )(tokens, gain_attn, perm, bias, *wq, *wk)

    wide = wo[0].shape[1]
    v, mixed, middle, router, gate, keep, send = pl.pallas_call(
        functools.partial(mix_kernel, head),
        grid=(groups,),
        out_shape=(
            shape_of((rows, model), BF),
            shape_of((rows, model), BF),
            shape_of((rows, model), F32),
            shape_of((model, experts), BF),
            shape_of((rows, 1), F32),
            shape_of((half, model), BF),
            shape_of((half, model), BF),
        ),
        in_specs=[
            full((rows, model)),
            full((model, model)),
            head_block,
            full((rows, model)),
            full((1, model)),
            full((rows, slots)),
            full((rows, 1)),
        ]
        + [cols(quarter, GROUP)] * 4
        + [full((quarter, wide))] * 4,
        out_specs=(
            cols(rows, GROUP),
            full((rows, model)),
            full((rows, model)),
            full((model, experts)),
            full((rows, 1)),
            full((half, model)),
            full((half, model)),
        ),
        scratch_shapes=[
            pltpu.VMEM((model, GROUP), BF),
            pltpu.VMEM((model, wide), BF),
            pltpu.VMEM((groups, rows, GROUP), BF),
        ],
        compiler_params=params(),
        cost_estimate=cost(8 * rows * model * model, 12 * model * model),
        name="mix",
    )(normed, perm, probs, tokens, gain_ffn, slots_t, routes, *wv, *wo)

    rows_all = at.send_out(keep, send)
    part = 512
    back, returned, router_grad = pl.pallas_call(
        expert_kernel,
        grid=(hidden // part,),
        out_shape=(
            shape_of((slots, model), BF),
            shape_of((slots, model), BF),
            shape_of((model, experts), F32),
        ),
        in_specs=[
            smem,
            full((slots, model)),
            full((slots, model)),
            full((model, experts)),
            pl.BlockSpec((1, model, part), lambda f: (0, 0, f)),
            pl.BlockSpec((1, part, model), lambda f: (0, f, 0)),
        ],
        out_specs=(full((slots, model)), full((slots, model)), full((model, experts))),
        scratch_shapes=[
            pltpu.VMEM((slots, model), BF),
            pltpu.VMEM((slots, experts), F32),
            pltpu.VMEM((slots, 1), F32),
            pltpu.VMEM((slots, model), F32),
            pltpu.VMEM((slots, model), F32),
        ],
        compiler_params=params(),
        cost_estimate=cost(8 * slots * model * hidden, 4 * model * hidden),
        name="expert",
    )(own, rows_all, dy_rows, router, expert_in, expert_out)

    back_keep, back_send = at.send_home(back)
    returned_keep, returned_send = at.send_home(returned)
    rows_dp = at.gather_rows(rows_all)
    dy_dp = at.gather_rows(dy_rows)
    every = sum(v.shape[0] for v in rows_dp)
    slice_width = hidden // at.dp
    grad_in, grad_out_w = pl.pallas_call(
        functools.partial(expert_grad_kernel, len(rows_dp)),
        grid_spec=pltpu.PrefetchScalarGridSpec(
            num_scalar_prefetch=1,
            grid=(1,),
            in_specs=[full(v.shape) for v in rows_dp]
            + [full(v.shape) for v in dy_dp]
            + [
                smem,
                full((model, experts)),
                pl.BlockSpec((1, model, slice_width), lambda g, place: (0, 0, place[0])),
                pl.BlockSpec((1, slice_width, model), lambda g, place: (0, place[0], 0)),
            ],
            out_specs=(full((1, model, slice_width)), full((1, slice_width, model))),
            scratch_shapes=[
                pltpu.VMEM((every, model), BF),
                pltpu.VMEM((every, model), BF),
                pltpu.VMEM((every, slice_width), BF),
                pltpu.VMEM((every, slice_width), BF),
            ],
        ),
        out_shape=(shape_of((1, model, slice_width), F32), shape_of((1, slice_width, model), F32)),
        compiler_params=params(),
        cost_estimate=cost(8 * every * model * slice_width, 20 * model * slice_width),
        name="expert_grads",
    )(at.row.astype(jnp.int32).reshape(1), *rows_dp, *dy_dp, own, router, expert_in, expert_out)

    pair = model // 2
    middle_grad, gain_ffn_grad, mixed_grad, value_grad, vo_mine, vo_theirs = pl.pallas_call(
        functools.partial(middle_kernel, head),
        grid=(groups,),
        out_shape=(
            shape_of((rows, model), F32),
            shape_of((1, model), F32),
            shape_of((rows, model), BF),
            shape_of((rows, model), BF),
            shape_of((2, pair, model), F32),
            shape_of((2, pair, model), BF),
        ),
        in_specs=[
            full((half, model)),
            full((half, model)),
            full((rows, slots)),
            full((rows, model)),
            full((rows, model)),
            full((1, model)),
            full((rows, model)),
            full((rows, model)),
            full((model, model)),
            head_block,
        ]
        + [pl.BlockSpec((quarter, model), lambda g: (0, 0))] * 4,
        out_specs=(
            full((rows, model)),
            full((1, model)),
            full((rows, model)),
            cols(rows, GROUP),
            full((2, pair, model)),
            full((2, pair, model)),
        ),
        scratch_shapes=[pltpu.VMEM((model, model), BF), pltpu.VMEM((groups, rows, GROUP), BF)],
        compiler_params=params(),
        cost_estimate=cost(10 * rows * model * model, 12 * model * model),
        name="middle",
    )(back_keep, back_send, slots_t, cotangent, middle, gain_ffn, mixed, normed, perm, probs, *wo)
    grad_value, grad_proj = at.scatter_two(vo_mine, vo_theirs)

    dq, dk, along_grad, qk_mine, qk_theirs = pl.pallas_call(
        functools.partial(score_grad_kernel, head),
        grid=(groups,),
        out_shape=(
            shape_of((rows, model), BF),
            shape_of((rows, model), BF),
            shape_of((head_count, 1, span), F32),
            shape_of((2, pair, model), F32),
            shape_of((2, pair, model), BF),
        ),
        in_specs=[cols(rows, GROUP)] * 4 + [head_block, full((rows, model))],
        out_specs=(
            cols(rows, GROUP),
            cols(rows, GROUP),
            pl.BlockSpec((per_group, 1, span), lambda g: (g, 0, 0)),
            pl.BlockSpec((2, pair, GROUP), lambda g: (0, 0, g)),
            pl.BlockSpec((2, pair, GROUP), lambda g: (0, 0, g)),
        ),
        compiler_params=params(),
        cost_estimate=cost(8 * rows * model * model, 12 * model * model),
        name="score_grads",
    )(mixed_grad, v, q, k, probs, normed)
    grad_query, grad_key = at.scatter_two(qk_mine, qk_theirs)

    input_grad, gain_attn_grad = pl.pallas_call(
        input_kernel,
        grid=(1,),
        out_shape=(shape_of((rows, model), F32), shape_of((1, model), F32)),
        in_specs=[full((rows, model))] * 4
        + [full((1, model)), full((model, model)), full((rows, model))]
        + [full((quarter, model))] * 8
        + [pl.BlockSpec((quarter, model), lambda g: (0, 0))] * 4,
        out_specs=(full((rows, model)), full((1, model))),
        scratch_shapes=[pltpu.VMEM((model, model), BF)],
        compiler_params=params(),
        cost_estimate=cost(10 * rows * model * model, 12 * model * model),
        name="inputs",
    )(dq, dk, value_grad, tokens, gain_attn, perm, middle_grad, *wq, *wk, *wv)

    rel_grad = jnp.dot(along_grad[:, 0, : span - 1], onehot_bucket, precision=PRECISE).T
    small = [gain_attn_grad, gain_ffn_grad, rel_grad, router_grad]
    flat = jnp.concatenate([v.reshape(-1) for v in small])
    summed = at.sum_small(jnp.pad(flat, (0, -flat.shape[0] % 1024)).reshape(-1, 128)).reshape(-1)
    outs, base = [], 0
    for v in small:
        outs.append(summed[base : base + v.size].reshape(v.shape))
        base += v.size
    device = at.row * at.experts + lax.axis_index("expert")
    grad_router = lax.dynamic_slice_in_dim(outs[3], device * shard, shard, axis=0)

    expert_result = mm(slots_t, jnp.concatenate([returned_keep, returned_send], axis=0))
    output = (middle + gate * expert_result).astype(BF)
    return (
        output,
        input_grad,
        outs[0].reshape(model),
        outs[1].reshape(model),
        outs[2],
        grad_query,
        grad_key,
        grad_value,
        grad_proj,
        grad_router,
        grad_in,
        grad_out_w,
    )


def solution(mesh):
    in_specs = (
        P(("dp", "expert"), None),
        P(("dp", "expert"), None),
        P(("dp", "expert"), None),
        P(),
        P(),
        P(),
        P(),
        P(("dp", "expert"), None),
        P(("dp", "expert"), None),
        P(("dp", "expert"), None),
        P(("dp", "expert"), None),
        P(("dp", "expert"), None),
        P("expert", None, None),
        P("expert", None, None),
    )
    out_specs = (
        P(("dp", "expert"), None),
        P(("dp", "expert"), None),
        P(),
        P(),
        P(),
        P(("dp", "expert"), None),
        P(("dp", "expert"), None),
        P(("dp", "expert"), None),
        P(("dp", "expert"), None),
        P(("dp", "expert"), None),
        P("expert", None, "dp"),
        P("expert", "dp", None),
    )
    return jax.shard_map(
        per_device, mesh=mesh, in_specs=in_specs, out_specs=out_specs, check_vma=False
    )
```

```python
import functools

import jax
import jax.numpy as jnp
from jax import lax
from jax.experimental import pallas as pl
from jax.experimental.pallas import tpu as pltpu
from jax.sharding import PartitionSpec as P

PRECISE = lax.Precision.HIGHEST
EPSILON = 1e-06
BF = jnp.bfloat16
F32 = jnp.float32
VMEM_BYTES = 20 * 1024 * 1024
GROUP = 256
FAR_FIRST = (2, 3, 1)


def mm(a, b):
    return jnp.dot(a, b, preferred_element_type=F32)


def mm_nt(a, b):
    return lax.dot_general(a, b, (((1,), (1,)), ((), ())), preferred_element_type=F32)


def mm_tn(a, b):
    return lax.dot_general(a, b, (((0,), (0,)), ((), ())), preferred_element_type=F32)


def full(shape):
    return pl.BlockSpec(shape, lambda *_: (0,) * len(shape))


def cols(rows, width):
    return pl.BlockSpec((rows, width), lambda g, *_: (0, g))


def shape_of(shape, dtype):
    return jax.ShapeDtypeStruct(shape, dtype)


def params():
    return pltpu.CompilerParams(vmem_limit_bytes=VMEM_BYTES)


def cost(flops, nbytes):
    return pl.CostEstimate(flops=1024, bytes_accessed=1024, transcendentals=0)


def after(v, *others):
    return lax.optimization_barrier((v, *others))[0]


def all_after(values, *others):
    return list(lax.optimization_barrier((*values, *others))[: len(values)])


def gelu_parts(v):
    square = v * v
    bent = jnp.tanh(0.7978845608 * v * (1.0 + 0.044715 * square))
    half = 0.5 * (1.0 + bent)
    slope = half + 0.5 * v * (1.0 - bent * bent) * (0.7978845608 * (1.0 + 0.134145 * square))
    return v * half, slope


def gate_of(rows, router, picked):
    logits = mm(rows, router)
    exponent = jnp.exp(logits - jnp.max(logits, axis=-1, keepdims=True))
    router_probs = exponent / jnp.sum(exponent, axis=-1, keepdims=True)
    return router_probs, jnp.sum(router_probs * picked, axis=-1, keepdims=True)


def one_lane(shape, lane):
    return (lax.broadcasted_iota(jnp.int32, shape, 1) == lane).astype(F32)


def pack_kernel(*refs):
    out_ref = refs[-1]
    base = 0
    for ref in refs[:-2]:
        out_ref[:, base : base + ref.shape[1]] = ref[...]
        base += ref.shape[1]
    router = refs[-2][...]
    out_ref[:, base:] = jnp.concatenate(
        [router, jnp.zeros((router.shape[0], out_ref.shape[1] - base - router.shape[1]), router.dtype)], axis=1
    )


def route_kernel(
    room,
    nz,
    near,
    where_ref,
    routes_ref,
    dy_ref,
    order_ref,
    x_ref,
    gain_ref,
    next_gain_ref,
    slots_ref,
    slots_t_ref,
    keep_ref,
    send_ref,
    perm_ref,
    normed_ref,
    picked_ref,
    gain_out_ref,
    gain_next_ref,
):
    slots, tokens = slots_ref.shape
    experts = picked_ref.shape[1]
    z, c = where_ref[0], where_ref[1]
    expert = routes_ref[...]
    lanes = lax.broadcasted_iota(jnp.int32, (128, tokens), 0)
    picked = (lanes == expert).astype(F32)
    upper = (
        lax.broadcasted_iota(jnp.int32, (tokens, tokens), 0)
        <= lax.broadcasted_iota(jnp.int32, (tokens, tokens), 1)
    ).astype(BF)
    counts = mm(picked.astype(BF), upper)
    rank = jnp.sum(picked * (counts - 1.0), axis=0, keepdims=True).astype(jnp.int32)
    to_z, to_c = expert >> 1, expert & 1
    ahead = to_z ^ z if near else to_z
    other = jnp.where(to_c == c, 0, 1)
    slot = (other * nz + ahead) * room + rank
    chosen = (lax.broadcasted_iota(jnp.int32, (slots, tokens), 0) == slot).astype(F32)
    slots_ref[...] = chosen.astype(BF)
    slots_t_ref[...] = chosen.T.astype(BF)
    dy_rows = mm(slots_ref[...], dy_ref[...]).astype(BF)
    keep_ref[...] = dy_rows[: slots // 2]
    send_ref[: slots // 2, :] = dy_rows[slots // 2 :]
    picked_ref[...] = picked.T[:, :experts]
    width = perm_ref.shape[0]
    perm = (lax.broadcasted_iota(jnp.int32, (width, width), 0) == order_ref[...]).astype(F32).astype(BF)
    perm_ref[...] = perm
    x = x_ref[...].astype(F32)
    scale = lax.rsqrt(jnp.mean(x * x, axis=-1, keepdims=True) + EPSILON)
    normed = mm((x * scale * gain_ref[...]).astype(BF), perm).astype(BF)
    normed_ref[...] = normed
    send_ref[slots // 2 :, : width // 2] = normed[: tokens // 2, width // 2 :]
    send_ref[slots // 2 :, width // 2 :] = normed[tokens // 2 :, width // 2 :]
    gain_out_ref[...] = gain_ref[...]
    gain_next_ref[...] = next_gain_ref[...]


def bias_kernel(buckets_ref, table_ref, bias_ref, along):
    heads, rows = bias_ref.shape[0], bias_ref.shape[1]
    half, span = rows // 2, buckets_ref.shape[1]
    step = pl.program_id(0)

    @pl.when(step == 0)
    def _():
        every = table_ref.shape[0]
        onehot = (lax.broadcasted_iota(jnp.int32, (every, span), 0) == buckets_ref[...]).astype(F32)
        values = lax.dot_general(
            table_ref[...], onehot, (((0,), (0,)), ((), ())), precision=PRECISE, preferred_element_type=F32
        )
        for h in range(along.shape[0]):
            along[h] = values[h : h + 1]

    for h in range(heads):
        line = jnp.broadcast_to(along[step * heads + h], (half, span))
        turned = pltpu.roll(line, span - rows + 1, 1, stride=1, stride_axis=0)
        bias_ref[h, :half, :] = turned[:, :rows]
        bias_ref[h, half:, :half] = turned[:, span - half :]
        bias_ref[h, half:, half:] = turned[:, :half]


def fill_x_first(pieces, out_ref):
    half = pieces[0].shape[0]
    for number, piece in enumerate(pieces):
        out_ref[number * half : (number + 1) * half, :] = piece[...]


def fill_y_first(pieces, out_ref, starts=(0, 0, 0, 0)):
    half = pieces[0].shape[0]
    part = half // 2
    width = out_ref.shape[1]
    for side in range(2):
        own, other = pieces[2 * side], pieces[2 * side + 1]
        at, at_other = [slice(start, start + width) for start in starts[2 * side : 2 * side + 2]]
        base = side * 2 * half
        out_ref[base : base + part, :] = own[:part, at]
        out_ref[base + part : base + half, :] = other[:part, at_other]
        out_ref[base + half : base + half + part, :] = own[part:, at]
        out_ref[base + half + part : base + 2 * half, :] = other[part:, at_other]


def near_kernel(qv_ref, qv_x_ref, ko_ref, ko_y_ref, qv_near_ref, ko_near_ref, both_ref):
    part, width = qv_ref.shape
    for number, (left, right) in enumerate(((qv_ref, ko_ref), (qv_x_ref, ko_y_ref))):
        at = slice(number * part, (number + 1) * part)
        qv_near_ref[at, :] = left[...]
        ko_near_ref[at, :] = right[...]
        both_ref[at, :width] = left[...]
        both_ref[at, width:] = right[...]


def attend_kernel(head, *refs):
    normed_ref, bias_ref, perm_ref, x_ref, gain_ref, slots_ref, picked_ref = refs[:7]
    wq_refs, wv_refs, wk_refs, ko_refs = refs[7:11], refs[11:15], refs[15:19], refs[19:23]
    q_ref, k_ref, v_ref, probs_ref, mixed_ref, mixed_other_ref = refs[23:29]
    middle_ref, router_ref, gate_ref, keep_ref, send_ref = refs[29:34]
    wq, wk, wv, wo, mixed = refs[34:]
    step = pl.program_id(0)
    experts = router_ref.shape[1]
    model = x_ref.shape[1]

    fill_x_first(wq_refs, wq)
    fill_y_first(wk_refs, wk)
    fill_x_first(wv_refs, wv)
    normed = normed_ref[...]
    q = mm(normed, wq[...]).astype(BF)
    k = mm(normed, wk[...]).astype(BF)
    v = mm(normed, wv[...]).astype(BF)
    q_ref[...] = q
    k_ref[...] = k
    v_ref[...] = v
    rows = []
    for h in range(q.shape[1] // head):
        part = slice(h * head, (h + 1) * head)
        scores = mm_nt(q[:, part], k[:, part]) + bias_ref[h]
        exponent = jnp.exp(scores - jnp.max(scores, axis=-1, keepdims=True))
        probs = exponent / jnp.sum(exponent, axis=-1, keepdims=True)
        probs_ref[h] = probs
        rows.append(mm(probs.astype(BF), v[:, part]))
    mixed[step] = jnp.concatenate(rows, axis=1).astype(BF)

    @pl.when(step == pl.num_programs(0) - 1)
    def _():
        fill_y_first(ko_refs, wo, (model, model, 3 * model, model))
        perm = perm_ref[...]
        every = jnp.concatenate([mixed[g] for g in range(mixed.shape[0])], axis=1)
        mixed_in_order = mm(every, perm).astype(BF)
        mixed_ref[...] = mixed_in_order[:, : model // 2]
        mixed_other_ref[...] = mixed_in_order[:, model // 2 :]
        middle = x_ref[...].astype(F32) + mm(mixed_in_order, wo[:, :model])
        middle_ref[...] = middle
        scale = lax.rsqrt(jnp.mean(middle * middle, axis=-1, keepdims=True) + EPSILON)
        ffn_in = (middle * scale * gain_ref[...]).astype(BF)
        router = mm(perm, wo[:, model:]).astype(BF)[:, :experts]
        router_ref[...] = router
        rows = mm(slots_ref[...], ffn_in).astype(BF)
        gate_ref[...] = gate_of(ffn_in, router, picked_ref[...])[1]
        half = rows.shape[0] // 2
        keep_ref[...] = rows[:half]
        send_ref[...] = rows[half:]


def join(refs, out_ref):
    base = 0
    for ref in refs:
        size = ref.shape[0]
        out_ref[base : base + size, :] = ref[...]
        base += size


def part_out(v, refs):
    base = 0
    for ref in refs:
        size = ref.shape[0]
        ref[...] = v[base : base + size]
        base += size


def expert_kernel(pieces, extra, own_ref, *refs):
    rows_refs, dy = refs[:pieces], refs[pieces]
    router_ref, w1_ref, w2_ref = refs[pieces + 1 : pieces + 4]
    refs = refs[pieces + 4 :]
    extra_refs, refs = refs[: sum(extra)], refs[sum(extra) :]
    back_refs, result_refs = refs[:pieces], refs[pieces : 2 * pieces]
    router_grad_ref, rows = refs[2 * pieces : 2 * pieces + 2]
    extra_out, refs = refs[2 * pieces + 2 : 2 * pieces + 2 + len(extra)], refs[2 * pieces + 2 + len(extra) :]
    branch, probs_ref, gate_ref, result, back = refs
    step = pl.program_id(0)
    own = own_ref[0]

    @pl.when(step == 0)
    def _():
        join(rows_refs, rows)
        base = 0
        for count, out_ref in zip(extra, extra_out, strict=True):
            join(extra_refs[base : base + count], out_ref)
            base += count
        router_probs, gate = gate_of(rows[...], router_ref[...], one_lane(probs_ref.shape, own))
        probs_ref[...] = router_probs
        gate_ref[...] = gate
        branch[...] = (dy[...].astype(F32) * gate).astype(BF)
        result[...] = jnp.zeros_like(result)
        back[...] = jnp.zeros_like(back)

    w1, w2 = w1_ref[0], w2_ref[0]
    hidden, slope = gelu_parts(mm(rows[...], w1))
    result[...] += mm(hidden.astype(BF), w2)
    pre_grad = (mm_nt(branch[...], w2) * slope).astype(BF)
    back[...] += mm_nt(pre_grad, w1)

    @pl.when(step == pl.num_programs(0) - 1)
    def _():
        returned = result[...].astype(BF)
        part_out(returned, result_refs)
        gate_grad = jnp.sum(dy[...].astype(F32) * returned.astype(F32), axis=-1, keepdims=True)
        router_probs, gate = probs_ref[...], gate_ref[...]
        picked = one_lane(router_probs.shape, own)
        logit_grad = (router_probs * (picked - gate) * gate_grad).astype(BF)
        router_grad_ref[...] = mm_tn(logit_grad, rows[...])
        part_out((back[...] + mm_nt(logit_grad, router_ref[...])).astype(BF), back_refs)


def expert_grad_kernel(pieces, more, place_ref, *refs):
    del place_ref
    rows_refs, dy_refs, refs = refs[:pieces], refs[pieces : 2 * pieces], refs[2 * pieces :]
    own_ref, router_ref, w1_ref, w2_ref = refs[:4]
    g1_ref, g2_ref, rows_all, branch_all = refs[-4:]

    @pl.when(pl.program_id(0) == 0)
    def _():
        join(rows_refs, rows_all)
        join(dy_refs, branch_all)
        picked = one_lane((rows_all.shape[0], router_ref.shape[1]), own_ref[0])
        gate = gate_of(rows_all[...], router_ref[...], picked)[1]
        branch_all[...] = (branch_all[...].astype(F32) * gate).astype(BF)

    rows, branch = rows_all[...], branch_all[...]
    hidden, slope = gelu_parts(mm(rows, w1_ref[0]))
    pre_grad = (mm_nt(branch, w2_ref[0]) * slope).astype(BF)
    g1, g2 = mm_tn(rows, pre_grad), mm_tn(hidden.astype(BF), branch)
    if more:
        g1, g2 = g1 + refs[4][0], g2 + refs[5][0]
    g1_ref[0] = g1
    g2_ref[0] = g2


def middle_kernel(head, pieces, *refs):
    keep_refs, refs = refs[:pieces], refs[pieces:]
    (send_ref, slots_t_ref, dy_ref, middle_ref, gain_ref, perm_ref, probs_ref, other_ref) = refs[:8]
    ko_refs = refs[8:12]
    (middle_grad_ref, gain_grad_ref, mixed_grad_ref, grads_ref, wo, mixed_grad) = refs[12:]
    rows, model = dy_ref.shape
    step = pl.program_id(0)
    keep_rows = send_ref.shape[0] // pieces

    @pl.when(step == 0)
    def _():
        fill_y_first(ko_refs, wo, (model, model, 3 * model, model))
        back = jnp.concatenate([ref[:keep_rows, :] for ref in keep_refs] + [send_ref[...]], axis=0)
        ffn_grad = mm(slots_t_ref[...], back)
        middle = middle_ref[...]
        scale = lax.rsqrt(jnp.mean(middle * middle, axis=-1, keepdims=True) + EPSILON)
        gain_grad_ref[...] = jnp.sum(ffn_grad * middle * scale, axis=0, keepdims=True)
        scaled = ffn_grad * gain_ref[...]
        along = jnp.mean(scaled * middle, axis=-1, keepdims=True)
        middle_grad = dy_ref[...].astype(F32) + scale * scaled - middle * (scale * scale * scale * along)
        middle_grad_ref[...] = middle_grad
        attn_grad = middle_grad.astype(BF)
        grads_ref[rows : 2 * rows, :] = attn_grad
        grads_ref[2 * rows :, : model // 2] = other_ref[: rows // 2, :]
        grads_ref[2 * rows :, model // 2 :] = other_ref[rows // 2 :, :]
        in_order = mm_nt(attn_grad, wo[...]).astype(BF)
        every = mm_nt(in_order, perm_ref[...]).astype(BF)
        mixed_grad_ref[...] = every
        for g in range(mixed_grad.shape[0]):
            mixed_grad[g] = every[:, g * GROUP : (g + 1) * GROUP]

    grads = mixed_grad[step]
    parts = [
        mm_tn(probs_ref[h].astype(BF), grads[:, h * head : (h + 1) * head]) for h in range(GROUP // head)
    ]
    value_grad = jnp.concatenate(parts, axis=1).astype(BF)
    at = pl.ds(pl.multiple_of(step * GROUP, GROUP), GROUP)
    grads_ref[:rows, at] = value_grad


def weight_grad_kernel(normed_ref, side_ref, mixed_ref, vo_ref, vo_side_ref, qk_ref, qk_side_ref, *outs):
    a_ref, a_low_ref, b_ref, b_low_ref = outs
    rows = normed_ref.shape[0]
    width = side_ref.shape[1] // 2
    model = normed_ref.shape[1]
    half, part = width // 2, width // 4

    def unpack(v):
        return [v[:, :width], v[:, width:]]

    normed = jnp.concatenate([normed_ref[:, :width], *unpack(side_ref[...])], axis=0)
    mixed = jnp.concatenate([mixed_ref[...], *unpack(vo_side_ref[2 * rows :, :])], axis=0)
    for number, (left, own, side) in enumerate(
        ((normed, vo_ref, vo_side_ref), (normed, qk_ref, qk_side_ref), (mixed, vo_ref, vo_side_ref), (normed, qk_ref, qk_side_ref))
    ):
        here = slice(0, rows) if number < 2 else slice(rows, 2 * rows)
        total = mm_tn(left, jnp.concatenate([own[here, :], side[here, :]], axis=0))
        at = slice(number % 2 * model, (number % 2 + 1) * model)
        if number < 2:
            a_ref[:, at] = total[:half]
            a_low_ref[:, at] = total[half:].astype(BF)
        else:
            b_ref[:part, at] = total[:part]
            b_ref[part:, at] = total[half : half + part]
            b_low_ref[:part, at] = total[part:half].astype(BF)
            b_low_ref[part:, at] = total[half + part :].astype(BF)


def fold_near_kernel(a_ref, a_got_ref, b_ref, b_got_ref, small_ref, small_got_ref, a2_ref, a2_low_ref, b2_ref, b2_low_ref):
    a = a_ref[...] + a_got_ref[...].astype(F32)
    b = b_ref[...] + b_got_ref[...].astype(F32)
    small = small_ref[...] + small_got_ref[...]
    half = a.shape[0] // 2
    a2_ref[...] = a[:half]
    a2_low_ref[:half, :] = a[half:].astype(BF)
    a2_low_ref[half:, :] = jnp.concatenate([small, jnp.zeros_like(small)], axis=1).astype(BF)
    b2_ref[...] = b[:half]
    b2_low_ref[...] = b[half:].astype(BF)


def fold_sums(a_ref, a_low_ref, a_got_ref, b_ref, b_got_ref):
    rows = a_ref.shape[0]
    a = a_ref[...] + a_got_ref[:rows, :].astype(F32)
    b = b_ref[...] + b_got_ref[...].astype(F32)
    model = a.shape[1] // 2
    return a, b, a_low_ref[rows:, :model].astype(F32) + a_got_ref[rows:, :model].astype(F32)


def fold_far_kernel(a_ref, a_low_ref, a_got_ref, b_ref, b_got_ref, keep_ref, *low_refs):
    a, b, small = fold_sums(a_ref, a_low_ref, a_got_ref, b_ref, b_got_ref)
    model = a.shape[1] // 2
    shard = a.shape[0] // 4
    for k in range(4):
        rows = slice(k * shard, (k + 1) * shard)
        blocks = [v[rows, half * model : (half + 1) * model] for v in (a, b) for half in range(2)]
        if k:
            low_refs[k - 1][...] = jnp.concatenate([small, *blocks], axis=0).astype(BF)
        else:
            keep_ref[...] = jnp.concatenate(blocks, axis=0)


def fold_last_kernel(keep_ref, own_ref, *refs):
    got, outs = [ref[...].astype(F32) for ref in refs[:3]], refs[3:]
    shard = outs[0].shape[0]
    first = outs[4].shape[0]
    total = keep_ref[...] + ((got[0][first:] + got[1][first:]) + got[2][first:])
    for number in range(4):
        outs[number][...] = total[number * shard : (number + 1) * shard]
    outs[4][...] = (own_ref[...][:first].astype(F32) + got[0][:first]) + (got[1][:first] + got[2][:first])


def score_grad_kernel(head, mixed_grad_ref, v_ref, q_ref, k_ref, probs_ref, grads_ref, along_ref):
    rows = q_ref.shape[0]
    flip = (
        lax.broadcasted_iota(jnp.int32, (rows, rows), 0) + lax.broadcasted_iota(jnp.int32, (rows, rows), 1)
        == rows - 1
    ).astype(F32).astype(BF)
    q_parts, k_parts = [], []
    for h in range(GROUP // head):
        part = slice(h * head, (h + 1) * head)
        probs = probs_ref[h]
        prob_grad = mm_nt(mixed_grad_ref[:, part], v_ref[:, part])
        inner = jnp.sum(probs * prob_grad, axis=-1, keepdims=True)
        score_grad = (probs * (prob_grad - inner)).astype(BF)
        q_parts.append(mm(score_grad, k_ref[:, part]))
        k_parts.append(mm_tn(score_grad, q_ref[:, part]))
        flipped = mm(flip, score_grad)
        half = rows // 2
        upper, lower = flipped[:half], flipped[half:]
        wide = jnp.concatenate(
            [upper[:, :half], upper[:, half:] + lower[:, :half], lower[:, half:], jnp.zeros_like(upper[:, :half])], axis=1
        )
        along_ref[h] = jnp.sum(pltpu.roll(wide, 0, 1, stride=1, stride_axis=0), axis=0, keepdims=True)
    grads_ref[:rows, :] = jnp.concatenate(q_parts, axis=1).astype(BF)
    grads_ref[rows:, :] = jnp.concatenate(k_parts, axis=1).astype(BF)


def input_kernel(table_rows, *refs):
    qk_ref, vo_ref, x_ref, gain_ref, perm_ref, middle_grad_ref = refs[:6]
    along_ref, buckets_ref, gain_next_ref, router_a_ref, router_b_ref = refs[6:11]
    qv_refs, wk_refs = refs[11:15], refs[15:19]
    input_grad_ref, small_ref, weight, wide = refs[19:]
    rows = x_ref.shape[0]
    experts, heads = router_a_ref.shape[0], along_ref.shape[0]
    every = table_rows
    onehot = (
        lax.broadcasted_iota(jnp.int32, (every, buckets_ref.shape[1]), 0) == buckets_ref[...]
    ).astype(F32)
    model = x_ref.shape[1]
    small_ref[...] = jnp.zeros_like(small_ref)
    small_ref[:experts, :] = router_a_ref[...] + router_b_ref[...]
    small_ref[experts + 1 : experts + 2, :] = gain_next_ref[...]
    along = jnp.concatenate([along_ref[h] for h in range(heads)], axis=0)
    table = lax.dot_general(
        along, onehot, (((1,), (1,)), ((), ())), precision=PRECISE, preferred_element_type=F32
    )
    small_ref[experts + 2 : experts + 3, : heads * every] = jnp.concatenate(
        [table[h : h + 1] for h in range(heads)], axis=1
    )
    fill_x_first(qv_refs, wide)
    total = mm_nt(jnp.concatenate([qk_ref[:rows, :], vo_ref[:rows, :]], axis=1), wide[...])
    fill_y_first(wk_refs, weight)
    total += mm_nt(qk_ref[rows:, :], weight[...])
    perm = perm_ref[...]
    high = total.astype(BF)
    low = (total - high.astype(F32)).astype(BF)
    normed_grad = mm_nt(high, perm) + mm_nt(low, perm)
    x = x_ref[...].astype(F32)
    scale = lax.rsqrt(jnp.mean(x * x, axis=-1, keepdims=True) + EPSILON)
    small_ref[experts : experts + 1, :] = jnp.sum(normed_grad * x * scale, axis=0, keepdims=True)
    scaled = normed_grad * gain_ref[...]
    along = jnp.mean(scaled * x, axis=-1, keepdims=True)
    input_grad_ref[...] = middle_grad_ref[...] + scale * scaled - x * (scale * scale * scale * along)


class Places:
    def __init__(self):
        self.experts = lax.axis_size("expert")
        self.nz = self.experts // 2
        self.dp = lax.axis_size("dp")
        self.near = self.nz == 4
        me = lax.axis_index("expert")
        self.z, self.c = me // 2, me % 2
        self.row = lax.axis_index("dp")
        self.columns = [[2 * z + c for z in range(self.nz)] for c in range(2)]

    def core(self, v):
        return lax.ppermute(v, "expert", [(i, i ^ 1) for i in range(self.experts)])

    def x(self, v):
        return lax.ppermute(v, "dp", [(i, i ^ 1) for i in range(self.dp)])

    def y(self, v):
        return lax.ppermute(v, "dp", [(i, i ^ 2) for i in range(self.dp)])

    def far(self, v, k):
        return lax.ppermute(v, "expert", [(i, i ^ (2 * k)) for i in range(self.experts)])

    def apart(self, v):
        return lax.all_to_all(
            v, "expert", split_axis=0, concat_axis=0, tiled=True, axis_index_groups=self.columns
        )

    def gather_z(self, v):
        if self.near:
            got = {k: self.far(v, k) for k in FAR_FIRST}
            return jnp.concatenate([v, got[1], got[2], got[3]], axis=0)
        return lax.all_gather(v, "expert", axis=0, tiled=True, axis_index_groups=self.columns)

    def z_order(self):
        steps = jnp.arange(self.nz, dtype=jnp.int32)
        return self.z ^ steps if self.near else steps

    def scatter_z(self, v):
        size = v.shape[0] // self.nz
        if self.near:
            total = v[:size]
            low = v.astype(BF)
            for k in FAR_FIRST:
                total = total + self.far(low[k * size : (k + 1) * size], k).astype(F32)
            return total
        got = self.apart(v.astype(BF).reshape(self.nz, size, v.shape[1]))
        mine = lax.dynamic_slice_in_dim(v, self.z * size, size, axis=0)
        steps = jnp.arange(self.nz, dtype=jnp.int32)[:, None, None]
        return mine + jnp.sum(jnp.where(steps == self.z, 0.0, got.astype(F32)), axis=0)

    def swap(self, blocks):
        got = {k: self.far(blocks[k], k) for k in FAR_FIRST}
        return [blocks[0], got[1], got[2], got[3]]

    def swap_relay(self, blocks, hold):
        size = blocks[0].shape[0]
        first = self.far(jnp.concatenate([blocks[2], blocks[3]], axis=0), 2)
        onward = after(jnp.concatenate([blocks[1], first[size:]], axis=0), *hold)
        second = self.far(onward, 1)
        return [blocks[0], second[:size], first[:size], second[size:]], onward

    def by_z(self, keep, got):
        room = keep.shape[0] // self.nz
        both = jnp.concatenate([v.reshape(self.nz, room, keep.shape[1]) for v in (keep, got)], axis=1)
        return [both[k] for k in range(4)] if self.near else both

    def halves(self, moved):
        moved = moved.reshape(-1, moved.shape[-1])
        half = moved.shape[0] // 2
        return [moved[:half]], [moved[half:]]

    def to_owners(self, keep, got, hold):
        blocks = self.by_z(keep, got)
        if self.near:
            blocks = all_after([blocks[k] for k in range(4)], *hold)
            two, one = self.far(blocks[2], 2), self.far(blocks[1], 1)
            three = self.far(after(blocks[3], two), 3)
            return [blocks[0], two], [one, three]
        return self.halves(self.apart(blocks))

    def send_more(self, blocks, k, hold):
        return self.far(after(blocks[k], *hold), k) if self.near else blocks

    def from_owners(self, first, second):
        width = first[0].shape[1]
        both = self.apart(jnp.concatenate([*first, *second], axis=0).reshape(self.nz, -1, width))
        room = both.shape[1] // 2
        return [both[:, :room].reshape(-1, width)], both[:, room:].reshape(-1, width)

    def to_senders(self, first, second):
        if self.near:
            two = self.far(first[1], 2)
            one, three = all_after(second, two)
            three, one = self.far(three, 3), self.far(one, 1)
            moved = [first[0], one, two, three]
            room = one.shape[0] // 2
            return moved, self.core(jnp.concatenate([v[room:] for v in moved], axis=0))
        keep, other = self.from_owners(first, second)
        return keep, self.core(other)

    def gather_far(self, a, b):
        return self.y(a), self.x(b)


def per_device(
    tokens,
    cotangent,
    routes,
    buckets,
    norm_attn,
    norm_ffn,
    rel_table,
    query_weight,
    key_weight,
    value_weight,
    out_weight,
    router_weight,
    expert_in,
    expert_out,
):
    at = Places()
    rows, model = tokens.shape
    head_count = rel_table.shape[1]
    head = model // head_count
    bucket_count = rel_table.shape[0]
    experts = router_weight.shape[1]
    shard = query_weight.shape[0]
    nz = at.nz
    room = max(2, 2 * rows // at.experts)
    slots = experts * room
    half = slots // 2
    groups = model // GROUP
    per_group = GROUP // head
    hidden = expert_in.shape[2]

    def in_hbm(*values):
        return [pltpu.with_memory_space_constraint(v, pltpu.HBM) for v in values]

    expert_in, expert_out = in_hbm(expert_in, expert_out)
    own = lax.axis_index("expert").astype(jnp.int32).reshape(1)
    smem = pl.BlockSpec(memory_space=pltpu.SMEM)

    core_of = at.c ^ jnp.arange(2, dtype=jnp.int32)
    row_of = at.row ^ jnp.arange(4, dtype=jnp.int32)
    device_of = (
        row_of[None, :, None] * at.experts + at.z_order()[None, None, :] * 2 + core_of[:, None, None]
    )
    order = (
        device_of[..., None] * shard + jnp.arange(shard, dtype=jnp.int32)
    ).reshape(1, model).astype(jnp.int32)

    shards = (query_weight, value_weight, key_weight, out_weight, router_weight)
    packed = pl.pallas_call(
        pack_kernel,
        out_shape=shape_of((shard, 4 * model + 128), BF),
        in_specs=[pl.BlockSpec(memory_space=pltpu.VMEM)] * 5,
        out_specs=pl.BlockSpec(memory_space=pltpu.VMEM),
        name="pack",
    )(*shards)
    line = at.gather_z(packed)
    span = 2 * rows
    bucket_line = jnp.pad(buckets, (0, 1), constant_values=-1).reshape(1, span)
    slots_map, slots_t, dy_keep, dy_send, perm, normed, picked, gain_attn, gain_ffn = pl.pallas_call(
        functools.partial(route_kernel, room, nz, at.near),
        out_shape=(
            shape_of((slots, rows), BF),
            shape_of((rows, slots), BF),
            shape_of((half, model), BF),
            shape_of((half + rows // 2, model), BF),
            shape_of((model, model), BF),
            shape_of((rows, model), BF),
            shape_of((rows, experts), F32),
            shape_of((1, model), F32),
            shape_of((1, model), F32),
        ),
        in_specs=[smem] + [pl.BlockSpec(memory_space=pltpu.VMEM)] * 6,
        compiler_params=params(),
        cost_estimate=cost(2 * rows * slots * model, 4 * rows * model),
        name="route",
    )(
        jnp.stack([at.z, at.c]).astype(jnp.int32),
        routes.reshape(1, rows),
        cotangent,
        order,
        tokens,
        norm_attn.reshape(1, model),
        norm_ffn.reshape(1, model),
    )
    dy_got = at.core(dy_send)
    normed_side = dy_got[half:]
    dy_got = dy_got[:half]
    qv, ko = line[:, : 2 * model], line[:, 2 * model :]
    qv, ko = all_after([qv, ko], dy_got)
    dy_keep, dy_got = all_after([dy_keep, dy_got], qv, ko)
    part_rows = qv.shape[0]
    dy_blocks = at.by_z(dy_keep, dy_got)
    dy_one = at.send_more(dy_blocks, 1, (dy_blocks,))
    qv_near, ko_near, both_near = pl.pallas_call(
        near_kernel,
        out_shape=tuple(shape_of((2 * part_rows, width), BF) for width in (2 * model, 2 * model + 128, 4 * model + 128)),
        in_specs=[pl.BlockSpec(memory_space=pltpu.VMEM)] * 4,
        out_specs=(pl.BlockSpec(memory_space=pltpu.VMEM),) * 3,
        compiler_params=params(),
        name="near",
    )(after(qv, dy_one), at.x(qv), ko, at.y(ko))
    bias = pl.pallas_call(
        bias_kernel,
        grid=(groups,),
        out_shape=shape_of((head_count, rows, rows), F32),
        in_specs=[full((1, span)), full((bucket_count, head_count))],
        out_specs=pl.BlockSpec((per_group, rows, rows), lambda g: (g, 0, 0)),
        scratch_shapes=[pltpu.VMEM((head_count, 1, span), F32)],
        compiler_params=params(),
        cost_estimate=cost(1 << 20, 4 * head_count * rows * rows),
        name="bias",
    )(after(bucket_line, qv, ko), rel_table)
    qv_far, ko_far = at.gather_far(*all_after([qv_near, ko_near], bias))
    both_side = at.core(both_near)
    dy_two = at.send_more(dy_blocks, 2, (qv_near, dy_one))
    qv_far, ko_far, dy_two = all_after([qv_far, ko_far, dy_two], both_side)
    dy_three = at.send_more(dy_blocks, 3, (qv_far, ko_far, dy_two))
    qv_pieces = (qv_near, qv_far, both_side, at.core(qv_far))
    ko_pieces = (ko_near, ko_far, both_side, at.core(ko_far))
    if at.near:
        dy_a = jnp.concatenate([dy_blocks[0], dy_two], axis=0)
    else:
        (dy_a,), (dy_b,) = at.halves(at.apart(dy_blocks))
    dy_a_later = after(dy_a, qv_far, ko_far)
    dy_ax, dy_ay = at.x(dy_a_later), at.y(dy_a_later)

    quarter = qv_near.shape[0]
    wide = ko_near.shape[1]
    side_wide = both_side.shape[1]
    head_block = pl.BlockSpec((per_group, rows, rows), lambda g: (g, 0, 0))
    later = pl.BlockSpec((quarter, GROUP), lambda g: (0, groups + g))
    side_k = pl.BlockSpec((quarter, GROUP), lambda g: (0, 2 * groups + g))
    first_k = cols(quarter, GROUP)
    ko_full = [full((quarter, wide)), full((quarter, wide)), full((quarter, side_wide)), full((quarter, wide))]
    q, k, v, probs, mixed, mixed_other, middle, router, gate, keep, send = pl.pallas_call(
        functools.partial(attend_kernel, head),
        grid=(groups,),
        out_shape=(shape_of((rows, model), BF),) * 3
        + (
            shape_of((head_count, rows, rows), F32),
            shape_of((rows, model // 2), BF),
            shape_of((rows, model // 2), BF),
            shape_of((rows, model), F32),
            shape_of((model, experts), BF),
            shape_of((rows, 1), F32),
            shape_of((half, model), BF),
            shape_of((half, model), BF),
        ),
        in_specs=[
            full((rows, model)),
            head_block,
            full((model, model)),
            full((rows, model)),
            full((1, model)),
            full((slots, rows)),
            full((rows, experts)),
        ]
        + [cols(quarter, GROUP)] * 4
        + [later] * 4
        + [first_k, first_k, side_k, first_k]
        + ko_full,
        out_specs=(cols(rows, GROUP),) * 3
        + (
            head_block,
            full((rows, model // 2)),
            full((rows, model // 2)),
            full((rows, model)),
            full((model, experts)),
            full((rows, 1)),
            full((half, model)),
            full((half, model)),
        ),
        scratch_shapes=[pltpu.VMEM((model, GROUP), BF)] * 3
        + [pltpu.VMEM((model, wide - model), BF), pltpu.VMEM((groups, rows, GROUP), BF)],
        compiler_params=params(),
        cost_estimate=cost(8 * rows * model * model, 12 * model * model),
        name="attend",
    )(normed, bias, perm, *in_hbm(tokens), gain_ffn, *in_hbm(slots_map), picked, *qv_pieces, *qv_pieces, *ko_pieces, *ko_pieces)

    got = at.core(after(send, dy_three))
    first, second = at.to_owners(keep, got, (dy_ax, dy_ay))
    if at.near:
        dy_b = jnp.concatenate([dy_one, dy_three], axis=0)
    dy_b_later = after(dy_b, got, dy_ax, dy_ay)
    dy_by, dy_bx = at.y(dy_b_later), at.x(dy_b_later)
    part = 1024

    def expert(rows_list, dy_rows, router_in, extra=()):
        sizes = [v.shape[0] for v in rows_list]
        count = sum(sizes)
        flat = [v for group in extra for v in group]
        joined = [sum(v.shape[0] for v in group) for group in extra]
        outs = pl.pallas_call(
            functools.partial(expert_kernel, len(sizes), tuple(len(group) for group in extra)),
            grid=(hidden // part,),
            out_shape=tuple(shape_of((n, model), BF) for n in sizes * 2)
            + (shape_of((experts, model), F32),)
            + tuple(shape_of((n, model), BF) for n in [count, *joined]),
            in_specs=[smem]
            + [full((n, model)) for n in [*sizes, count]]
            + [
                full((model, experts)),
                pl.BlockSpec((1, model, part), lambda f: (0, 0, f)),
                pl.BlockSpec((1, part, model), lambda f: (0, f, 0)),
            ]
            + [full(v.shape) for v in flat],
            out_specs=tuple(full((n, model)) for n in sizes * 2)
            + (full((experts, model)),)
            + tuple(full((n, model)) for n in [count, *joined]),
            scratch_shapes=[
                pltpu.VMEM((count, model), BF),
                pltpu.VMEM((count, experts), F32),
                pltpu.VMEM((count, 1), F32),
                pltpu.VMEM((count, model), F32),
                pltpu.VMEM((count, model), F32),
            ],
            compiler_params=params(),
            cost_estimate=cost(8 * count * model * hidden, 4 * model * hidden),
            name="expert",
        )(own, *rows_list, dy_rows, router_in, expert_in, expert_out, *flat)
        n = len(sizes)
        return list(outs[:n]), list(outs[n : 2 * n]), outs[2 * n], outs[2 * n + 1 :]

    dy_ax_later, dy_by_later = all_after([dy_ax, dy_by], first[-1], dy_bx)
    dy_axy, dy_byx = at.y(dy_ax_later), at.x(dy_by_later)
    back_a, returned_a, router_grad_a, (rows_a,) = expert(first, dy_a, after(router, dy_by, dy_bx))
    rows_ax, rows_ay = at.x(rows_a), at.y(rows_a)
    back_b, returned_b, router_grad_b, (rows_b,) = expert(second, dy_b, after(router, router_grad_a, dy_axy, dy_byx))
    rows_b_later = after(rows_b, rows_ax, rows_ay)
    rows_by, rows_bx = at.y(rows_b_later), at.x(rows_b_later)
    back_keep, back_send = at.to_senders(back_a, back_b)

    slice_width = hidden // at.dp
    place = at.row.astype(jnp.int32).reshape(1)

    steps = slice_width // GROUP

    def expert_grads(rows_list, dy_list, router_in, before):
        sizes = [v.shape[0] for v in rows_list]
        count = sum(sizes)
        outs = (
            pl.BlockSpec((1, model, GROUP), lambda g, place: (0, 0, g)),
            pl.BlockSpec((1, GROUP, model), lambda g, place: (0, g, 0)),
        )
        return pl.pallas_call(
            functools.partial(expert_grad_kernel, len(sizes), bool(before)),
            grid_spec=pltpu.PrefetchScalarGridSpec(
                num_scalar_prefetch=1,
                grid=(steps,),
                in_specs=[full((n, model)) for n in sizes * 2]
                + [
                    smem,
                    full((model, experts)),
                    pl.BlockSpec((1, model, GROUP), lambda g, place: (0, 0, place[0] * steps + g)),
                    pl.BlockSpec((1, GROUP, model), lambda g, place: (0, place[0] * steps + g, 0)),
                ]
                + list(outs if before else ()),
                out_specs=outs,
                scratch_shapes=[pltpu.VMEM((count, model), BF), pltpu.VMEM((count, model), BF)],
            ),
            out_shape=(pltpu.HBM((1, model, slice_width), F32), pltpu.HBM((1, slice_width, model), F32)),
            compiler_params=params(),
            cost_estimate=cost(8 * count * model * slice_width, 20 * model * slice_width),
            name="expert_grads",
        )(place, *in_hbm(*rows_list, *dy_list), own, router_in, expert_in, expert_out, *before)

    rows_axy, rows_byx = at.y(after(rows_ax, rows_by, rows_bx, back_send)), at.x(after(rows_by, rows_bx, back_send))

    middle_grad, gain_ffn_grad, mixed_grad, vo_grads = pl.pallas_call(
        functools.partial(middle_kernel, head, len(back_keep)),
        grid=(groups,),
        out_shape=(
            shape_of((rows, model), F32),
            shape_of((1, model), F32),
            shape_of((rows, model), BF),
            shape_of((2 * rows + rows // 2, model), BF),
        ),
        in_specs=[full(v.shape) for v in back_keep]
        + [
            full((half, model)),
            full((rows, slots)),
            full((rows, model)),
            full((rows, model)),
            full((1, model)),
            full((model, model)),
            head_block,
            full((rows, model // 2)),
        ]
        + ko_full,
        out_specs=(
            full((rows, model)),
            full((1, model)),
            full((rows, model)),
            full((2 * rows + rows // 2, model)),
        ),
        scratch_shapes=[pltpu.VMEM((model, model), BF), pltpu.VMEM((groups, rows, GROUP), BF)],
        compiler_params=params(),
        cost_estimate=cost(10 * rows * model * model, 12 * model * model),
        name="middle",
    )(*back_keep, back_send, slots_t, cotangent, middle, after(gain_ffn, rows_by, rows_bx), perm, probs, mixed_other, *ko_pieces)
    vo_side = at.core(vo_grads)
    qk_grads, along_grad = pl.pallas_call(
        functools.partial(score_grad_kernel, head),
        grid=(groups,),
        out_shape=(shape_of((2 * rows, model), BF), shape_of((head_count, 1, span), F32)),
        in_specs=[cols(rows, GROUP)] * 4 + [head_block],
        out_specs=(cols(2 * rows, GROUP), pl.BlockSpec((per_group, 1, span), lambda g: (g, 0, 0))),
        compiler_params=params(),
        cost_estimate=cost(8 * rows * model * model, 12 * model * model),
        name="score_grads",
    )(mixed_grad, v, q, k, probs)
    qk_side = at.core(after(qk_grads, vo_side, rows_axy, rows_byx))
    small_rows = -(-(experts + 3) // 16) * 16
    input_grad, small = pl.pallas_call(
        functools.partial(input_kernel, bucket_count),
        grid=(1,),
        out_shape=(shape_of((rows, model), F32), shape_of((small_rows, model), F32)),
        in_specs=[full((2 * rows, model)), full((2 * rows + rows // 2, model))]
        + [full((rows, model)), full((1, model)), full((model, model)), full((rows, model))]
        + [full((head_count, 1, span)), full((1, span)), full((1, model))]
        + [full((experts, model))] * 2
        + [full((quarter, 2 * model))] * 4
        + [pl.BlockSpec((quarter, model), lambda g, at=at_k: (0, at)) for at_k in (0, 0, 2, 0)],
        out_specs=(full((rows, model)), full((small_rows, model))),
        scratch_shapes=[pltpu.VMEM((model, model), BF), pltpu.VMEM((model, 2 * model), BF)],
        compiler_params=params(),
        cost_estimate=cost(10 * rows * model * model, 12 * model * model),
        name="inputs",
    )(
        qk_grads,
        vo_grads,
        tokens,
        gain_attn,
        perm,
        middle_grad,
        along_grad,
        bucket_line,
        gain_ffn_grad,
        router_grad_a,
        router_grad_b,
        *qv_pieces,
        *ko_pieces,
    )
    quarter_rows = model // 4

    def vmem_call(kernel, name, shapes, *ins):
        return pl.pallas_call(
            kernel,
            out_shape=tuple(shape_of(*v) for v in shapes),
            in_specs=[pl.BlockSpec(v.shape, lambda: (0, 0)) for v in ins],
            out_specs=tuple(pl.BlockSpec(v[0], lambda: (0, 0)) for v in shapes),
            compiler_params=params(),
            name=name,
        )(*ins)

    pair = 2 * model
    a, a_low, b, b_low = vmem_call(
        weight_grad_kernel,
        "weight_grads",
        [((quarter_rows, pair), F32), ((quarter_rows, pair), BF)] * 2,
        normed,
        normed_side,
        mixed,
        vo_grads,
        vo_side,
        qk_grads,
        qk_side,
    )
    small = small + after(at.core(small), a_low)
    a_got, b_got = at.y(a_low), at.x(b_low)
    small_got = at.y(small)
    if at.near:
        home_two = at.far(after(returned_a[1], a_low, b_low), 2)
    else:
        home_two = at.apart(jnp.concatenate([*returned_a, *returned_b], axis=0).reshape(nz, -1, model))
    near_sums = expert_grads(
        [rows_a, rows_b, rows_ax, rows_by, rows_ay, rows_bx],
        [dy_a, dy_b, dy_ax, dy_by, dy_ay, dy_bx],
        after(router, a_low, b_low),
        (),
    )
    eighth = quarter_rows // 2
    a, a_low, b, b_low = vmem_call(
        fold_near_kernel,
        "fold_near",
        [((eighth, pair), F32), ((eighth + small_rows, pair), BF), ((eighth, pair), F32), ((eighth, pair), BF)],
        a,
        after(a_got, near_sums[0], home_two),
        b,
        b_got,
        small,
        small_got,
    )
    a_got, b_got = at.x(a_low), at.y(b_low)
    far_sums = expert_grads(
        [rows_axy, rows_byx],
        [dy_axy, dy_byx],
        after(router, a_low, b_low),
        near_sums,
    )
    if at.near:
        home = [at.far(v, k) for v, k in zip(all_after([returned_b[1], returned_b[0]], a_low, b_low), (3, 1))]
        home_blocks = [returned_a[0], home[1], home_two, home[0]]
        room = half // nz
        returned_keep = home_blocks
        returned_other = jnp.concatenate([v[room:] for v in home_blocks], axis=0)
    else:
        room = home_two.shape[1] // 2
        returned_keep = [home_two[:, :room].reshape(half, model)]
        returned_other = home_two[:, room:].reshape(half, model)
    if at.near:
        keep_sum, *low = vmem_call(
            fold_far_kernel,
            "fold_far",
            [((4 * shard, model), F32)] + [((small_rows + 4 * shard, model), BF)] * 3,
            a,
            a_low,
            after(a_got, far_sums[0], *home),
            b,
            b_got,
        )
        hold = keep_sum
        got_z = {k: at.far(low[k - 1], k) for k in FAR_FIRST}
    else:
        a = a + a_got[:eighth].astype(F32)
        b = b + b_got.astype(F32)
        summed = (a_low[eighth:].astype(F32) + a_got[eighth:].astype(F32))[:, :model]
        hold = jnp.concatenate([a, b], axis=1)
        sums = at.scatter_z(hold)
        grad_value, grad_query, grad_proj, grad_key = [sums[:, n * model : (n + 1) * model] for n in range(4)]
        summed = lax.psum(summed, "expert", axis_index_groups=at.columns)
    returned_send = at.core(after(returned_other, hold))
    grad_in, grad_out_w = far_sums
    keep_rows = half // len(returned_keep)
    expert_result = mm(
        slots_t,
        jnp.concatenate([v[:keep_rows] for v in returned_keep] + [returned_send], axis=0),
    )
    output = (middle + gate * expert_result).astype(BF)
    if at.near:
        grad_value, grad_query, grad_proj, grad_key, summed = vmem_call(
            fold_last_kernel,
            "fold_last",
            [((shard, model), F32)] * 4 + [((small_rows, model), F32)],
            after(keep_sum, output),
            low[0],
            *[got_z[k] for k in (1, 2, 3)],
        )
    device = at.row * at.experts + lax.axis_index("expert")
    grad_router = lax.dynamic_slice_in_dim(summed[:experts], device * shard, shard, axis=1).T
    return (
        output,
        input_grad,
        summed[experts],
        summed[experts + 1],
        summed[experts + 2, : head_count * bucket_count].reshape(head_count, bucket_count).T,
        grad_query,
        grad_key,
        grad_value,
        grad_proj,
        grad_router,
        grad_in,
        grad_out_w,
    )


def solution(mesh):
    in_specs = (
        P(("dp", "expert"), None),
        P(("dp", "expert"), None),
        P(("dp", "expert"), None),
        P(),
        P(),
        P(),
        P(),
        P(("dp", "expert"), None),
        P(("dp", "expert"), None),
        P(("dp", "expert"), None),
        P(("dp", "expert"), None),
        P(("dp", "expert"), None),
        P("expert", None, None),
        P("expert", None, None),
    )
    out_specs = (
        P(("dp", "expert"), None),
        P(("dp", "expert"), None),
        P(),
        P(),
        P(),
        P(("dp", "expert"), None),
        P(("dp", "expert"), None),
        P(("dp", "expert"), None),
        P(("dp", "expert"), None),
        P(("dp", "expert"), None),
        P("expert", None, "dp"),
        P("expert", "dp", None),
    )
    return jax.shard_map(
        per_device, mesh=mesh, in_specs=in_specs, out_specs=out_specs, check_vma=False
    )
```

```python
import functools

import jax
import jax.numpy as jnp
from jax import lax
from jax.experimental import pallas as pl
from jax.experimental.pallas import tpu as pltpu
from jax.sharding import PartitionSpec as P

PRECISE = lax.Precision.HIGHEST
EPSILON = 1e-06
BF = jnp.bfloat16
F32 = jnp.float32
GROUP = 256
FAR_FIRST = (2, 3, 1)


def mm(a, b):
    return jnp.dot(a, b, preferred_element_type=F32)


def mm_nt(a, b):
    return lax.dot_general(a, b, (((1,), (1,)), ((), ())), preferred_element_type=F32)


def mm_tn(a, b):
    return lax.dot_general(a, b, (((0,), (0,)), ((), ())), preferred_element_type=F32)


def full(shape):
    return pl.BlockSpec(shape, lambda *_: (0,) * len(shape))


def cols(rows, width):
    return pl.BlockSpec((rows, width), lambda g, *_: (0, g))


def shape_of(shape, dtype):
    return jax.ShapeDtypeStruct(shape, dtype)


def params(megabytes=20):
    return pltpu.CompilerParams(vmem_limit_bytes=megabytes * 1024 * 1024)


def cost(flops, nbytes):
    return pl.CostEstimate(flops=1024, bytes_accessed=1024, transcendentals=0)


def after(v, *others):
    return lax.optimization_barrier((v, *others))[0]


def all_after(values, *others):
    return list(lax.optimization_barrier((*values, *others))[: len(values)])


def gelu_parts(v):
    square = v * v
    bent = jnp.tanh(0.7978845608 * v * (1.0 + 0.044715 * square))
    half = 0.5 * (1.0 + bent)
    slope = half + 0.5 * v * (1.0 - bent * bent) * (0.7978845608 * (1.0 + 0.134145 * square))
    return v * half, slope


def gate_of(rows, router, picked):
    logits = mm(rows, router)
    exponent = jnp.exp(logits - jnp.max(logits, axis=-1, keepdims=True))
    router_probs = exponent / jnp.sum(exponent, axis=-1, keepdims=True)
    return router_probs, jnp.sum(router_probs * picked, axis=-1, keepdims=True)


def one_lane(shape, lane):
    return (lax.broadcasted_iota(jnp.int32, shape, 1) == lane).astype(F32)


def pack_kernel(*refs):
    out_ref = refs[-1]
    base = 0
    for ref in refs[:-2]:
        out_ref[:, base : base + ref.shape[1]] = ref[...]
        base += ref.shape[1]
    router = refs[-2][...].astype(F32).T.astype(BF)
    out_ref[:, base:] = jnp.concatenate(
        [router, jnp.zeros((router.shape[0], out_ref.shape[1] - base - router.shape[1]), router.dtype)], axis=1
    )


def route_kernel(
    room,
    nz,
    near,
    where_ref,
    routes_ref,
    dy_ref,
    order_ref,
    x_ref,
    gain_ref,
    next_gain_ref,
    slots_ref,
    slots_t_ref,
    keep_ref,
    send_ref,
    perm_ref,
    normed_ref,
    picked_ref,
    gain_out_ref,
    gain_next_ref,
):
    slots, tokens = slots_ref.shape
    experts = picked_ref.shape[1]
    z, c = where_ref[0], where_ref[1]
    expert = routes_ref[...]
    lanes = lax.broadcasted_iota(jnp.int32, (128, tokens), 0)
    picked = (lanes == expert).astype(F32)
    upper = (
        lax.broadcasted_iota(jnp.int32, (tokens, tokens), 0)
        <= lax.broadcasted_iota(jnp.int32, (tokens, tokens), 1)
    ).astype(BF)
    counts = mm(picked.astype(BF), upper)
    rank = jnp.sum(picked * (counts - 1.0), axis=0, keepdims=True).astype(jnp.int32)
    to_z, to_c = expert >> 1, expert & 1
    ahead = to_z ^ z if near else to_z
    other = jnp.where(to_c == c, 0, 1)
    slot = (other * nz + ahead) * room + rank
    chosen = (lax.broadcasted_iota(jnp.int32, (slots, tokens), 0) == slot).astype(F32)
    slots_ref[...] = chosen.astype(BF)
    slots_t_ref[...] = chosen.T.astype(BF)
    dy_rows = mm(slots_ref[...], dy_ref[...]).astype(BF)
    keep_ref[...] = dy_rows[: slots // 2]
    send_ref[: slots // 2, :] = dy_rows[slots // 2 :]
    picked_ref[...] = picked.T[:, :experts]
    width = perm_ref.shape[0]
    perm = (lax.broadcasted_iota(jnp.int32, (width, width), 0) == order_ref[...]).astype(F32).astype(BF)
    perm_ref[...] = perm
    x = x_ref[...].astype(F32)
    scale = lax.rsqrt(jnp.mean(x * x, axis=-1, keepdims=True) + EPSILON)
    normed = mm((x * scale * gain_ref[...]).astype(BF), perm).astype(BF)
    normed_ref[...] = normed
    send_ref[slots // 2 :, : width // 2] = normed[: tokens // 2, width // 2 :]
    send_ref[slots // 2 :, width // 2 :] = normed[tokens // 2 :, width // 2 :]
    gain_out_ref[...] = gain_ref[...]
    gain_next_ref[...] = next_gain_ref[...]


def bias_kernel(buckets_ref, table_ref, bias_ref, along):
    heads, rows = bias_ref.shape[0], bias_ref.shape[1]
    half, span = rows // 2, buckets_ref.shape[1]
    step = pl.program_id(0)

    @pl.when(step == 0)
    def _():
        every = table_ref.shape[0]
        onehot = (lax.broadcasted_iota(jnp.int32, (every, span), 0) == buckets_ref[...]).astype(F32)
        values = lax.dot_general(
            table_ref[...], onehot, (((0,), (0,)), ((), ())), precision=PRECISE, preferred_element_type=F32
        )
        for h in range(along.shape[0]):
            along[h] = values[h : h + 1]

    for h in range(heads):
        line = jnp.broadcast_to(along[step * heads + h], (half, span))
        turned = pltpu.roll(line, span - rows + 1, 1, stride=1, stride_axis=0)
        bias_ref[h, :half, :] = turned[:, :rows]
        bias_ref[h, half:, :half] = turned[:, span - half :]
        bias_ref[h, half:, half:] = turned[:, :half]


def fill_x_first(pieces, out_ref):
    half = pieces[0].shape[0]
    for number, piece in enumerate(pieces):
        out_ref[number * half : (number + 1) * half, :] = piece[...]


def fill_y_first(pieces, out_ref, starts=(0, 0, 0, 0)):
    half = pieces[0].shape[0]
    part = half // 2
    width = out_ref.shape[1]
    for side in range(2):
        own, other = pieces[2 * side], pieces[2 * side + 1]
        at, at_other = [slice(start, start + width) for start in starts[2 * side : 2 * side + 2]]
        base = side * 2 * half
        out_ref[base : base + part, :] = own[:part, at]
        out_ref[base + part : base + half, :] = other[:part, at_other]
        out_ref[base + half : base + half + part, :] = own[part:, at]
        out_ref[base + half + part : base + 2 * half, :] = other[part:, at_other]


def near_kernel(qv_ref, qv_x_ref, ko_ref, ko_y_ref, qv_near_ref, ko_near_ref, both_ref):
    part, width = qv_ref.shape
    for number, (left, right) in enumerate(((qv_ref, ko_ref), (qv_x_ref, ko_y_ref))):
        at = slice(number * part, (number + 1) * part)
        qv_near_ref[at, :] = left[...]
        ko_near_ref[at, :] = right[...]
        both_ref[at, :width] = left[...]
        both_ref[at, width:] = right[...]


def attend_kernel(head, *refs):
    normed_ref, bias_ref, perm_ref, x_ref, gain_ref, slots_ref, picked_ref = refs[:7]
    wq_refs, wv_refs, wk_refs, ko_refs = refs[7:11], refs[11:15], refs[15:19], refs[19:23]
    q_ref, k_ref, v_ref, probs_ref, mixed_ref, mixed_other_ref = refs[23:29]
    middle_ref, router_ref, gate_ref, keep_ref, send_ref = refs[29:34]
    wq, wk, wv, wo, mixed = refs[34:]
    step = pl.program_id(0)
    experts = router_ref.shape[1]
    model = x_ref.shape[1]

    fill_x_first(wq_refs, wq)
    fill_y_first(wk_refs, wk)
    fill_x_first(wv_refs, wv)
    normed = normed_ref[...]
    q = mm(normed, wq[...]).astype(BF)
    k = mm(normed, wk[...]).astype(BF)
    v = mm(normed, wv[...]).astype(BF)
    q_ref[...] = q
    k_ref[...] = k
    v_ref[...] = v
    rows = []
    for h in range(q.shape[1] // head):
        part = slice(h * head, (h + 1) * head)
        scores = mm_nt(q[:, part], k[:, part]) + bias_ref[h]
        exponent = jnp.exp(scores - jnp.max(scores, axis=-1, keepdims=True))
        probs = exponent / jnp.sum(exponent, axis=-1, keepdims=True)
        probs_ref[h] = probs
        rows.append(mm(probs.astype(BF), v[:, part]))
    mixed[step] = jnp.concatenate(rows, axis=1).astype(BF)

    @pl.when(step == pl.num_programs(0) - 1)
    def _():
        fill_y_first(ko_refs, wo, (model, model, 3 * model, model))
        perm = perm_ref[...]
        every = jnp.concatenate([mixed[g] for g in range(mixed.shape[0])], axis=1)
        mixed_in_order = mm(every, perm).astype(BF)
        mixed_ref[...] = mixed_in_order[:, : model // 2]
        mixed_other_ref[...] = mixed_in_order[:, model // 2 :]
        middle = x_ref[...].astype(F32) + mm(mixed_in_order, wo[:, :model])
        middle_ref[...] = middle
        scale = lax.rsqrt(jnp.mean(middle * middle, axis=-1, keepdims=True) + EPSILON)
        ffn_in = (middle * scale * gain_ref[...]).astype(BF)
        router = mm(perm, wo[:, model:]).astype(BF)[:, :experts]
        router_ref[...] = router
        rows = mm(slots_ref[...], ffn_in).astype(BF)
        gate_ref[...] = gate_of(ffn_in, router, picked_ref[...])[1]
        half = rows.shape[0] // 2
        keep_ref[...] = rows[:half]
        send_ref[...] = rows[half:]


def join(refs, out_ref):
    base = 0
    for ref in refs:
        size = ref.shape[0]
        out_ref[base : base + size, :] = ref[...]
        base += size


def part_out(v, refs):
    base = 0
    for ref in refs:
        size = ref.shape[0]
        ref[...] = v[base : base + size]
        base += size


def load_kernel(after_ref, w1_ref, w2_ref, w1_out, w2_out, token_ref, sems):
    copies = []
    for ref, out_ref in ((w1_ref, w1_out), (w2_ref, w2_out)):
        rows = ref.shape[1] // 4
        for part in range(4):
            at = pl.ds(part * rows, rows)
            copies.append(pltpu.make_async_copy(ref.at[0, at], out_ref.at[at], sems.at[len(copies)]))
    for copy in copies:
        copy.start()
    token_ref[...] = jnp.zeros_like(token_ref)
    for copy in copies:
        copy.wait()


def hidden_grad_kernel(first_ref, second_ref, w2_ref, first_out, second_out):
    rows = first_ref.shape[0]
    dy = jnp.concatenate([first_ref[...], second_ref[...]], axis=0)
    width = first_out.shape[1] // 3
    for part in range(3):
        at = slice(part * width, (part + 1) * width)
        both = mm_nt(dy, w2_ref[at, :])
        first_out[:, at] = both[:rows]
        second_out[:, at] = both[rows:]


def expert_kernel(pieces, own_ref, *refs):
    rows_refs, dy = refs[:pieces], refs[pieces]
    router_ref, w1_ref, w2_ref, hidden_grad_ref = refs[pieces + 1 : pieces + 5]
    refs = refs[pieces + 5 :]
    back_refs, result_refs = refs[:pieces], refs[pieces : 2 * pieces]
    router_grad_ref, rows = refs[2 * pieces :]
    own = own_ref[0]
    join(rows_refs, rows)
    picked = one_lane((rows.shape[0], router_ref.shape[1]), own)
    router_probs, gate = gate_of(rows[...], router_ref[...], picked)
    result, back = 0.0, 0.0
    width = w1_ref.shape[1] // 2
    for part in range(2):
        at = slice(part * width, (part + 1) * width)
        hidden, slope = gelu_parts(mm(rows[...], w1_ref[:, at]))
        result += mm(hidden.astype(BF), w2_ref[at, :])
        pre_grad = (hidden_grad_ref[:, at] * gate * slope).astype(BF)
        back += mm_nt(pre_grad, w1_ref[:, at])
    returned = result.astype(BF)
    part_out(returned, result_refs)
    gate_grad = jnp.sum(dy[...].astype(F32) * returned.astype(F32), axis=-1, keepdims=True)
    logit_grad = (router_probs * (picked - gate) * gate_grad).astype(BF)
    router_grad_ref[...] = mm_tn(logit_grad, rows[...])
    part_out((back + mm_nt(logit_grad, router_ref[...])).astype(BF), back_refs)


def expert_grad_kernel(pieces, more, place_ref, *refs):
    del place_ref
    rows_refs, dy_refs, refs = refs[:pieces], refs[pieces : 2 * pieces], refs[2 * pieces :]
    own_ref, router_ref, w1_ref, w2_ref = refs[:4]
    g1_ref, g2_ref, rows_all, branch_all = refs[-4:]

    @pl.when(pl.program_id(0) == 0)
    def _():
        join(rows_refs, rows_all)
        join(dy_refs, branch_all)
        picked = one_lane((rows_all.shape[0], router_ref.shape[1]), own_ref[0])
        gate = gate_of(rows_all[...], router_ref[...], picked)[1]
        branch_all[...] = (branch_all[...].astype(F32) * gate).astype(BF)

    rows, branch = rows_all[...], branch_all[...]
    hidden, slope = gelu_parts(mm(rows, w1_ref[0]))
    pre_grad = (mm_nt(branch, w2_ref[0]) * slope).astype(BF)
    g1, g2 = mm_tn(rows, pre_grad), mm_tn(hidden.astype(BF), branch)
    if more:
        g1, g2 = g1 + refs[4][0], g2 + refs[5][0]
    g1_ref[0] = g1
    g2_ref[0] = g2


def middle_kernel(head, pieces, *refs):
    keep_refs, refs = refs[:pieces], refs[pieces:]
    (send_ref, slots_t_ref, dy_ref, middle_ref, gain_ref, perm_ref, probs_ref, other_ref) = refs[:8]
    ko_refs = refs[8:12]
    (middle_grad_ref, gain_grad_ref, mixed_grad_ref, grads_ref, wo, mixed_grad) = refs[12:]
    rows, model = dy_ref.shape
    step = pl.program_id(0)
    keep_rows = send_ref.shape[0] // pieces

    @pl.when(step == 0)
    def _():
        fill_y_first(ko_refs, wo, (model, model, 3 * model, model))
        back = jnp.concatenate([ref[:keep_rows, :] for ref in keep_refs] + [send_ref[...]], axis=0)
        ffn_grad = mm(slots_t_ref[...], back)
        middle = middle_ref[...]
        scale = lax.rsqrt(jnp.mean(middle * middle, axis=-1, keepdims=True) + EPSILON)
        gain_grad_ref[...] = jnp.sum(ffn_grad * middle * scale, axis=0, keepdims=True)
        scaled = ffn_grad * gain_ref[...]
        along = jnp.mean(scaled * middle, axis=-1, keepdims=True)
        middle_grad = dy_ref[...].astype(F32) + scale * scaled - middle * (scale * scale * scale * along)
        middle_grad_ref[...] = middle_grad
        attn_grad = middle_grad.astype(BF)
        grads_ref[rows : 2 * rows, :] = attn_grad
        grads_ref[2 * rows :, : model // 2] = other_ref[: rows // 2, :]
        grads_ref[2 * rows :, model // 2 :] = other_ref[rows // 2 :, :]
        in_order = mm_nt(attn_grad, wo[...]).astype(BF)
        every = mm_nt(in_order, perm_ref[...]).astype(BF)
        mixed_grad_ref[...] = every
        for g in range(mixed_grad.shape[0]):
            mixed_grad[g] = every[:, g * GROUP : (g + 1) * GROUP]

    grads = mixed_grad[step]
    parts = [
        mm_tn(probs_ref[h].astype(BF), grads[:, h * head : (h + 1) * head]) for h in range(GROUP // head)
    ]
    value_grad = jnp.concatenate(parts, axis=1).astype(BF)
    at = pl.ds(pl.multiple_of(step * GROUP, GROUP), GROUP)
    grads_ref[:rows, at] = value_grad


def weight_grad_kernel(normed_ref, side_ref, mixed_ref, vo_ref, vo_side_ref, qk_ref, qk_side_ref, *outs):
    a_ref, a_low_ref, b_ref, b_low_ref = outs
    rows = normed_ref.shape[0]
    width = side_ref.shape[1] // 2
    model = normed_ref.shape[1]
    half, part = width // 2, width // 4

    def unpack(v):
        return [v[:, :width], v[:, width:]]

    normed = jnp.concatenate([normed_ref[:, :width], *unpack(side_ref[...])], axis=0)
    mixed = jnp.concatenate([mixed_ref[...], *unpack(vo_side_ref[2 * rows :, :])], axis=0)
    for number, (left, own, side) in enumerate(
        ((normed, vo_ref, vo_side_ref), (normed, qk_ref, qk_side_ref), (mixed, vo_ref, vo_side_ref), (normed, qk_ref, qk_side_ref))
    ):
        here = slice(0, rows) if number < 2 else slice(rows, 2 * rows)
        total = mm_tn(left, jnp.concatenate([own[here, :], side[here, :]], axis=0))
        at = slice(number % 2 * model, (number % 2 + 1) * model)
        if number < 2:
            a_ref[:, at] = total[:half]
            a_low_ref[:, at] = total[half:].astype(BF)
        else:
            b_ref[:part, at] = total[:part]
            b_ref[part:, at] = total[half : half + part]
            b_low_ref[:part, at] = total[part:half].astype(BF)
            b_low_ref[part:, at] = total[half + part :].astype(BF)


def fold_near_kernel(a_ref, a_got_ref, b_ref, b_got_ref, small_ref, small_got_ref, a2_ref, a2_low_ref, b2_ref, b2_low_ref):
    a = a_ref[...] + a_got_ref[...].astype(F32)
    b = b_ref[...] + b_got_ref[...].astype(F32)
    small = small_ref[...] + small_got_ref[...]
    half = a.shape[0] // 2
    a2_ref[...] = a[:half]
    a2_low_ref[:half, :] = a[half:].astype(BF)
    a2_low_ref[half:, :] = jnp.concatenate([small, jnp.zeros_like(small)], axis=1).astype(BF)
    b2_ref[...] = b[:half]
    b2_low_ref[...] = b[half:].astype(BF)


def fold_sums(a_ref, a_low_ref, a_got_ref, b_ref, b_got_ref):
    rows = a_ref.shape[0]
    a = a_ref[...] + a_got_ref[:rows, :].astype(F32)
    b = b_ref[...] + b_got_ref[...].astype(F32)
    model = a.shape[1] // 2
    return a, b, a_low_ref[rows:, :model].astype(F32) + a_got_ref[rows:, :model].astype(F32)


def fold_far_kernel(a_ref, a_low_ref, a_got_ref, b_ref, b_got_ref, keep_ref, *low_refs):
    a, b, small = fold_sums(a_ref, a_low_ref, a_got_ref, b_ref, b_got_ref)
    model = a.shape[1] // 2
    shard = a.shape[0] // 4
    for k in range(4):
        rows = slice(k * shard, (k + 1) * shard)
        blocks = [v[rows, half * model : (half + 1) * model] for v in (a, b) for half in range(2)]
        if k:
            low_refs[k - 1][...] = jnp.concatenate([small, *blocks], axis=0).astype(BF)
        else:
            keep_ref[...] = jnp.concatenate(blocks, axis=0)


def fold_last_kernel(keep_ref, own_ref, *refs):
    got, outs = [ref[...].astype(F32) for ref in refs[:3]], refs[3:]
    shard = outs[0].shape[0]
    first = outs[4].shape[0]
    total = keep_ref[...] + ((got[0][first:] + got[1][first:]) + got[2][first:])
    for number in range(4):
        outs[number][...] = total[number * shard : (number + 1) * shard]
    outs[4][...] = (own_ref[...][:first].astype(F32) + got[0][:first]) + (got[1][:first] + got[2][:first])


def score_grad_kernel(head, mixed_grad_ref, v_ref, q_ref, k_ref, probs_ref, grads_ref, along_ref):
    rows = q_ref.shape[0]
    flip = (
        lax.broadcasted_iota(jnp.int32, (rows, rows), 0) + lax.broadcasted_iota(jnp.int32, (rows, rows), 1)
        == rows - 1
    ).astype(F32).astype(BF)
    q_parts, k_parts = [], []
    for h in range(GROUP // head):
        part = slice(h * head, (h + 1) * head)
        probs = probs_ref[h]
        prob_grad = mm_nt(mixed_grad_ref[:, part], v_ref[:, part])
        inner = jnp.sum(probs * prob_grad, axis=-1, keepdims=True)
        score_grad = (probs * (prob_grad - inner)).astype(BF)
        q_parts.append(mm(score_grad, k_ref[:, part]))
        k_parts.append(mm_tn(score_grad, q_ref[:, part]))
        flipped = mm(flip, score_grad)
        half = rows // 2
        upper, lower = flipped[:half], flipped[half:]
        wide = jnp.concatenate(
            [upper[:, :half], upper[:, half:] + lower[:, :half], lower[:, half:], jnp.zeros_like(upper[:, :half])], axis=1
        )
        along_ref[h] = jnp.sum(pltpu.roll(wide, 0, 1, stride=1, stride_axis=0), axis=0, keepdims=True)
    grads_ref[:rows, :] = jnp.concatenate(q_parts, axis=1).astype(BF)
    grads_ref[rows:, :] = jnp.concatenate(k_parts, axis=1).astype(BF)


def input_kernel(table_rows, *refs):
    qk_ref, vo_ref, x_ref, gain_ref, perm_ref, middle_grad_ref = refs[:6]
    along_ref, buckets_ref, gain_next_ref, router_a_ref, router_b_ref = refs[6:11]
    qv_refs, wk_refs = refs[11:15], refs[15:19]
    input_grad_ref, small_ref, weight, wide = refs[19:]
    rows = x_ref.shape[0]
    experts, heads = router_a_ref.shape[0], along_ref.shape[0]
    every = table_rows
    onehot = (
        lax.broadcasted_iota(jnp.int32, (every, buckets_ref.shape[1]), 0) == buckets_ref[...]
    ).astype(F32)
    model = x_ref.shape[1]
    small_ref[...] = jnp.zeros_like(small_ref)
    small_ref[:experts, :] = router_a_ref[...] + router_b_ref[...]
    small_ref[experts + 1 : experts + 2, :] = gain_next_ref[...]
    along = jnp.concatenate([along_ref[h] for h in range(heads)], axis=0)
    table = lax.dot_general(
        along, onehot, (((1,), (1,)), ((), ())), precision=PRECISE, preferred_element_type=F32
    )
    small_ref[experts + 2 : experts + 3, : heads * every] = jnp.concatenate(
        [table[h : h + 1] for h in range(heads)], axis=1
    )
    fill_x_first(qv_refs, wide)
    total = mm_nt(jnp.concatenate([qk_ref[:rows, :], vo_ref[:rows, :]], axis=1), wide[...])
    fill_y_first(wk_refs, weight)
    total += mm_nt(qk_ref[rows:, :], weight[...])
    perm = perm_ref[...]
    high = total.astype(BF)
    low = (total - high.astype(F32)).astype(BF)
    normed_grad = mm_nt(high, perm) + mm_nt(low, perm)
    x = x_ref[...].astype(F32)
    scale = lax.rsqrt(jnp.mean(x * x, axis=-1, keepdims=True) + EPSILON)
    small_ref[experts : experts + 1, :] = jnp.sum(normed_grad * x * scale, axis=0, keepdims=True)
    scaled = normed_grad * gain_ref[...]
    along = jnp.mean(scaled * x, axis=-1, keepdims=True)
    input_grad_ref[...] = middle_grad_ref[...] + scale * scaled - x * (scale * scale * scale * along)


class Places:
    def __init__(self):
        self.experts = lax.axis_size("expert")
        self.nz = self.experts // 2
        self.dp = lax.axis_size("dp")
        self.near = self.nz == 4
        me = lax.axis_index("expert")
        self.z, self.c = me // 2, me % 2
        self.row = lax.axis_index("dp")
        self.columns = [[2 * z + c for z in range(self.nz)] for c in range(2)]

    def core(self, v):
        return lax.ppermute(v, "expert", [(i, i ^ 1) for i in range(self.experts)])

    def x(self, v):
        return lax.ppermute(v, "dp", [(i, i ^ 1) for i in range(self.dp)])

    def y(self, v):
        return lax.ppermute(v, "dp", [(i, i ^ 2) for i in range(self.dp)])

    def far(self, v, k):
        return lax.ppermute(v, "expert", [(i, i ^ (2 * k)) for i in range(self.experts)])

    def apart(self, v):
        return lax.all_to_all(
            v, "expert", split_axis=0, concat_axis=0, tiled=True, axis_index_groups=self.columns
        )

    def gather_z(self, v):
        if self.near:
            got = {k: self.far(v, k) for k in FAR_FIRST}
            return jnp.concatenate([v, got[1], got[2], got[3]], axis=0)
        return lax.all_gather(v, "expert", axis=0, tiled=True, axis_index_groups=self.columns)

    def z_order(self):
        steps = jnp.arange(self.nz, dtype=jnp.int32)
        return self.z ^ steps if self.near else steps

    def scatter_z(self, v):
        size = v.shape[0] // self.nz
        if self.near:
            total = v[:size]
            low = v.astype(BF)
            for k in FAR_FIRST:
                total = total + self.far(low[k * size : (k + 1) * size], k).astype(F32)
            return total
        got = self.apart(v.astype(BF).reshape(self.nz, size, v.shape[1]))
        mine = lax.dynamic_slice_in_dim(v, self.z * size, size, axis=0)
        steps = jnp.arange(self.nz, dtype=jnp.int32)[:, None, None]
        return mine + jnp.sum(jnp.where(steps == self.z, 0.0, got.astype(F32)), axis=0)

    def swap(self, blocks):
        got = {k: self.far(blocks[k], k) for k in FAR_FIRST}
        return [blocks[0], got[1], got[2], got[3]]

    def swap_relay(self, blocks, hold):
        size = blocks[0].shape[0]
        first = self.far(jnp.concatenate([blocks[2], blocks[3]], axis=0), 2)
        onward = after(jnp.concatenate([blocks[1], first[size:]], axis=0), *hold)
        second = self.far(onward, 1)
        return [blocks[0], second[:size], first[:size], second[size:]], onward

    def by_z(self, keep, got):
        room = keep.shape[0] // self.nz
        both = jnp.concatenate([v.reshape(self.nz, room, keep.shape[1]) for v in (keep, got)], axis=1)
        return [both[k] for k in range(4)] if self.near else both

    def halves(self, moved):
        moved = moved.reshape(-1, moved.shape[-1])
        half = moved.shape[0] // 2
        return [moved[:half]], [moved[half:]]

    def to_owners(self, keep, got, hold):
        blocks = self.by_z(keep, got)
        if self.near:
            blocks = all_after([blocks[k] for k in range(4)], *hold)
            two, one = self.far(blocks[2], 2), self.far(blocks[1], 1)
            three = self.far(after(blocks[3], two), 3)
            return [blocks[0], two], [one, three]
        return self.halves(self.apart(blocks))

    def send_more(self, blocks, k, hold):
        return self.far(after(blocks[k], *hold), k) if self.near else blocks

    def from_owners(self, first, second):
        width = first[0].shape[1]
        both = self.apart(jnp.concatenate([*first, *second], axis=0).reshape(self.nz, -1, width))
        room = both.shape[1] // 2
        return [both[:, :room].reshape(-1, width)], both[:, room:].reshape(-1, width)

    def to_senders(self, first, second):
        if self.near:
            two = self.far(first[1], 2)
            one, three = all_after(second, two)
            three, one = self.far(three, 3), self.far(one, 1)
            moved = [first[0], one, two, three]
            room = one.shape[0] // 2
            return moved, self.core(jnp.concatenate([v[room:] for v in moved], axis=0))
        keep, other = self.from_owners(first, second)
        return keep, self.core(other)

    def gather_far(self, a, b):
        return self.y(a), self.x(b)


def per_device(
    tokens,
    cotangent,
    routes,
    buckets,
    norm_attn,
    norm_ffn,
    rel_table,
    query_weight,
    key_weight,
    value_weight,
    out_weight,
    router_weight,
    expert_in,
    expert_out,
):
    at = Places()
    rows, model = tokens.shape
    head_count = rel_table.shape[1]
    head = model // head_count
    bucket_count = rel_table.shape[0]
    experts = router_weight.shape[1]
    shard = query_weight.shape[0]
    nz = at.nz
    room = max(2, 2 * rows // at.experts)
    slots = experts * room
    half = slots // 2
    groups = model // GROUP
    per_group = GROUP // head
    hidden = expert_in.shape[2]

    def in_hbm(*values):
        return [pltpu.with_memory_space_constraint(v, pltpu.HBM) for v in values]

    expert_in, expert_out = in_hbm(expert_in, expert_out)
    own = lax.axis_index("expert").astype(jnp.int32).reshape(1)
    smem = pl.BlockSpec(memory_space=pltpu.SMEM)

    core_of = at.c ^ jnp.arange(2, dtype=jnp.int32)
    row_of = at.row ^ jnp.arange(4, dtype=jnp.int32)
    device_of = (
        row_of[None, :, None] * at.experts + at.z_order()[None, None, :] * 2 + core_of[:, None, None]
    )
    order = (
        device_of[..., None] * shard + jnp.arange(shard, dtype=jnp.int32)
    ).reshape(1, model).astype(jnp.int32)

    shards = (query_weight, value_weight, key_weight, out_weight, router_weight.T)
    packed = pl.pallas_call(
        pack_kernel,
        out_shape=shape_of((shard, 4 * model + 128), BF),
        in_specs=[pl.BlockSpec(memory_space=pltpu.VMEM)] * 5,
        out_specs=pl.BlockSpec(memory_space=pltpu.VMEM),
        name="pack",
    )(*shards)
    line = at.gather_z(packed)
    span = 2 * rows
    bucket_line = jnp.pad(buckets, (0, 1), constant_values=-1).reshape(1, span)
    slots_map, slots_t, dy_keep, dy_send, perm, normed, picked, gain_attn, gain_ffn = pl.pallas_call(
        functools.partial(route_kernel, room, nz, at.near),
        out_shape=(
            shape_of((slots, rows), BF),
            shape_of((rows, slots), BF),
            shape_of((half, model), BF),
            shape_of((half + rows // 2, model), BF),
            shape_of((model, model), BF),
            shape_of((rows, model), BF),
            shape_of((rows, experts), F32),
            shape_of((1, model), F32),
            shape_of((1, model), F32),
        ),
        in_specs=[smem] + [pl.BlockSpec(memory_space=pltpu.VMEM)] * 6,
        compiler_params=params(),
        cost_estimate=cost(2 * rows * slots * model, 4 * rows * model),
        name="route",
    )(
        jnp.stack([at.z, at.c]).astype(jnp.int32),
        routes.reshape(1, rows),
        cotangent,
        order,
        tokens,
        norm_attn.reshape(1, model),
        norm_ffn.reshape(1, model),
    )
    dy_got = at.core(dy_send)
    normed_side = dy_got[half:]
    dy_got = dy_got[:half]
    qv, ko = line[:, : 2 * model], line[:, 2 * model :]
    qv, ko = all_after([qv, ko], dy_got)
    dy_keep, dy_got = all_after([dy_keep, dy_got], qv, ko)
    part_rows = qv.shape[0]
    dy_blocks = at.by_z(dy_keep, dy_got)
    dy_one = at.send_more(dy_blocks, 1, (dy_blocks,))
    qv_near, ko_near, both_near = pl.pallas_call(
        near_kernel,
        out_shape=tuple(shape_of((2 * part_rows, width), BF) for width in (2 * model, 2 * model + 128, 4 * model + 128)),
        in_specs=[pl.BlockSpec(memory_space=pltpu.VMEM)] * 4,
        out_specs=(pl.BlockSpec(memory_space=pltpu.VMEM),) * 3,
        compiler_params=params(),
        name="near",
    )(after(qv, dy_one), at.x(qv), ko, at.y(ko))
    bias = pl.pallas_call(
        bias_kernel,
        grid=(groups,),
        out_shape=shape_of((head_count, rows, rows), F32),
        in_specs=[full((1, span)), full((bucket_count, head_count))],
        out_specs=pl.BlockSpec((per_group, rows, rows), lambda g: (g, 0, 0)),
        scratch_shapes=[pltpu.VMEM((head_count, 1, span), F32)],
        compiler_params=params(),
        cost_estimate=cost(1 << 20, 4 * head_count * rows * rows),
        name="bias",
    )(after(bucket_line, qv, ko), rel_table)
    qv_far, ko_far = at.gather_far(*all_after([qv_near, ko_near], bias))
    w_first, w_second, loaded = pl.pallas_call(
        load_kernel,
        out_shape=(pltpu.VMEM((model, hidden), BF), pltpu.VMEM((hidden, model), BF), shape_of((8, 128), F32)),
        in_specs=[pl.BlockSpec(memory_space=pltpu.VMEM)] + [pl.BlockSpec(memory_space=pl.ANY)] * 2,
        out_specs=(pl.BlockSpec(memory_space=pltpu.VMEM),) * 3,
        scratch_shapes=[pltpu.SemaphoreType.DMA((8,))],
        compiler_params=params(),
        name="load",
    )(bias[0, :8, :128], expert_in, expert_out)
    both_side = at.core(both_near)
    dy_two = at.send_more(dy_blocks, 2, (qv_near, dy_one))
    qv_far, ko_far, dy_two = all_after([qv_far, ko_far, dy_two], both_side)
    dy_three = at.send_more(dy_blocks, 3, (qv_far, ko_far, dy_two))
    qv_pieces = (qv_near, qv_far, both_side, at.core(qv_far))
    ko_pieces = (ko_near, ko_far, both_side, at.core(ko_far))
    if at.near:
        dy_a = jnp.concatenate([dy_blocks[0], dy_two], axis=0)
    else:
        (dy_a,), (dy_b,) = at.halves(at.apart(dy_blocks))
    dy_a_later = after(dy_a, qv_far, ko_far)
    dy_ax, dy_ay = at.x(dy_a_later), at.y(dy_a_later)

    quarter = qv_near.shape[0]
    wide = ko_near.shape[1]
    side_wide = both_side.shape[1]
    head_block = pl.BlockSpec((per_group, rows, rows), lambda g: (g, 0, 0))
    later = pl.BlockSpec((quarter, GROUP), lambda g: (0, groups + g))
    side_k = pl.BlockSpec((quarter, GROUP), lambda g: (0, 2 * groups + g))
    first_k = cols(quarter, GROUP)
    ko_full = [full((quarter, wide)), full((quarter, wide)), full((quarter, side_wide)), full((quarter, wide))]
    q, k, v, probs, mixed, mixed_other, middle, router, gate, keep, send = pl.pallas_call(
        functools.partial(attend_kernel, head),
        grid=(groups,),
        out_shape=(shape_of((rows, model), BF),) * 3
        + (
            shape_of((head_count, rows, rows), F32),
            shape_of((rows, model // 2), BF),
            shape_of((rows, model // 2), BF),
            shape_of((rows, model), F32),
            shape_of((model, experts), BF),
            shape_of((rows, 1), F32),
            shape_of((half, model), BF),
            shape_of((half, model), BF),
        ),
        in_specs=[
            full((rows, model)),
            head_block,
            full((model, model)),
            full((rows, model)),
            full((1, model)),
            full((slots, rows)),
            full((rows, experts)),
        ]
        + [cols(quarter, GROUP)] * 4
        + [later] * 4
        + [first_k, first_k, side_k, first_k]
        + ko_full,
        out_specs=(cols(rows, GROUP),) * 3
        + (
            head_block,
            full((rows, model // 2)),
            full((rows, model // 2)),
            full((rows, model)),
            full((model, experts)),
            full((rows, 1)),
            full((half, model)),
            full((half, model)),
        ),
        scratch_shapes=[pltpu.VMEM((model, GROUP), BF)] * 3
        + [pltpu.VMEM((model, wide - model), BF), pltpu.VMEM((groups, rows, GROUP), BF)],
        compiler_params=params(),
        cost_estimate=cost(8 * rows * model * model, 12 * model * model),
        name="attend",
    )(normed, bias, perm, *in_hbm(tokens), after(gain_ffn, loaded), *in_hbm(slots_map), picked, *qv_pieces, *qv_pieces, *ko_pieces, *ko_pieces)

    got = at.core(after(send, dy_three))
    first, second = at.to_owners(keep, got, (dy_ax, dy_ay))
    if at.near:
        dy_b = jnp.concatenate([dy_one, dy_three], axis=0)
    dy_b_later = after(dy_b, got, dy_ax, dy_ay)
    dy_by, dy_bx = at.y(dy_b_later), at.x(dy_b_later)
    in_vmem = pl.BlockSpec(memory_space=pltpu.VMEM)
    hidden_grads = pl.pallas_call(
        hidden_grad_kernel,
        out_shape=(shape_of((half, hidden), F32),) * 2,
        in_specs=[in_vmem] * 3,
        out_specs=(in_vmem,) * 2,
        compiler_params=params(),
        name="hidden_grads",
    )(dy_a, dy_b, w_second)

    def expert(rows_list, dy_rows, hidden_grad, router_in):
        sizes = [v.shape[0] for v in rows_list]
        count = sum(sizes)
        shapes = [((n, model), BF) for n in sizes * 2] + [((experts, model), F32), ((count, model), BF)]
        outs = pl.pallas_call(
            functools.partial(expert_kernel, len(sizes)),
            out_shape=tuple(shape_of(*v) for v in shapes),
            in_specs=[smem] + [in_vmem] * (len(sizes) + 5),
            out_specs=(in_vmem,) * len(shapes),
            compiler_params=params(),
            name="expert",
        )(own, *rows_list, dy_rows, router_in, w_first, w_second, hidden_grad)
        n = len(sizes)
        return list(outs[:n]), list(outs[n : 2 * n]), outs[2 * n], outs[2 * n + 1]

    dy_ax_later, dy_by_later = all_after([dy_ax, dy_by], first[-1], dy_bx, hidden_grads[1])
    dy_axy, dy_byx = at.y(dy_ax_later), at.x(dy_by_later)
    back_a, returned_a, router_grad_a, rows_a = expert(first, dy_a, hidden_grads[0], after(router, dy_by, dy_bx))
    rows_ax, rows_ay = at.x(rows_a), at.y(rows_a)
    back_b, returned_b, router_grad_b, rows_b = expert(
        second, dy_b, hidden_grads[1], after(router, router_grad_a, dy_axy, dy_byx)
    )
    rows_b_later = after(rows_b, rows_ax, rows_ay)
    rows_by, rows_bx = at.y(rows_b_later), at.x(rows_b_later)
    back_keep, back_send = at.to_senders(back_a, back_b)

    slice_width = hidden // at.dp
    place = at.row.astype(jnp.int32).reshape(1)

    steps = slice_width // GROUP

    def expert_grads(rows_list, dy_list, router_in, before):
        sizes = [v.shape[0] for v in rows_list]
        count = sum(sizes)
        outs = (
            pl.BlockSpec((1, model, GROUP), lambda g, place: (0, 0, g)),
            pl.BlockSpec((1, GROUP, model), lambda g, place: (0, g, 0)),
        )
        return pl.pallas_call(
            functools.partial(expert_grad_kernel, len(sizes), bool(before)),
            grid_spec=pltpu.PrefetchScalarGridSpec(
                num_scalar_prefetch=1,
                grid=(steps,),
                in_specs=[full((n, model)) for n in sizes * 2]
                + [
                    smem,
                    full((model, experts)),
                    pl.BlockSpec((1, model, GROUP), lambda g, place: (0, 0, place[0] * steps + g)),
                    pl.BlockSpec((1, GROUP, model), lambda g, place: (0, place[0] * steps + g, 0)),
                ]
                + list(outs if before else ()),
                out_specs=outs,
                scratch_shapes=[pltpu.VMEM((count, model), BF), pltpu.VMEM((count, model), BF)],
            ),
            out_shape=(pltpu.HBM((1, model, slice_width), F32), pltpu.HBM((1, slice_width, model), F32)),
            compiler_params=params(),
            cost_estimate=cost(8 * count * model * slice_width, 20 * model * slice_width),
            name="expert_grads",
        )(place, *in_hbm(*rows_list, *dy_list), own, router_in, expert_in, expert_out, *in_hbm(*before))

    rows_axy, rows_byx = at.y(after(rows_ax, rows_by, rows_bx, back_send)), at.x(after(rows_by, rows_bx, back_send))

    middle_grad, gain_ffn_grad, mixed_grad, vo_grads = pl.pallas_call(
        functools.partial(middle_kernel, head, len(back_keep)),
        grid=(groups,),
        out_shape=(
            shape_of((rows, model), F32),
            shape_of((1, model), F32),
            shape_of((rows, model), BF),
            shape_of((2 * rows + rows // 2, model), BF),
        ),
        in_specs=[full(v.shape) for v in back_keep]
        + [
            full((half, model)),
            full((rows, slots)),
            full((rows, model)),
            full((rows, model)),
            full((1, model)),
            full((model, model)),
            head_block,
            full((rows, model // 2)),
        ]
        + ko_full,
        out_specs=(
            full((rows, model)),
            full((1, model)),
            full((rows, model)),
            full((2 * rows + rows // 2, model)),
        ),
        scratch_shapes=[pltpu.VMEM((model, model), BF), pltpu.VMEM((groups, rows, GROUP), BF)],
        compiler_params=params(),
        cost_estimate=cost(10 * rows * model * model, 12 * model * model),
        name="middle",
    )(*back_keep, back_send, slots_t, cotangent, middle, after(gain_ffn, rows_by, rows_bx), perm, probs, mixed_other, *ko_pieces)
    vo_side = at.core(vo_grads)
    qk_grads, along_grad = pl.pallas_call(
        functools.partial(score_grad_kernel, head),
        grid=(groups,),
        out_shape=(shape_of((2 * rows, model), BF), shape_of((head_count, 1, span), F32)),
        in_specs=[cols(rows, GROUP)] * 4 + [head_block],
        out_specs=(cols(2 * rows, GROUP), pl.BlockSpec((per_group, 1, span), lambda g: (g, 0, 0))),
        compiler_params=params(),
        cost_estimate=cost(8 * rows * model * model, 12 * model * model),
        name="score_grads",
    )(mixed_grad, v, q, k, probs)
    qk_side = at.core(after(qk_grads, vo_side, rows_axy, rows_byx))
    small_rows = -(-(experts + 3) // 16) * 16
    input_grad, small = pl.pallas_call(
        functools.partial(input_kernel, bucket_count),
        grid=(1,),
        out_shape=(shape_of((rows, model), F32), shape_of((small_rows, model), F32)),
        in_specs=[full((2 * rows, model)), full((2 * rows + rows // 2, model))]
        + [full((rows, model)), full((1, model)), full((model, model)), full((rows, model))]
        + [full((head_count, 1, span)), full((1, span)), full((1, model))]
        + [full((experts, model))] * 2
        + [full((quarter, 2 * model))] * 4
        + [pl.BlockSpec((quarter, model), lambda g, at=at_k: (0, at)) for at_k in (0, 0, 2, 0)],
        out_specs=(full((rows, model)), full((small_rows, model))),
        scratch_shapes=[pltpu.VMEM((model, model), BF), pltpu.VMEM((model, 2 * model), BF)],
        compiler_params=params(),
        cost_estimate=cost(10 * rows * model * model, 12 * model * model),
        name="inputs",
    )(
        qk_grads,
        vo_grads,
        tokens,
        gain_attn,
        perm,
        middle_grad,
        along_grad,
        bucket_line,
        gain_ffn_grad,
        router_grad_a,
        router_grad_b,
        *qv_pieces,
        *ko_pieces,
    )
    quarter_rows = model // 4

    def vmem_call(kernel, name, shapes, *ins):
        return pl.pallas_call(
            kernel,
            out_shape=tuple(shape_of(*v) for v in shapes),
            in_specs=[pl.BlockSpec(v.shape, lambda: (0, 0)) for v in ins],
            out_specs=tuple(pl.BlockSpec(v[0], lambda: (0, 0)) for v in shapes),
            compiler_params=params(),
            name=name,
        )(*ins)

    pair = 2 * model
    a, a_low, b, b_low = vmem_call(
        weight_grad_kernel,
        "weight_grads",
        [((quarter_rows, pair), F32), ((quarter_rows, pair), BF)] * 2,
        normed,
        after(normed_side, small),
        mixed,
        vo_grads,
        vo_side,
        qk_grads,
        qk_side,
    )
    small = small + after(at.core(small), a_low)
    a_got, b_got = at.y(a_low), at.x(b_low)
    small_got = at.y(small)
    if at.near:
        home_two = at.far(after(returned_a[1], a_low, b_low), 2)
    else:
        home_two = at.apart(jnp.concatenate([*returned_a, *returned_b], axis=0).reshape(nz, -1, model))
    near_sums = expert_grads(
        [rows_a, rows_b, rows_ax, rows_by],
        [dy_a, dy_b, dy_ax, dy_by],
        after(router, a_low, b_low),
        (),
    )
    eighth = quarter_rows // 2
    a, a_low, b, b_low = vmem_call(
        fold_near_kernel,
        "fold_near",
        [((eighth, pair), F32), ((eighth + small_rows, pair), BF), ((eighth, pair), F32), ((eighth, pair), BF)],
        a,
        after(a_got, near_sums[0], home_two),
        b,
        b_got,
        small,
        small_got,
    )
    a_got, b_got = at.x(a_low), at.y(b_low)
    mid_sums = expert_grads([rows_ay, rows_bx], [dy_ay, dy_bx], after(router, a_low, b_low), near_sums)
    if at.near:
        home = [at.far(v, k) for v, k in zip(all_after([returned_b[1], returned_b[0]], a_low, b_low), (3, 1))]
        home_blocks = [returned_a[0], home[1], home_two, home[0]]
        room = half // nz
        returned_keep = home_blocks
        returned_other = jnp.concatenate([v[room:] for v in home_blocks], axis=0)
    else:
        room = home_two.shape[1] // 2
        returned_keep = [home_two[:, :room].reshape(half, model)]
        returned_other = home_two[:, room:].reshape(half, model)
    if at.near:
        keep_sum, *low = vmem_call(
            fold_far_kernel,
            "fold_far",
            [((4 * shard, model), F32)] + [((small_rows + 4 * shard, model), BF)] * 3,
            a,
            a_low,
            after(a_got, mid_sums[0], *home),
            b,
            b_got,
        )
        hold = keep_sum
        got_z = {k: at.far(low[k - 1], k) for k in FAR_FIRST}
    else:
        a = a + a_got[:eighth].astype(F32)
        b = b + b_got.astype(F32)
        summed = (a_low[eighth:].astype(F32) + a_got[eighth:].astype(F32))[:, :model]
        hold = jnp.concatenate([a, b], axis=1)
        sums = at.scatter_z(hold)
        grad_value, grad_query, grad_proj, grad_key = [sums[:, n * model : (n + 1) * model] for n in range(4)]
        summed = lax.psum(summed, "expert", axis_index_groups=at.columns)
    returned_send = at.core(after(returned_other, hold))
    grad_in, grad_out_w = expert_grads([rows_axy, rows_byx], [dy_axy, dy_byx], after(router, hold), mid_sums)
    keep_rows = half // len(returned_keep)
    expert_result = mm(
        slots_t,
        jnp.concatenate([v[:keep_rows] for v in returned_keep] + [returned_send], axis=0),
    )
    output = (middle + gate * expert_result).astype(BF)
    if at.near:
        grad_value, grad_query, grad_proj, grad_key, summed = vmem_call(
            fold_last_kernel,
            "fold_last",
            [((shard, model), F32)] * 4 + [((small_rows, model), F32)],
            after(keep_sum, output, grad_in),
            low[0],
            *[got_z[k] for k in (1, 2, 3)],
        )
    device = at.row * at.experts + lax.axis_index("expert")
    grad_router = lax.dynamic_slice_in_dim(summed[:experts], device * shard, shard, axis=1).T
    return (
        output,
        input_grad,
        summed[experts],
        summed[experts + 1],
        summed[experts + 2, : head_count * bucket_count].reshape(head_count, bucket_count).T,
        grad_query,
        grad_key,
        grad_value,
        grad_proj,
        grad_router,
        grad_in,
        grad_out_w,
    )


def solution(mesh):
    in_specs = (
        P(("dp", "expert"), None),
        P(("dp", "expert"), None),
        P(("dp", "expert"), None),
        P(),
        P(),
        P(),
        P(),
        P(("dp", "expert"), None),
        P(("dp", "expert"), None),
        P(("dp", "expert"), None),
        P(("dp", "expert"), None),
        P(("dp", "expert"), None),
        P("expert", None, None),
        P("expert", None, None),
    )
    out_specs = (
        P(("dp", "expert"), None),
        P(("dp", "expert"), None),
        P(),
        P(),
        P(),
        P(("dp", "expert"), None),
        P(("dp", "expert"), None),
        P(("dp", "expert"), None),
        P(("dp", "expert"), None),
        P(("dp", "expert"), None),
        P("expert", None, "dp"),
        P("expert", "dp", None),
    )
    return jax.shard_map(
        per_device, mesh=mesh, in_specs=in_specs, out_specs=out_specs, check_vma=False
    )
```

```python
import functools

import jax
import jax.numpy as jnp
from jax import lax
from jax.experimental import pallas as pl
from jax.experimental.pallas import tpu as pltpu
from jax.sharding import PartitionSpec as P

PRECISE = lax.Precision.HIGHEST
EPSILON = 1e-06
BF = jnp.bfloat16
F32 = jnp.float32
GROUP = 256
FAR_FIRST = (2, 3, 1)


def mm(a, b):
    return jnp.dot(a, b, preferred_element_type=F32)


def mm_nt(a, b):
    return lax.dot_general(a, b, (((1,), (1,)), ((), ())), preferred_element_type=F32)


def mm_tn(a, b):
    return lax.dot_general(a, b, (((0,), (0,)), ((), ())), preferred_element_type=F32)


def full(shape):
    return pl.BlockSpec(shape, lambda *_: (0,) * len(shape))


def cols(rows, width):
    return pl.BlockSpec((rows, width), lambda g, *_: (0, g))


def shape_of(shape, dtype):
    return jax.ShapeDtypeStruct(shape, dtype)


def params(megabytes=20):
    return pltpu.CompilerParams(vmem_limit_bytes=megabytes * 1024 * 1024)


def cost(flops, nbytes):
    return pl.CostEstimate(flops=1024, bytes_accessed=1024, transcendentals=0)


def after(v, *others):
    return lax.optimization_barrier((v, *others))[0]


def all_after(values, *others):
    return list(lax.optimization_barrier((*values, *others))[: len(values)])


def gelu_parts(v):
    square = v * v
    bent = jnp.tanh(0.7978845608 * v * (1.0 + 0.044715 * square))
    half = 0.5 * (1.0 + bent)
    slope = half + 0.5 * v * (1.0 - bent * bent) * (0.7978845608 * (1.0 + 0.134145 * square))
    return v * half, slope


def gate_of(rows, router, picked):
    logits = mm(rows, router)
    exponent = jnp.exp(logits - jnp.max(logits, axis=-1, keepdims=True))
    router_probs = exponent / jnp.sum(exponent, axis=-1, keepdims=True)
    return router_probs, jnp.sum(router_probs * picked, axis=-1, keepdims=True)


def one_lane(shape, lane):
    return (lax.broadcasted_iota(jnp.int32, shape, 1) == lane).astype(F32)


def pack_kernel(*refs):
    out_ref = refs[-1]
    base = 0
    for ref in refs[:-2]:
        out_ref[:, base : base + ref.shape[1]] = ref[...]
        base += ref.shape[1]
    router = refs[-2][...].astype(F32).T.astype(BF)
    out_ref[:, base:] = jnp.concatenate(
        [router, jnp.zeros((router.shape[0], out_ref.shape[1] - base - router.shape[1]), router.dtype)], axis=1
    )


def route_kernel(
    room,
    nz,
    near,
    where_ref,
    routes_ref,
    dy_ref,
    order_ref,
    x_ref,
    gain_ref,
    next_gain_ref,
    slots_ref,
    slots_t_ref,
    keep_ref,
    send_ref,
    perm_ref,
    normed_ref,
    picked_ref,
    gain_out_ref,
    gain_next_ref,
):
    slots, tokens = slots_ref.shape
    experts = picked_ref.shape[1]
    z, c = where_ref[0], where_ref[1]
    expert = routes_ref[...]
    lanes = lax.broadcasted_iota(jnp.int32, (128, tokens), 0)
    picked = (lanes == expert).astype(F32)
    upper = (
        lax.broadcasted_iota(jnp.int32, (tokens, tokens), 0)
        <= lax.broadcasted_iota(jnp.int32, (tokens, tokens), 1)
    ).astype(BF)
    counts = mm(picked.astype(BF), upper)
    rank = jnp.sum(picked * (counts - 1.0), axis=0, keepdims=True).astype(jnp.int32)
    to_z, to_c = expert >> 1, expert & 1
    ahead = to_z ^ z if near else to_z
    other = jnp.where(to_c == c, 0, 1)
    slot = (other * nz + ahead) * room + rank
    chosen = (lax.broadcasted_iota(jnp.int32, (slots, tokens), 0) == slot).astype(F32)
    slots_ref[...] = chosen.astype(BF)
    slots_t_ref[...] = chosen.T.astype(BF)
    dy_rows = mm(slots_ref[...], dy_ref[...]).astype(BF)
    keep_ref[...] = dy_rows[: slots // 2]
    send_ref[: slots // 2, :] = dy_rows[slots // 2 :]
    picked_ref[...] = picked.T[:, :experts]
    width = perm_ref.shape[0]
    perm = (lax.broadcasted_iota(jnp.int32, (width, width), 0) == order_ref[...]).astype(F32).astype(BF)
    perm_ref[...] = perm
    x = x_ref[...].astype(F32)
    scale = lax.rsqrt(jnp.mean(x * x, axis=-1, keepdims=True) + EPSILON)
    normed = mm((x * scale * gain_ref[...]).astype(BF), perm).astype(BF)
    normed_ref[...] = normed
    send_ref[slots // 2 :, : width // 2] = normed[: tokens // 2, width // 2 :]
    send_ref[slots // 2 :, width // 2 :] = normed[tokens // 2 :, width // 2 :]
    gain_out_ref[...] = gain_ref[...]
    gain_next_ref[...] = next_gain_ref[...]


def bias_kernel(buckets_ref, table_ref, bias_ref, along):
    heads, rows = bias_ref.shape[0], bias_ref.shape[1]
    half, span = rows // 2, buckets_ref.shape[1]
    step = pl.program_id(0)

    @pl.when(step == 0)
    def _():
        every = table_ref.shape[0]
        onehot = (lax.broadcasted_iota(jnp.int32, (every, span), 0) == buckets_ref[...]).astype(F32)
        values = lax.dot_general(
            table_ref[...], onehot, (((0,), (0,)), ((), ())), precision=PRECISE, preferred_element_type=F32
        )
        for h in range(along.shape[0]):
            along[h] = values[h : h + 1]

    for h in range(heads):
        line = jnp.broadcast_to(along[step * heads + h], (half, span))
        turned = pltpu.roll(line, span - rows + 1, 1, stride=1, stride_axis=0)
        bias_ref[h, :half, :] = turned[:, :rows]
        bias_ref[h, half:, :half] = turned[:, span - half :]
        bias_ref[h, half:, half:] = turned[:, :half]


def fill_x_first(pieces, out_ref):
    half = pieces[0].shape[0]
    for number, piece in enumerate(pieces):
        out_ref[number * half : (number + 1) * half, :] = piece[:, : out_ref.shape[1]]


def fill_y_first(pieces, out_ref, starts=(0, 0, 0, 0)):
    half = pieces[0].shape[0]
    part = half // 2
    width = out_ref.shape[1]
    for side in range(2):
        own, other = pieces[2 * side], pieces[2 * side + 1]
        at, at_other = [slice(start, start + width) for start in starts[2 * side : 2 * side + 2]]
        base = side * 2 * half
        out_ref[base : base + part, :] = own[:part, at]
        out_ref[base + part : base + half, :] = other[:part, at_other]
        out_ref[base + half : base + half + part, :] = own[part:, at]
        out_ref[base + half + part : base + 2 * half, :] = other[part:, at_other]


def near_kernel(qv_ref, qv_x_ref, ko_ref, ko_y_ref, qv_near_ref, ko_near_ref, both_ref, qv_kept_ref, ko_kept_ref):
    part, width = qv_ref.shape
    for number, (left, right) in enumerate(((qv_ref, ko_ref), (qv_x_ref, ko_y_ref))):
        at = slice(number * part, (number + 1) * part)
        qv_near_ref[at, :] = left[...]
        ko_near_ref[at, :] = right[...]
        qv_kept_ref[at, :] = left[...]
        ko_kept_ref[at, :] = right[...]
        both_ref[at, :width] = left[...]
        both_ref[at, width:] = right[...]


def attend_kernel(head, *refs):
    normed_ref, bias_ref, perm_ref, x_ref, gain_ref, slots_ref, picked_ref = refs[:7]
    qv_refs, ko_refs = refs[7:11], refs[11:15]
    q_ref, k_ref, v_ref, probs_ref, mixed_ref, mixed_other_ref = refs[15:21]
    middle_ref, router_ref, gate_ref, keep_ref, send_ref = refs[21:26]
    wqv, wk, wo = refs[26:]
    experts = router_ref.shape[1]
    model = x_ref.shape[1]

    fill_x_first(qv_refs, wqv)
    fill_y_first(ko_refs, wk, (0, 0, 2 * model, 0))
    fill_y_first(ko_refs, wo, (model, model, 3 * model, model))
    normed = normed_ref[...]
    mixed = []
    for group in range(model // GROUP):
        at = slice(group * GROUP, (group + 1) * GROUP)
        q = mm(normed, wqv[:, at]).astype(BF)
        k = mm(normed, wk[:, at]).astype(BF)
        v = mm(normed, wqv[:, model + group * GROUP : model + (group + 1) * GROUP]).astype(BF)
        q_ref[:, at] = q
        k_ref[:, at] = k
        v_ref[:, at] = v
        for h in range(GROUP // head):
            part = slice(h * head, (h + 1) * head)
            number = group * (GROUP // head) + h
            scores = mm_nt(q[:, part], k[:, part]) + bias_ref[number]
            exponent = jnp.exp(scores - jnp.max(scores, axis=-1, keepdims=True))
            probs = exponent / jnp.sum(exponent, axis=-1, keepdims=True)
            probs_ref[number] = probs
            mixed.append(mm(probs.astype(BF), v[:, part]))
    perm = perm_ref[...]
    mixed_in_order = mm(jnp.concatenate(mixed, axis=1).astype(BF), perm).astype(BF)
    mixed_ref[...] = mixed_in_order[:, : model // 2]
    mixed_other_ref[...] = mixed_in_order[:, model // 2 :]
    middle = x_ref[...].astype(F32) + mm(mixed_in_order, wo[:, :model])
    middle_ref[...] = middle
    scale = lax.rsqrt(jnp.mean(middle * middle, axis=-1, keepdims=True) + EPSILON)
    ffn_in = (middle * scale * gain_ref[...]).astype(BF)
    router = mm(perm, wo[:, model:]).astype(BF)[:, :experts]
    router_ref[...] = router
    rows = mm(slots_ref[...], ffn_in).astype(BF)
    gate_ref[...] = gate_of(ffn_in, router, picked_ref[...])[1]
    half = rows.shape[0] // 2
    keep_ref[...] = rows[:half]
    send_ref[...] = rows[half:]


def join(refs, out_ref):
    base = 0
    for ref in refs:
        size = ref.shape[0]
        out_ref[base : base + size, :] = ref[...]
        base += size


def part_out(v, refs):
    base = 0
    for ref in refs:
        size = ref.shape[0]
        ref[...] = v[base : base + size]
        base += size


def load_kernel(after_ref, w1_ref, w2_ref, w1_out, w2_out, token_ref, sems):
    copies = []
    for ref, out_ref in ((w1_ref, w1_out), (w2_ref, w2_out)):
        rows = ref.shape[1] // 4
        for part in range(4):
            at = pl.ds(part * rows, rows)
            copies.append(pltpu.make_async_copy(ref.at[0, at], out_ref.at[at], sems.at[len(copies)]))
    for copy in copies:
        copy.start()
    token_ref[...] = jnp.zeros_like(token_ref)
    for copy in copies:
        copy.wait()


def hidden_grad_kernel(first_ref, second_ref, w2_ref, first_out, second_out):
    rows = first_ref.shape[0]
    dy = jnp.concatenate([first_ref[...], second_ref[...]], axis=0)
    width = first_out.shape[1] // 3
    for part in range(3):
        at = slice(part * width, (part + 1) * width)
        both = mm_nt(dy, w2_ref[at, :])
        first_out[:, at] = both[:rows]
        second_out[:, at] = both[rows:]


def expert_kernel(pieces, own_ref, *refs):
    rows_refs, dy = refs[:pieces], refs[pieces]
    router_ref, w1_ref, w2_ref, hidden_grad_ref = refs[pieces + 1 : pieces + 5]
    refs = refs[pieces + 5 :]
    back_refs, result_refs = refs[:pieces], refs[pieces : 2 * pieces]
    router_grad_ref, rows = refs[2 * pieces :]
    own = own_ref[0]
    join(rows_refs, rows)
    picked = one_lane((rows.shape[0], router_ref.shape[1]), own)
    router_probs, gate = gate_of(rows[...], router_ref[...], picked)
    result, back = 0.0, 0.0
    width = w1_ref.shape[1] // 2
    for part in range(2):
        at = slice(part * width, (part + 1) * width)
        hidden, slope = gelu_parts(mm(rows[...], w1_ref[:, at]))
        result += mm(hidden.astype(BF), w2_ref[at, :])
        pre_grad = (hidden_grad_ref[:, at] * gate * slope).astype(BF)
        back += mm_nt(pre_grad, w1_ref[:, at])
    returned = result.astype(BF)
    part_out(returned, result_refs)
    gate_grad = jnp.sum(dy[...].astype(F32) * returned.astype(F32), axis=-1, keepdims=True)
    logit_grad = (router_probs * (picked - gate) * gate_grad).astype(BF)
    router_grad_ref[...] = mm_tn(logit_grad, rows[...])
    part_out((back + mm_nt(logit_grad, router_ref[...])).astype(BF), back_refs)


def expert_grad_rows(pieces, refs, own_ref, router_ref, rows_all, branch_all):
    join(refs[:pieces], rows_all)
    join(refs[pieces:], branch_all)
    picked = one_lane((rows_all.shape[0], router_ref.shape[1]), own_ref[0])
    gate = gate_of(rows_all[...], router_ref[...], picked)[1]
    branch_all[...] = (branch_all[...].astype(F32) * gate).astype(BF)


def expert_grad_part(rows, branch, w1, w2):
    hidden, slope = gelu_parts(mm(rows, w1))
    pre_grad = (mm_nt(branch, w2) * slope).astype(BF)
    return mm_tn(rows, pre_grad), mm_tn(hidden.astype(BF), branch)


def first_expert_grad_kernel(pieces, own_ref, place_ref, *refs):
    router_ref, w1_ref, w2_ref, g1_ref, g2_ref, rows_all, branch_all = refs[2 * pieces :]
    expert_grad_rows(pieces, refs[: 2 * pieces], own_ref, router_ref, rows_all, branch_all)
    width = g1_ref.shape[1]
    for part in range(width // GROUP):
        at = pl.ds(pl.multiple_of(place_ref[0] * width + part * GROUP, GROUP), GROUP)
        here = slice(part * GROUP, (part + 1) * GROUP)
        g1, g2 = expert_grad_part(rows_all[...], branch_all[...], w1_ref[:, at], w2_ref[at, :])
        g1_ref[:, here] = g1
        g2_ref[here, :] = g2


def next_expert_grad_kernel(pieces, own_ref, place_ref, *refs):
    router_ref, w1_ref, w2_ref, before1_ref, before2_ref, g1_ref, g2_ref, rows_all, branch_all = refs[2 * pieces :]
    step = pl.program_id(0)

    @pl.when(step == 0)
    def _():
        expert_grad_rows(pieces, refs[: 2 * pieces], own_ref, router_ref, rows_all, branch_all)

    width = before1_ref.shape[1]
    at = pl.ds(pl.multiple_of(place_ref[0] * width + step * GROUP, GROUP), GROUP)
    here = pl.ds(pl.multiple_of(step * GROUP, GROUP), GROUP)
    g1, g2 = expert_grad_part(rows_all[...], branch_all[...], w1_ref[:, at], w2_ref[at, :])
    g1_ref[0] = g1 + before1_ref[:, here]
    g2_ref[0] = g2 + before2_ref[here, :]


def expert_grad_kernel(pieces, more, place_ref, *refs):
    del place_ref
    rows_refs, dy_refs, refs = refs[:pieces], refs[pieces : 2 * pieces], refs[2 * pieces :]
    own_ref, router_ref, w1_ref, w2_ref = refs[:4]
    g1_ref, g2_ref, rows_all, branch_all = refs[-4:]

    @pl.when(pl.program_id(0) == 0)
    def _():
        join(rows_refs, rows_all)
        join(dy_refs, branch_all)
        picked = one_lane((rows_all.shape[0], router_ref.shape[1]), own_ref[0])
        gate = gate_of(rows_all[...], router_ref[...], picked)[1]
        branch_all[...] = (branch_all[...].astype(F32) * gate).astype(BF)

    rows, branch = rows_all[...], branch_all[...]
    hidden, slope = gelu_parts(mm(rows, w1_ref[0]))
    pre_grad = (mm_nt(branch, w2_ref[0]) * slope).astype(BF)
    g1, g2 = mm_tn(rows, pre_grad), mm_tn(hidden.astype(BF), branch)
    if more:
        g1, g2 = g1 + refs[4][0], g2 + refs[5][0]
    g1_ref[0] = g1
    g2_ref[0] = g2


def middle_kernel(head, pieces, *refs):
    keep_refs, refs = refs[:pieces], refs[pieces:]
    (send_ref, slots_t_ref, dy_ref, middle_ref, gain_ref, perm_ref, probs_ref, other_ref) = refs[:8]
    ko_refs = refs[8:12]
    (middle_grad_ref, gain_grad_ref, mixed_grad_ref, grads_ref, wo, mixed_grad) = refs[12:]
    rows, model = dy_ref.shape
    step = pl.program_id(0)
    keep_rows = send_ref.shape[0] // pieces

    @pl.when(step == 0)
    def _():
        fill_y_first(ko_refs, wo, (model, model, 3 * model, model))
        back = jnp.concatenate([ref[:keep_rows, :] for ref in keep_refs] + [send_ref[...]], axis=0)
        ffn_grad = mm(slots_t_ref[...], back)
        middle = middle_ref[...]
        scale = lax.rsqrt(jnp.mean(middle * middle, axis=-1, keepdims=True) + EPSILON)
        gain_grad_ref[...] = jnp.sum(ffn_grad * middle * scale, axis=0, keepdims=True)
        scaled = ffn_grad * gain_ref[...]
        along = jnp.mean(scaled * middle, axis=-1, keepdims=True)
        middle_grad = dy_ref[...].astype(F32) + scale * scaled - middle * (scale * scale * scale * along)
        middle_grad_ref[...] = middle_grad
        attn_grad = middle_grad.astype(BF)
        grads_ref[rows : 2 * rows, :] = attn_grad
        grads_ref[2 * rows :, : model // 2] = other_ref[: rows // 2, :]
        grads_ref[2 * rows :, model // 2 :] = other_ref[rows // 2 :, :]
        in_order = mm_nt(attn_grad, wo[...]).astype(BF)
        every = mm_nt(in_order, perm_ref[...]).astype(BF)
        mixed_grad_ref[...] = every
        for g in range(mixed_grad.shape[0]):
            mixed_grad[g] = every[:, g * GROUP : (g + 1) * GROUP]

    grads = mixed_grad[step]
    parts = [
        mm_tn(probs_ref[h].astype(BF), grads[:, h * head : (h + 1) * head]) for h in range(GROUP // head)
    ]
    value_grad = jnp.concatenate(parts, axis=1).astype(BF)
    at = pl.ds(pl.multiple_of(step * GROUP, GROUP), GROUP)
    grads_ref[:rows, at] = value_grad


def weight_grad_kernel(normed_ref, side_ref, mixed_ref, vo_ref, vo_side_ref, qk_ref, qk_side_ref, *outs):
    a_ref, a_low_ref, b_ref, b_low_ref = outs
    rows = normed_ref.shape[0]
    width = side_ref.shape[1] // 2
    model = normed_ref.shape[1]
    half, part = width // 2, width // 4

    def unpack(v):
        return [v[:, :width], v[:, width:]]

    normed = jnp.concatenate([normed_ref[:, :width], *unpack(side_ref[...])], axis=0)
    mixed = jnp.concatenate([mixed_ref[...], *unpack(vo_side_ref[2 * rows :, :])], axis=0)
    for number, (left, own, side) in enumerate(
        ((normed, vo_ref, vo_side_ref), (normed, qk_ref, qk_side_ref), (mixed, vo_ref, vo_side_ref), (normed, qk_ref, qk_side_ref))
    ):
        here = slice(0, rows) if number < 2 else slice(rows, 2 * rows)
        total = mm_tn(left, jnp.concatenate([own[here, :], side[here, :]], axis=0))
        at = slice(number % 2 * model, (number % 2 + 1) * model)
        if number < 2:
            a_ref[:, at] = total[:half]
            a_low_ref[:, at] = total[half:].astype(BF)
        else:
            b_ref[:part, at] = total[:part]
            b_ref[part:, at] = total[half : half + part]
            b_low_ref[:part, at] = total[part:half].astype(BF)
            b_low_ref[part:, at] = total[half + part :].astype(BF)


def fold_near_kernel(a_ref, a_got_ref, b_ref, b_got_ref, small_ref, small_got_ref, a2_ref, a2_low_ref, b2_ref, b2_low_ref):
    a = a_ref[...] + a_got_ref[...].astype(F32)
    b = b_ref[...] + b_got_ref[...].astype(F32)
    small = small_ref[...] + small_got_ref[...]
    half = a.shape[0] // 2
    a2_ref[...] = a[:half]
    a2_low_ref[:half, :] = a[half:].astype(BF)
    a2_low_ref[half:, :] = jnp.concatenate([small, jnp.zeros_like(small)], axis=1).astype(BF)
    b2_ref[...] = b[:half]
    b2_low_ref[...] = b[half:].astype(BF)


def fold_sums(a_ref, a_low_ref, a_got_ref, b_ref, b_got_ref):
    rows = a_ref.shape[0]
    a = a_ref[...] + a_got_ref[:rows, :].astype(F32)
    b = b_ref[...] + b_got_ref[...].astype(F32)
    model = a.shape[1] // 2
    return a, b, a_low_ref[rows:, :model].astype(F32) + a_got_ref[rows:, :model].astype(F32)


def fold_far_kernel(a_ref, a_low_ref, a_got_ref, b_ref, b_got_ref, keep_ref, *low_refs):
    a, b, small = fold_sums(a_ref, a_low_ref, a_got_ref, b_ref, b_got_ref)
    model = a.shape[1] // 2
    shard = a.shape[0] // 4
    for k in range(4):
        rows = slice(k * shard, (k + 1) * shard)
        blocks = [v[rows, half * model : (half + 1) * model] for v in (a, b) for half in range(2)]
        if k:
            low_refs[k - 1][...] = jnp.concatenate([small, *blocks], axis=0).astype(BF)
        else:
            keep_ref[...] = jnp.concatenate(blocks, axis=0)


def fold_last_kernel(heads, device_ref, keep_ref, own_ref, *refs):
    got, outs = [ref[...].astype(F32) for ref in refs[:3]], refs[3:]
    shard = outs[0].shape[0]
    experts = outs[7].shape[0]
    first = got[0].shape[0] - 4 * shard
    total = keep_ref[...] + ((got[0][first:] + got[1][first:]) + got[2][first:])
    for number in range(4):
        outs[number][...] = total[number * shard : (number + 1) * shard]
    small = (own_ref[...][:first].astype(F32) + got[0][:first]) + (got[1][:first] + got[2][:first])
    outs[4][...] = small[experts : experts + 1]
    outs[5][...] = small[experts + 1 : experts + 2]
    every = outs[6].shape[1]
    line = small[experts + 2 : experts + 3]
    outs[6][...] = jnp.concatenate([line[:, h * every : (h + 1) * every] for h in range(heads)], axis=0)
    spots = (small.shape[1], shard)
    mine = lax.broadcasted_iota(jnp.int32, spots, 0) == lax.broadcasted_iota(jnp.int32, spots, 1) + device_ref[0] * shard
    outs[7][...] = lax.dot_general(
        small[:experts], mine.astype(F32), (((1,), (0,)), ((), ())), precision=PRECISE, preferred_element_type=F32
    )


def score_grad_kernel(head, mixed_grad_ref, v_ref, q_ref, k_ref, probs_ref, grads_ref, along_ref):
    rows = q_ref.shape[0]
    flip = (
        lax.broadcasted_iota(jnp.int32, (rows, rows), 0) + lax.broadcasted_iota(jnp.int32, (rows, rows), 1)
        == rows - 1
    ).astype(F32).astype(BF)
    q_parts, k_parts = [], []
    for h in range(GROUP // head):
        part = slice(h * head, (h + 1) * head)
        probs = probs_ref[h]
        prob_grad = mm_nt(mixed_grad_ref[:, part], v_ref[:, part])
        inner = jnp.sum(probs * prob_grad, axis=-1, keepdims=True)
        score_grad = (probs * (prob_grad - inner)).astype(BF)
        q_parts.append(mm(score_grad, k_ref[:, part]))
        k_parts.append(mm_tn(score_grad, q_ref[:, part]))
        flipped = mm(flip, score_grad)
        half = rows // 2
        upper, lower = flipped[:half], flipped[half:]
        wide = jnp.concatenate(
            [upper[:, :half], upper[:, half:] + lower[:, :half], lower[:, half:], jnp.zeros_like(upper[:, :half])], axis=1
        )
        along_ref[h] = jnp.sum(pltpu.roll(wide, 0, 1, stride=1, stride_axis=0), axis=0, keepdims=True)
    grads_ref[:rows, :] = jnp.concatenate(q_parts, axis=1).astype(BF)
    grads_ref[rows:, :] = jnp.concatenate(k_parts, axis=1).astype(BF)


def input_kernel(table_rows, *refs):
    qk_ref, vo_ref, x_ref, gain_ref, perm_ref, middle_grad_ref = refs[:6]
    along_ref, buckets_ref, gain_next_ref, router_a_ref, router_b_ref = refs[6:11]
    qv_refs, wk_refs = refs[11:15], refs[15:19]
    input_grad_ref, small_ref, weight, wide = refs[19:]
    rows = x_ref.shape[0]
    experts, heads = router_a_ref.shape[0], along_ref.shape[0]
    every = table_rows
    onehot = (
        lax.broadcasted_iota(jnp.int32, (every, buckets_ref.shape[1]), 0) == buckets_ref[...]
    ).astype(F32)
    model = x_ref.shape[1]
    small_ref[...] = jnp.zeros_like(small_ref)
    small_ref[:experts, :] = router_a_ref[...] + router_b_ref[...]
    small_ref[experts + 1 : experts + 2, :] = gain_next_ref[...]
    along = jnp.concatenate([along_ref[h] for h in range(heads)], axis=0)
    table = lax.dot_general(
        along, onehot, (((1,), (1,)), ((), ())), precision=PRECISE, preferred_element_type=F32
    )
    small_ref[experts + 2 : experts + 3, : heads * every] = jnp.concatenate(
        [table[h : h + 1] for h in range(heads)], axis=1
    )
    fill_x_first(qv_refs, wide)
    total = mm_nt(jnp.concatenate([qk_ref[:rows, :], vo_ref[:rows, :]], axis=1), wide[...])
    fill_y_first(wk_refs, weight)
    total += mm_nt(qk_ref[rows:, :], weight[...])
    perm = perm_ref[...]
    high = total.astype(BF)
    low = (total - high.astype(F32)).astype(BF)
    normed_grad = mm_nt(high, perm) + mm_nt(low, perm)
    x = x_ref[...].astype(F32)
    scale = lax.rsqrt(jnp.mean(x * x, axis=-1, keepdims=True) + EPSILON)
    small_ref[experts : experts + 1, :] = jnp.sum(normed_grad * x * scale, axis=0, keepdims=True)
    scaled = normed_grad * gain_ref[...]
    along = jnp.mean(scaled * x, axis=-1, keepdims=True)
    input_grad_ref[...] = middle_grad_ref[...] + scale * scaled - x * (scale * scale * scale * along)


class Places:
    def __init__(self):
        self.experts = lax.axis_size("expert")
        self.nz = self.experts // 2
        self.dp = lax.axis_size("dp")
        self.near = self.nz == 4
        me = lax.axis_index("expert")
        self.z, self.c = me // 2, me % 2
        self.row = lax.axis_index("dp")
        self.columns = [[2 * z + c for z in range(self.nz)] for c in range(2)]

    def core(self, v):
        return lax.ppermute(v, "expert", [(i, i ^ 1) for i in range(self.experts)])

    def x(self, v):
        return lax.ppermute(v, "dp", [(i, i ^ 1) for i in range(self.dp)])

    def y(self, v):
        return lax.ppermute(v, "dp", [(i, i ^ 2) for i in range(self.dp)])

    def far(self, v, k):
        return lax.ppermute(v, "expert", [(i, i ^ (2 * k)) for i in range(self.experts)])

    def apart(self, v):
        return lax.all_to_all(
            v, "expert", split_axis=0, concat_axis=0, tiled=True, axis_index_groups=self.columns
        )

    def gather_z(self, v):
        if self.near:
            got = {k: self.far(v, k) for k in FAR_FIRST}
            return jnp.concatenate([v, got[1], got[2], got[3]], axis=0)
        return lax.all_gather(v, "expert", axis=0, tiled=True, axis_index_groups=self.columns)

    def z_order(self):
        steps = jnp.arange(self.nz, dtype=jnp.int32)
        return self.z ^ steps if self.near else steps

    def scatter_z(self, v):
        size = v.shape[0] // self.nz
        if self.near:
            total = v[:size]
            low = v.astype(BF)
            for k in FAR_FIRST:
                total = total + self.far(low[k * size : (k + 1) * size], k).astype(F32)
            return total
        got = self.apart(v.astype(BF).reshape(self.nz, size, v.shape[1]))
        mine = lax.dynamic_slice_in_dim(v, self.z * size, size, axis=0)
        steps = jnp.arange(self.nz, dtype=jnp.int32)[:, None, None]
        return mine + jnp.sum(jnp.where(steps == self.z, 0.0, got.astype(F32)), axis=0)

    def swap(self, blocks):
        got = {k: self.far(blocks[k], k) for k in FAR_FIRST}
        return [blocks[0], got[1], got[2], got[3]]

    def swap_relay(self, blocks, hold):
        size = blocks[0].shape[0]
        first = self.far(jnp.concatenate([blocks[2], blocks[3]], axis=0), 2)
        onward = after(jnp.concatenate([blocks[1], first[size:]], axis=0), *hold)
        second = self.far(onward, 1)
        return [blocks[0], second[:size], first[:size], second[size:]], onward

    def by_z(self, keep, got):
        room = keep.shape[0] // self.nz
        both = jnp.concatenate([v.reshape(self.nz, room, keep.shape[1]) for v in (keep, got)], axis=1)
        return [both[k] for k in range(4)] if self.near else both

    def halves(self, moved):
        moved = moved.reshape(-1, moved.shape[-1])
        half = moved.shape[0] // 2
        return [moved[:half]], [moved[half:]]

    def to_owners(self, keep, got, hold):
        blocks = self.by_z(keep, got)
        if self.near:
            blocks = all_after([blocks[k] for k in range(4)], *hold)
            two, one = self.far(blocks[2], 2), self.far(blocks[1], 1)
            three = self.far(after(blocks[3], two), 3)
            return [blocks[0], two], [one, three]
        return self.halves(self.apart(blocks))

    def send_more(self, blocks, k, hold):
        return self.far(after(blocks[k], *hold), k) if self.near else blocks

    def from_owners(self, first, second):
        width = first[0].shape[1]
        both = self.apart(jnp.concatenate([*first, *second], axis=0).reshape(self.nz, -1, width))
        room = both.shape[1] // 2
        return [both[:, :room].reshape(-1, width)], both[:, room:].reshape(-1, width)

    def to_senders(self, first, second):
        if self.near:
            two = self.far(first[1], 2)
            one, three = all_after(second, two)
            three, one = self.far(three, 3), self.far(one, 1)
            moved = [first[0], one, two, three]
            room = one.shape[0] // 2
            return moved, self.core(jnp.concatenate([v[room:] for v in moved], axis=0))
        keep, other = self.from_owners(first, second)
        return keep, self.core(other)

    def gather_far(self, a, b):
        return self.y(a), self.x(b)


def per_device(
    tokens,
    cotangent,
    routes,
    buckets,
    norm_attn,
    norm_ffn,
    rel_table,
    query_weight,
    key_weight,
    value_weight,
    out_weight,
    router_weight,
    expert_in,
    expert_out,
):
    at = Places()
    rows, model = tokens.shape
    head_count = rel_table.shape[1]
    head = model // head_count
    bucket_count = rel_table.shape[0]
    experts = router_weight.shape[1]
    shard = query_weight.shape[0]
    nz = at.nz
    room = max(2, 2 * rows // at.experts)
    slots = experts * room
    half = slots // 2
    groups = model // GROUP
    per_group = GROUP // head
    hidden = expert_in.shape[2]

    def in_hbm(*values):
        return [pltpu.with_memory_space_constraint(v, pltpu.HBM) for v in values]

    expert_in, expert_out = in_hbm(expert_in, expert_out)
    own = lax.axis_index("expert").astype(jnp.int32).reshape(1)
    smem = pl.BlockSpec(memory_space=pltpu.SMEM)

    core_of = at.c ^ jnp.arange(2, dtype=jnp.int32)
    row_of = at.row ^ jnp.arange(4, dtype=jnp.int32)
    device_of = (
        row_of[None, :, None] * at.experts + at.z_order()[None, None, :] * 2 + core_of[:, None, None]
    )
    order = (
        device_of[..., None] * shard + jnp.arange(shard, dtype=jnp.int32)
    ).reshape(1, model).astype(jnp.int32)

    shards = (query_weight, value_weight, key_weight, out_weight, router_weight.T)
    packed = pl.pallas_call(
        pack_kernel,
        out_shape=shape_of((shard, 4 * model + 128), BF),
        in_specs=[pl.BlockSpec(memory_space=pltpu.VMEM)] * 5,
        out_specs=pl.BlockSpec(memory_space=pltpu.VMEM),
        name="pack",
    )(*shards)
    line = at.gather_z(packed)
    span = 2 * rows
    bucket_line = jnp.pad(buckets, (0, 1), constant_values=-1).reshape(1, span)
    slots_map, slots_t, dy_keep, dy_send, perm, normed, picked, gain_attn, gain_ffn = pl.pallas_call(
        functools.partial(route_kernel, room, nz, at.near),
        out_shape=(
            shape_of((slots, rows), BF),
            shape_of((rows, slots), BF),
            shape_of((half, model), BF),
            shape_of((half + rows // 2, model), BF),
            shape_of((model, model), BF),
            shape_of((rows, model), BF),
            shape_of((rows, experts), F32),
            shape_of((1, model), F32),
            shape_of((1, model), F32),
        ),
        in_specs=[smem] + [pl.BlockSpec(memory_space=pltpu.VMEM)] * 6,
        compiler_params=params(),
        cost_estimate=cost(2 * rows * slots * model, 4 * rows * model),
        name="route",
    )(
        jnp.stack([at.z, at.c]).astype(jnp.int32),
        routes.reshape(1, rows),
        cotangent,
        order,
        tokens,
        norm_attn.reshape(1, model),
        norm_ffn.reshape(1, model),
    )
    dy_got = at.core(dy_send)
    normed_side = dy_got[half:]
    dy_got = dy_got[:half]
    qv, ko = line[:, : 2 * model], line[:, 2 * model :]
    qv, ko = all_after([qv, ko], slots_t)
    dy_keep, dy_got = all_after([dy_keep, dy_got], qv, ko)
    part_rows = qv.shape[0]
    dy_blocks = at.by_z(dy_keep, dy_got)
    dy_one = at.send_more(dy_blocks, 1, (dy_blocks,))
    bias = pl.pallas_call(
        bias_kernel,
        grid=(groups,),
        out_shape=shape_of((head_count, rows, rows), F32),
        in_specs=[full((1, span)), full((bucket_count, head_count))],
        out_specs=pl.BlockSpec((per_group, rows, rows), lambda g: (g, 0, 0)),
        scratch_shapes=[pltpu.VMEM((head_count, 1, span), F32)],
        compiler_params=params(),
        cost_estimate=cost(1 << 20, 4 * head_count * rows * rows),
        name="bias",
    )(after(bucket_line, slots_t), rel_table)
    qv_near, ko_near, both_near, qv_kept, ko_kept = pl.pallas_call(
        near_kernel,
        out_shape=tuple(pltpu.HBM((2 * part_rows, width), BF) for width in (2 * model, 2 * model + 128, 4 * model + 128))
        + tuple(shape_of((2 * part_rows, width), BF) for width in (2 * model, 2 * model + 128)),
        in_specs=[pl.BlockSpec(memory_space=pltpu.VMEM)] * 4,
        out_specs=tuple(pl.BlockSpec((2 * part_rows, width), lambda: (0, 0)) for width in (2 * model, 2 * model + 128, 4 * model + 128))
        + (pl.BlockSpec(memory_space=pltpu.VMEM),) * 2,
        compiler_params=params(),
        name="near",
    )(after(qv, dy_one, bias), at.x(qv), ko, at.y(ko))
    qv_far, ko_far = at.gather_far(qv_near, ko_near)
    w_first, w_second, loaded = pl.pallas_call(
        load_kernel,
        out_shape=(pltpu.VMEM((model, hidden), BF), pltpu.VMEM((hidden, model), BF), shape_of((8, 128), F32)),
        in_specs=[pl.BlockSpec(memory_space=pltpu.VMEM)] + [pl.BlockSpec(memory_space=pl.ANY)] * 2,
        out_specs=(pl.BlockSpec(memory_space=pltpu.VMEM),) * 3,
        scratch_shapes=[pltpu.SemaphoreType.DMA((8,))],
        compiler_params=params(),
        name="load",
    )(bias[0, :8, :128], expert_in, expert_out)
    both_side = at.core(both_near)
    dy_two = at.send_more(dy_blocks, 2, (qv_near, dy_one))
    qv_far, ko_far, dy_two = all_after([qv_far, ko_far, dy_two], both_side)
    dy_three = at.send_more(dy_blocks, 3, (qv_far, ko_far, dy_two))
    qv_pieces = (qv_kept, qv_far, both_side, at.core(qv_far))
    ko_pieces = (ko_kept, ko_far, both_side, at.core(ko_far))
    if at.near:
        dy_a = jnp.concatenate([dy_blocks[0], dy_two], axis=0)
    else:
        (dy_a,), (dy_b,) = at.halves(at.apart(dy_blocks))
    dy_a_later = after(dy_a, qv_far, ko_far)
    dy_ax, dy_ay = at.x(dy_a_later), at.y(dy_a_later)

    quarter = qv_near.shape[0]
    wide = ko_near.shape[1]
    side_wide = both_side.shape[1]
    head_block = pl.BlockSpec((per_group, rows, rows), lambda g: (g, 0, 0))
    in_vmem = pl.BlockSpec(memory_space=pltpu.VMEM)
    ko_full = [full((quarter, wide)), full((quarter, wide)), full((quarter, side_wide)), full((quarter, wide))]
    attend_shapes = [((rows, model), BF)] * 3 + [
        ((head_count, rows, rows), F32),
        ((rows, model // 2), BF),
        ((rows, model // 2), BF),
        ((rows, model), F32),
        ((model, experts), BF),
        ((rows, 1), F32),
        ((half, model), BF),
        ((half, model), BF),
    ]
    q, k, v, probs, mixed, mixed_other, middle, router, gate, keep, send = pl.pallas_call(
        functools.partial(attend_kernel, head),
        out_shape=tuple(pltpu.HBM(*v) if v[0] == (rows, 1) else shape_of(*v) for v in attend_shapes),
        in_specs=[in_vmem] * 3
        + [pl.BlockSpec((rows, model), lambda: (0, 0)), in_vmem]
        + [pl.BlockSpec((slots, rows), lambda: (0, 0)), pl.BlockSpec((rows, experts), lambda: (0, 0))]
        + [in_vmem] * 8,
        out_specs=(in_vmem,) * 8 + (pl.BlockSpec((rows, 1), lambda: (0, 0)),) + (in_vmem,) * 2,
        scratch_shapes=[
            pltpu.VMEM((model, 2 * model), BF),
            pltpu.VMEM((model, model), BF),
            pltpu.VMEM((model, wide - model), BF),
        ],
        compiler_params=params(),
        name="attend",
    )(
        normed,
        bias,
        perm,
        *in_hbm(tokens),
        after(gain_ffn, loaded),
        *in_hbm(slots_map, picked),
        *qv_pieces,
        *ko_pieces,
    )

    got = at.core(after(send, dy_three))
    first, second = at.to_owners(keep, got, (dy_ax, dy_ay))
    if at.near:
        dy_b = jnp.concatenate([dy_one, dy_three], axis=0)
    dy_b_later = after(dy_b, got, dy_ax, dy_ay)
    dy_by, dy_bx = at.y(dy_b_later), at.x(dy_b_later)
    hidden_grads = pl.pallas_call(
        hidden_grad_kernel,
        out_shape=(shape_of((half, hidden), F32),) * 2,
        in_specs=[in_vmem] * 3,
        out_specs=(in_vmem,) * 2,
        compiler_params=params(),
        name="hidden_grads",
    )(dy_a, dy_b, w_second)

    def expert(rows_list, dy_rows, hidden_grad, router_in):
        sizes = [v.shape[0] for v in rows_list]
        count = sum(sizes)
        shapes = [((n, model), BF) for n in sizes * 2] + [((experts, model), F32), ((count, model), BF)]
        outs = pl.pallas_call(
            functools.partial(expert_kernel, len(sizes)),
            out_shape=tuple(shape_of(*v) for v in shapes),
            in_specs=[smem] + [in_vmem] * (len(sizes) + 5),
            out_specs=(in_vmem,) * len(shapes),
            compiler_params=params(),
            name="expert",
        )(own, *rows_list, dy_rows, router_in, w_first, w_second, hidden_grad)
        n = len(sizes)
        return list(outs[:n]), list(outs[n : 2 * n]), outs[2 * n], outs[2 * n + 1]

    dy_ax_later, dy_by_later = all_after([dy_ax, dy_by], first[-1], dy_bx, hidden_grads[1])
    dy_axy, dy_byx = at.y(dy_ax_later), at.x(dy_by_later)
    back_a, returned_a, router_grad_a, rows_a = expert(first, dy_a, hidden_grads[0], after(router, dy_by, dy_bx))
    rows_ax, rows_ay = at.x(rows_a), at.y(rows_a)
    back_b, returned_b, router_grad_b, rows_b = expert(
        second, dy_b, hidden_grads[1], after(router, router_grad_a, dy_axy, dy_byx)
    )
    rows_b_later = after(rows_b, rows_ax, rows_ay)
    rows_by, rows_bx = at.y(rows_b_later), at.x(rows_b_later)
    back_keep, back_send = at.to_senders(back_a, back_b)

    slice_width = hidden // at.dp
    place = at.row.astype(jnp.int32).reshape(1)

    steps = slice_width // GROUP

    def expert_grads(rows_list, dy_list, router_in, before):
        sizes = [v.shape[0] for v in rows_list]
        count = sum(sizes)
        outs = (
            pl.BlockSpec((1, model, GROUP), lambda g, place: (0, 0, g)),
            pl.BlockSpec((1, GROUP, model), lambda g, place: (0, g, 0)),
        )
        return pl.pallas_call(
            functools.partial(expert_grad_kernel, len(sizes), bool(before)),
            grid_spec=pltpu.PrefetchScalarGridSpec(
                num_scalar_prefetch=1,
                grid=(steps,),
                in_specs=[full((n, model)) for n in sizes * 2]
                + [
                    smem,
                    full((model, experts)),
                    pl.BlockSpec((1, model, GROUP), lambda g, place: (0, 0, place[0] * steps + g)),
                    pl.BlockSpec((1, GROUP, model), lambda g, place: (0, place[0] * steps + g, 0)),
                ]
                + list(outs if before else ()),
                out_specs=outs,
                scratch_shapes=[pltpu.VMEM((count, model), BF), pltpu.VMEM((count, model), BF)],
            ),
            out_shape=(pltpu.HBM((1, model, slice_width), F32), pltpu.HBM((1, slice_width, model), F32)),
            compiler_params=params(),
            cost_estimate=cost(8 * count * model * slice_width, 20 * model * slice_width),
            name="expert_grads",
        )(place, *in_hbm(*rows_list, *dy_list), own, router_in, expert_in, expert_out, *in_hbm(*before))

    whole_vmem = pl.BlockSpec(memory_space=pltpu.VMEM)

    def first_expert_grads(rows_list, dy_list, router_in):
        count = sum(v.shape[0] for v in rows_list)
        ins = [*rows_list, *dy_list, router_in, w_first, w_second]
        return pl.pallas_call(
            functools.partial(first_expert_grad_kernel, len(rows_list)),
            out_shape=(shape_of((model, slice_width), F32), shape_of((slice_width, model), F32)),
            in_specs=[smem] * 2 + [whole_vmem] * len(ins),
            out_specs=(whole_vmem,) * 2,
            scratch_shapes=[pltpu.VMEM((count, model), BF)] * 2,
            compiler_params=params(24),
            name="expert_grads",
        )(own, place, *ins)

    def next_expert_grads(rows_list, dy_list, router_in, before):
        count = sum(v.shape[0] for v in rows_list)
        pieces = [*rows_list, *dy_list]
        return pl.pallas_call(
            functools.partial(next_expert_grad_kernel, len(rows_list)),
            grid=(slice_width // GROUP,),
            out_shape=(pltpu.HBM((1, model, slice_width), F32), pltpu.HBM((1, slice_width, model), F32)),
            in_specs=[smem] * 2 + [full(v.shape) for v in pieces] + [whole_vmem] * 5,
            out_specs=(
                pl.BlockSpec((1, model, GROUP), lambda g: (0, 0, g)),
                pl.BlockSpec((1, GROUP, model), lambda g: (0, g, 0)),
            ),
            scratch_shapes=[pltpu.VMEM((count, model), BF)] * 2,
            compiler_params=params(24),
            name="expert_grads",
        )(own, place, *in_hbm(*pieces), router_in, w_first, w_second, *before)

    rows_axy, rows_byx = at.y(after(rows_ax, rows_by, rows_bx, back_send)), at.x(after(rows_by, rows_bx, back_send))

    middle_grad, gain_ffn_grad, mixed_grad, vo_grads = pl.pallas_call(
        functools.partial(middle_kernel, head, len(back_keep)),
        grid=(groups,),
        out_shape=(
            shape_of((rows, model), F32),
            shape_of((1, model), F32),
            shape_of((rows, model), BF),
            shape_of((2 * rows + rows // 2, model), BF),
        ),
        in_specs=[full(v.shape) for v in back_keep]
        + [
            full((half, model)),
            full((rows, slots)),
            full((rows, model)),
            full((rows, model)),
            full((1, model)),
            full((model, model)),
            head_block,
            full((rows, model // 2)),
        ]
        + ko_full,
        out_specs=(
            full((rows, model)),
            full((1, model)),
            full((rows, model)),
            full((2 * rows + rows // 2, model)),
        ),
        scratch_shapes=[pltpu.VMEM((model, model), BF), pltpu.VMEM((groups, rows, GROUP), BF)],
        compiler_params=params(),
        cost_estimate=cost(10 * rows * model * model, 12 * model * model),
        name="middle",
    )(*back_keep, back_send, slots_t, cotangent, middle, after(gain_ffn, rows_by, rows_bx), perm, probs, mixed_other, *ko_pieces)
    vo_side = at.core(vo_grads)
    qk_grads, along_grad = pl.pallas_call(
        functools.partial(score_grad_kernel, head),
        grid=(groups,),
        out_shape=(shape_of((2 * rows, model), BF), shape_of((head_count, 1, span), F32)),
        in_specs=[cols(rows, GROUP)] * 4 + [head_block],
        out_specs=(cols(2 * rows, GROUP), pl.BlockSpec((per_group, 1, span), lambda g: (g, 0, 0))),
        compiler_params=params(),
        cost_estimate=cost(8 * rows * model * model, 12 * model * model),
        name="score_grads",
    )(mixed_grad, v, q, k, probs)
    qk_side = at.core(after(qk_grads, vo_side, rows_axy, rows_byx))
    small_rows = -(-(experts + 3) // 16) * 16
    input_grad, small = pl.pallas_call(
        functools.partial(input_kernel, bucket_count),
        grid=(1,),
        out_shape=(shape_of((rows, model), F32), shape_of((small_rows, model), F32)),
        in_specs=[full((2 * rows, model)), full((2 * rows + rows // 2, model))]
        + [full((rows, model)), full((1, model)), full((model, model)), full((rows, model))]
        + [full((head_count, 1, span)), full((1, span)), full((1, model))]
        + [full((experts, model))] * 2
        + [full((quarter, 2 * model))] * 4
        + [pl.BlockSpec((quarter, model), lambda g, at=at_k: (0, at)) for at_k in (0, 0, 2, 0)],
        out_specs=(full((rows, model)), full((small_rows, model))),
        scratch_shapes=[pltpu.VMEM((model, model), BF), pltpu.VMEM((model, 2 * model), BF)],
        compiler_params=params(),
        cost_estimate=cost(10 * rows * model * model, 12 * model * model),
        name="inputs",
    )(
        qk_grads,
        vo_grads,
        tokens,
        gain_attn,
        perm,
        middle_grad,
        along_grad,
        bucket_line,
        gain_ffn_grad,
        router_grad_a,
        router_grad_b,
        *qv_pieces,
        *ko_pieces,
    )
    quarter_rows = model // 4

    def vmem_call(kernel, name, shapes, *ins):
        return pl.pallas_call(
            kernel,
            out_shape=tuple(shape_of(*v) for v in shapes),
            in_specs=[pl.BlockSpec(v.shape, lambda: (0, 0)) for v in ins],
            out_specs=tuple(pl.BlockSpec(v[0], lambda: (0, 0)) for v in shapes),
            compiler_params=params(),
            name=name,
        )(*ins)

    pair = 2 * model
    a, a_low, b, b_low = vmem_call(
        weight_grad_kernel,
        "weight_grads",
        [((quarter_rows, pair), F32), ((quarter_rows, pair), BF)] * 2,
        normed,
        normed_side,
        mixed,
        vo_grads,
        vo_side,
        qk_grads,
        qk_side,
    )
    small = small + after(at.core(small), a_low)
    a_got, b_got = at.y(a_low), at.x(b_low)
    small_got = at.y(small)
    if at.near:
        home_two = at.far(after(returned_a[1], a_low, b_low), 2)
    else:
        home_two = at.apart(jnp.concatenate([*returned_a, *returned_b], axis=0).reshape(nz, -1, model))
    near_sums = first_expert_grads(
        [rows_a, rows_b, rows_ax, rows_by], [dy_a, dy_b, dy_ax, dy_by], after(router, a_low, b_low)
    )
    eighth = quarter_rows // 2
    a, a_low, b, b_low = vmem_call(
        fold_near_kernel,
        "fold_near",
        [((eighth, pair), F32), ((eighth + small_rows, pair), BF), ((eighth, pair), F32), ((eighth, pair), BF)],
        a,
        after(a_got, near_sums[0], home_two),
        b,
        b_got,
        small,
        small_got,
    )
    a_got, b_got = at.x(a_low), at.y(b_low)
    mid_sums = next_expert_grads([rows_ay, rows_bx], [dy_ay, dy_bx], after(router, a_low, b_low), near_sums)
    if at.near:
        home = [at.far(v, k) for v, k in zip(all_after([returned_b[1], returned_b[0]], a_low, b_low), (3, 1))]
        home_blocks = [returned_a[0], home[1], home_two, home[0]]
        room = half // nz
        returned_keep = home_blocks
        returned_other = jnp.concatenate([v[room:] for v in home_blocks], axis=0)
    else:
        room = home_two.shape[1] // 2
        returned_keep = [home_two[:, :room].reshape(half, model)]
        returned_other = home_two[:, room:].reshape(half, model)
    if at.near:
        keep_sum, *low = vmem_call(
            fold_far_kernel,
            "fold_far",
            [((4 * shard, model), F32)] + [((small_rows + 4 * shard, model), BF)] * 3,
            a,
            a_low,
            after(a_got, mid_sums[0], *home),
            b,
            b_got,
        )
        hold = keep_sum
        got_z = {k: at.far(low[k - 1], k) for k in FAR_FIRST}
    else:
        a = a + a_got[:eighth].astype(F32)
        b = b + b_got.astype(F32)
        summed = (a_low[eighth:].astype(F32) + a_got[eighth:].astype(F32))[:, :model]
        hold = jnp.concatenate([a, b], axis=1)
        sums = at.scatter_z(hold)
        grad_value, grad_query, grad_proj, grad_key = [sums[:, n * model : (n + 1) * model] for n in range(4)]
        summed = lax.psum(summed, "expert", axis_index_groups=at.columns)
    returned_send = at.core(after(returned_other, hold))
    grad_in, grad_out_w = expert_grads([rows_axy, rows_byx], [dy_axy, dy_byx], after(router, hold), mid_sums)
    keep_rows = half // len(returned_keep)
    expert_result = mm(
        slots_t,
        jnp.concatenate([v[:keep_rows] for v in returned_keep] + [returned_send], axis=0),
    )
    output = (middle + gate * expert_result).astype(BF)
    device = (at.row * at.experts + lax.axis_index("expert")).astype(jnp.int32)
    if at.near:
        last_ins = [after(keep_sum, output, grad_in), low[0], *[got_z[k] for k in (1, 2, 3)]]
        last_shapes = [(shard, model)] * 4 + [(1, model)] * 2 + [(head_count, bucket_count), (experts, shard)]
        grad_value, grad_query, grad_proj, grad_key, gain_1, gain_2, table, router_t = pl.pallas_call(
            functools.partial(fold_last_kernel, head_count),
            out_shape=tuple(shape_of(v, F32) for v in last_shapes),
            in_specs=[smem] + [pl.BlockSpec(v.shape, lambda: (0, 0)) for v in last_ins],
            out_specs=tuple(pl.BlockSpec(v, lambda: (0, 0)) for v in last_shapes),
            compiler_params=params(),
            name="fold_last",
        )(device.reshape(1), *last_ins)
    else:
        gain_1, gain_2 = summed[experts], summed[experts + 1]
        table = summed[experts + 2, : head_count * bucket_count].reshape(head_count, bucket_count)
        router_t = lax.dynamic_slice_in_dim(summed[:experts], device * shard, shard, axis=1)
    return (
        output,
        input_grad,
        gain_1.reshape(model),
        gain_2.reshape(model),
        table.T,
        grad_query,
        grad_key,
        grad_value,
        grad_proj,
        router_t.T,
        grad_in,
        grad_out_w,
    )


def solution(mesh):
    in_specs = (
        P(("dp", "expert"), None),
        P(("dp", "expert"), None),
        P(("dp", "expert"), None),
        P(),
        P(),
        P(),
        P(),
        P(("dp", "expert"), None),
        P(("dp", "expert"), None),
        P(("dp", "expert"), None),
        P(("dp", "expert"), None),
        P(("dp", "expert"), None),
        P("expert", None, None),
        P("expert", None, None),
    )
    out_specs = (
        P(("dp", "expert"), None),
        P(("dp", "expert"), None),
        P(),
        P(),
        P(),
        P(("dp", "expert"), None),
        P(("dp", "expert"), None),
        P(("dp", "expert"), None),
        P(("dp", "expert"), None),
        P(("dp", "expert"), None),
        P("expert", None, "dp"),
        P("expert", "dp", None),
    )
    return jax.shard_map(
        per_device, mesh=mesh, in_specs=in_specs, out_specs=out_specs, check_vma=False
    )
```

```python
import functools

import jax
import jax.numpy as jnp
from jax import lax
from jax.experimental import pallas as pl
from jax.experimental.pallas import tpu as pltpu
from jax.sharding import PartitionSpec as P

PRECISE = lax.Precision.HIGHEST
EPSILON = 1e-06
BF = jnp.bfloat16
F32 = jnp.float32
GROUP = 256
FAR_FIRST = (2, 3, 1)


def mm(a, b):
    return jnp.dot(a, b, preferred_element_type=F32)


def mm_nt(a, b):
    return lax.dot_general(a, b, (((1,), (1,)), ((), ())), preferred_element_type=F32)


def mm_tn(a, b):
    return lax.dot_general(a, b, (((0,), (0,)), ((), ())), preferred_element_type=F32)


def full(shape):
    return pl.BlockSpec(shape, lambda *_: (0,) * len(shape))


def cols(rows, width):
    return pl.BlockSpec((rows, width), lambda g, *_: (0, g))


def shape_of(shape, dtype):
    return jax.ShapeDtypeStruct(shape, dtype)


def params(megabytes=20):
    return pltpu.CompilerParams(vmem_limit_bytes=megabytes * 1024 * 1024)


def cost(flops, nbytes):
    return pl.CostEstimate(flops=1024, bytes_accessed=1024, transcendentals=0)


def after(v, *others):
    return lax.optimization_barrier((v, *others))[0]


def all_after(values, *others):
    return list(lax.optimization_barrier((*values, *others))[: len(values)])


def gelu_parts(v):
    square = v * v
    bent = jnp.tanh(0.7978845608 * v * (1.0 + 0.044715 * square))
    half = 0.5 * (1.0 + bent)
    slope = half + 0.5 * v * (1.0 - bent * bent) * (0.7978845608 * (1.0 + 0.134145 * square))
    return v * half, slope


def gate_of(rows, router, picked):
    logits = mm(rows, router)
    exponent = jnp.exp(logits - jnp.max(logits, axis=-1, keepdims=True))
    router_probs = exponent / jnp.sum(exponent, axis=-1, keepdims=True)
    return router_probs, jnp.sum(router_probs * picked, axis=-1, keepdims=True)


def one_lane(shape, lane):
    return (lax.broadcasted_iota(jnp.int32, shape, 1) == lane).astype(F32)


def pack_kernel(*refs):
    out_ref = refs[-1]
    base = 0
    for ref in refs[:-2]:
        out_ref[:, base : base + ref.shape[1]] = ref[...]
        base += ref.shape[1]
    router = refs[-2][...].astype(F32).T.astype(BF)
    out_ref[:, base:] = jnp.concatenate(
        [router, jnp.zeros((router.shape[0], out_ref.shape[1] - base - router.shape[1]), router.dtype)], axis=1
    )


def route_kernel(
    room,
    nz,
    near,
    where_ref,
    routes_ref,
    dy_ref,
    order_ref,
    x_ref,
    gain_ref,
    next_gain_ref,
    slots_ref,
    slots_t_ref,
    keep_ref,
    send_ref,
    perm_ref,
    normed_ref,
    picked_ref,
    gain_out_ref,
    gain_next_ref,
):
    slots, tokens = slots_ref.shape
    experts = picked_ref.shape[1]
    z, c = where_ref[0], where_ref[1]
    expert = routes_ref[...]
    lanes = lax.broadcasted_iota(jnp.int32, (128, tokens), 0)
    picked = (lanes == expert).astype(F32)
    upper = (
        lax.broadcasted_iota(jnp.int32, (tokens, tokens), 0)
        <= lax.broadcasted_iota(jnp.int32, (tokens, tokens), 1)
    ).astype(BF)
    counts = mm(picked.astype(BF), upper)
    rank = jnp.sum(picked * (counts - 1.0), axis=0, keepdims=True).astype(jnp.int32)
    to_z, to_c = expert >> 1, expert & 1
    ahead = to_z ^ z if near else to_z
    other = jnp.where(to_c == c, 0, 1)
    slot = (other * nz + ahead) * room + rank
    chosen = (lax.broadcasted_iota(jnp.int32, (slots, tokens), 0) == slot).astype(F32)
    slots_ref[...] = chosen.astype(BF)
    slots_t_ref[...] = chosen.T.astype(BF)
    dy_rows = mm(slots_ref[...], dy_ref[...]).astype(BF)
    keep_ref[...] = dy_rows[: slots // 2]
    send_ref[: slots // 2, :] = dy_rows[slots // 2 :]
    picked_ref[...] = picked.T[:, :experts]
    width = perm_ref.shape[0]
    perm = (lax.broadcasted_iota(jnp.int32, (width, width), 0) == order_ref[...]).astype(F32).astype(BF)
    perm_ref[...] = perm
    x = x_ref[...].astype(F32)
    scale = lax.rsqrt(jnp.mean(x * x, axis=-1, keepdims=True) + EPSILON)
    normed = mm((x * scale * gain_ref[...]).astype(BF), perm).astype(BF)
    normed_ref[...] = normed
    send_ref[slots // 2 :, : width // 2] = normed[: tokens // 2, width // 2 :]
    send_ref[slots // 2 :, width // 2 :] = normed[tokens // 2 :, width // 2 :]
    gain_out_ref[...] = gain_ref[...]
    gain_next_ref[...] = next_gain_ref[...]


def bias_kernel(buckets_ref, table_ref, bias_ref, along):
    heads, rows = bias_ref.shape[0], bias_ref.shape[1]
    half, span = rows // 2, buckets_ref.shape[1]
    step = pl.program_id(0)

    @pl.when(step == 0)
    def _():
        every = table_ref.shape[0]
        onehot = (lax.broadcasted_iota(jnp.int32, (every, span), 0) == buckets_ref[...]).astype(F32)
        values = lax.dot_general(
            table_ref[...], onehot, (((0,), (0,)), ((), ())), precision=PRECISE, preferred_element_type=F32
        )
        for h in range(along.shape[0]):
            along[h] = values[h : h + 1]

    for h in range(heads):
        line = jnp.broadcast_to(along[step * heads + h], (half, span))
        turned = pltpu.roll(line, span - rows + 1, 1, stride=1, stride_axis=0)
        bias_ref[h, :half, :] = turned[:, :rows]
        bias_ref[h, half:, :half] = turned[:, span - half :]
        bias_ref[h, half:, half:] = turned[:, :half]


def fill_x_first(pieces, out_ref):
    half = pieces[0].shape[0]
    for number, piece in enumerate(pieces):
        out_ref[number * half : (number + 1) * half, :] = piece[:, : out_ref.shape[1]]


def fill_y_first(pieces, out_ref, starts=(0, 0, 0, 0)):
    half = pieces[0].shape[0]
    part = half // 2
    width = out_ref.shape[1]
    for side in range(2):
        own, other = pieces[2 * side], pieces[2 * side + 1]
        at, at_other = [slice(start, start + width) for start in starts[2 * side : 2 * side + 2]]
        base = side * 2 * half
        out_ref[base : base + part, :] = own[:part, at]
        out_ref[base + part : base + half, :] = other[:part, at_other]
        out_ref[base + half : base + half + part, :] = own[part:, at]
        out_ref[base + half + part : base + 2 * half, :] = other[part:, at_other]


def near_kernel(qv_ref, qv_x_ref, ko_ref, ko_y_ref, qv_near_ref, ko_near_ref, both_ref, qv_kept_ref, ko_kept_ref):
    part, width = qv_ref.shape
    for number, (left, right) in enumerate(((qv_ref, ko_ref), (qv_x_ref, ko_y_ref))):
        at = slice(number * part, (number + 1) * part)
        qv_near_ref[at, :] = left[...]
        ko_near_ref[at, :] = right[...]
        qv_kept_ref[at, :] = left[...]
        ko_kept_ref[at, :] = right[...]
        both_ref[at, :width] = left[...]
        both_ref[at, width:] = right[...]


def attend_kernel(head, *refs):
    normed_ref, bias_ref, perm_ref, x_ref, gain_ref, slots_ref, picked_ref = refs[:7]
    qv_refs, ko_refs = refs[7:11], refs[11:15]
    q_ref, k_ref, v_ref, probs_ref, mixed_ref, mixed_other_ref = refs[15:21]
    middle_ref, router_ref, gate_ref, keep_ref, send_ref = refs[21:26]
    wqv, wk, wo = refs[26:]
    experts = router_ref.shape[1]
    model = x_ref.shape[1]

    fill_x_first(qv_refs, wqv)
    fill_y_first(ko_refs, wk, (0, 0, 2 * model, 0))
    fill_y_first(ko_refs, wo, (model, model, 3 * model, model))
    normed = normed_ref[...]
    mixed = []
    for group in range(model // GROUP):
        at = slice(group * GROUP, (group + 1) * GROUP)
        q = mm(normed, wqv[:, at]).astype(BF)
        k = mm(normed, wk[:, at]).astype(BF)
        v = mm(normed, wqv[:, model + group * GROUP : model + (group + 1) * GROUP]).astype(BF)
        q_ref[:, at] = q
        k_ref[:, at] = k
        v_ref[:, at] = v
        for h in range(GROUP // head):
            part = slice(h * head, (h + 1) * head)
            number = group * (GROUP // head) + h
            scores = mm_nt(q[:, part], k[:, part]) + bias_ref[number]
            exponent = jnp.exp(scores - jnp.max(scores, axis=-1, keepdims=True))
            probs = exponent / jnp.sum(exponent, axis=-1, keepdims=True)
            probs_ref[number] = probs
            mixed.append(mm(probs.astype(BF), v[:, part]))
    perm = perm_ref[...]
    mixed_in_order = mm(jnp.concatenate(mixed, axis=1).astype(BF), perm).astype(BF)
    mixed_ref[...] = mixed_in_order[:, : model // 2]
    mixed_other_ref[...] = mixed_in_order[:, model // 2 :]
    middle = x_ref[...].astype(F32) + mm(mixed_in_order, wo[:, :model])
    middle_ref[...] = middle
    scale = lax.rsqrt(jnp.mean(middle * middle, axis=-1, keepdims=True) + EPSILON)
    ffn_in = (middle * scale * gain_ref[...]).astype(BF)
    router = mm(perm, wo[:, model:]).astype(BF)[:, :experts]
    router_ref[...] = router
    rows = mm(slots_ref[...], ffn_in).astype(BF)
    gate_ref[...] = gate_of(ffn_in, router, picked_ref[...])[1]
    half = rows.shape[0] // 2
    keep_ref[...] = rows[:half]
    send_ref[...] = rows[half:]


def join(refs, out_ref):
    base = 0
    for ref in refs:
        size = ref.shape[0]
        out_ref[base : base + size, :] = ref[...]
        base += size


def part_out(v, refs):
    base = 0
    for ref in refs:
        size = ref.shape[0]
        ref[...] = v[base : base + size]
        base += size


def load_kernel(after_ref, w1_ref, w2_ref, w1_out, w2_out, token_ref, sems):
    copies = []
    for ref, out_ref in ((w1_ref, w1_out), (w2_ref, w2_out)):
        rows = ref.shape[1] // 4
        for part in range(4):
            at = pl.ds(part * rows, rows)
            copies.append(pltpu.make_async_copy(ref.at[0, at], out_ref.at[at], sems.at[len(copies)]))
    for copy in copies:
        copy.start()
    token_ref[...] = jnp.zeros_like(token_ref)
    for copy in copies:
        copy.wait()


def hidden_grad_kernel(first_ref, second_ref, w2_ref, first_out, second_out):
    rows = first_ref.shape[0]
    dy = jnp.concatenate([first_ref[...], second_ref[...]], axis=0)
    width = first_out.shape[1] // 3
    for part in range(3):
        at = slice(part * width, (part + 1) * width)
        both = mm_nt(dy, w2_ref[at, :])
        first_out[:, at] = both[:rows]
        second_out[:, at] = both[rows:]


def expert_kernel(pieces, own_ref, *refs):
    rows_refs, dy = refs[:pieces], refs[pieces]
    router_ref, w1_ref, w2_ref, hidden_grad_ref = refs[pieces + 1 : pieces + 5]
    refs = refs[pieces + 5 :]
    back_refs, result_refs = refs[:pieces], refs[pieces : 2 * pieces]
    router_grad_ref, rows = refs[2 * pieces :]
    own = own_ref[0]
    join(rows_refs, rows)
    picked = one_lane((rows.shape[0], router_ref.shape[1]), own)
    router_probs, gate = gate_of(rows[...], router_ref[...], picked)
    result, back = 0.0, 0.0
    width = w1_ref.shape[1] // 2
    for part in range(2):
        at = slice(part * width, (part + 1) * width)
        hidden, slope = gelu_parts(mm(rows[...], w1_ref[:, at]))
        result += mm(hidden.astype(BF), w2_ref[at, :])
        pre_grad = (hidden_grad_ref[:, at] * gate * slope).astype(BF)
        back += mm_nt(pre_grad, w1_ref[:, at])
    returned = result.astype(BF)
    part_out(returned, result_refs)
    gate_grad = jnp.sum(dy[...].astype(F32) * returned.astype(F32), axis=-1, keepdims=True)
    logit_grad = (router_probs * (picked - gate) * gate_grad).astype(BF)
    router_grad_ref[...] = mm_tn(logit_grad, rows[...])
    part_out((back + mm_nt(logit_grad, router_ref[...])).astype(BF), back_refs)


def expert_grad_rows(pieces, refs, own_ref, router_ref, rows_all, branch_all):
    join(refs[:pieces], rows_all)
    join(refs[pieces:], branch_all)
    picked = one_lane((rows_all.shape[0], router_ref.shape[1]), own_ref[0])
    gate = gate_of(rows_all[...], router_ref[...], picked)[1]
    branch_all[...] = (branch_all[...].astype(F32) * gate).astype(BF)


def expert_grad_part(rows, branch, w1, w2):
    hidden, slope = gelu_parts(mm(rows, w1))
    pre_grad = (mm_nt(branch, w2) * slope).astype(BF)
    return mm_tn(rows, pre_grad), mm_tn(hidden.astype(BF), branch)


def first_expert_grad_kernel(pieces, own_ref, place_ref, *refs):
    router_ref, w1_ref, w2_ref, g1_ref, g2_ref, rows_all, branch_all = refs[2 * pieces :]
    expert_grad_rows(pieces, refs[: 2 * pieces], own_ref, router_ref, rows_all, branch_all)
    width = g1_ref.shape[1]
    for part in range(width // GROUP):
        at = pl.ds(pl.multiple_of(place_ref[0] * width + part * GROUP, GROUP), GROUP)
        here = slice(part * GROUP, (part + 1) * GROUP)
        g1, g2 = expert_grad_part(rows_all[...], branch_all[...], w1_ref[:, at], w2_ref[at, :])
        g1_ref[:, here] = g1
        g2_ref[here, :] = g2


def next_expert_grad_kernel(pieces, own_ref, place_ref, *refs):
    router_ref, w1_ref, w2_ref, before1_ref, before2_ref, g1_ref, g2_ref, rows_all, branch_all = refs[2 * pieces :]
    step = pl.program_id(0)

    @pl.when(step == 0)
    def _():
        expert_grad_rows(pieces, refs[: 2 * pieces], own_ref, router_ref, rows_all, branch_all)

    width = before1_ref.shape[1]
    at = pl.ds(pl.multiple_of(place_ref[0] * width + step * GROUP, GROUP), GROUP)
    here = pl.ds(pl.multiple_of(step * GROUP, GROUP), GROUP)
    g1, g2 = expert_grad_part(rows_all[...], branch_all[...], w1_ref[:, at], w2_ref[at, :])
    g1_ref[0] = g1 + before1_ref[:, here]
    g2_ref[0] = g2 + before2_ref[here, :]


def expert_grad_kernel(pieces, more, place_ref, *refs):
    del place_ref
    rows_refs, dy_refs, refs = refs[:pieces], refs[pieces : 2 * pieces], refs[2 * pieces :]
    own_ref, router_ref, w1_ref, w2_ref = refs[:4]
    g1_ref, g2_ref, rows_all, branch_all = refs[-4:]

    @pl.when(pl.program_id(0) == 0)
    def _():
        join(rows_refs, rows_all)
        join(dy_refs, branch_all)
        picked = one_lane((rows_all.shape[0], router_ref.shape[1]), own_ref[0])
        gate = gate_of(rows_all[...], router_ref[...], picked)[1]
        branch_all[...] = (branch_all[...].astype(F32) * gate).astype(BF)

    rows, branch = rows_all[...], branch_all[...]
    hidden, slope = gelu_parts(mm(rows, w1_ref[0]))
    pre_grad = (mm_nt(branch, w2_ref[0]) * slope).astype(BF)
    g1, g2 = mm_tn(rows, pre_grad), mm_tn(hidden.astype(BF), branch)
    if more:
        g1, g2 = g1 + refs[4][0], g2 + refs[5][0]
    g1_ref[0] = g1
    g2_ref[0] = g2


def middle_kernel(head, pieces, *refs):
    keep_refs, refs = refs[:pieces], refs[pieces:]
    (send_ref, slots_t_ref, dy_ref, middle_ref, gain_ref, perm_ref, probs_ref, other_ref) = refs[:8]
    ko_refs = refs[8:12]
    (middle_grad_ref, gain_grad_ref, mixed_grad_ref, grads_ref, wo, mixed_grad) = refs[12:]
    rows, model = dy_ref.shape
    step = pl.program_id(0)
    keep_rows = send_ref.shape[0] // pieces

    @pl.when(step == 0)
    def _():
        fill_y_first(ko_refs, wo, (model, model, 3 * model, model))
        back = jnp.concatenate([ref[:keep_rows, :] for ref in keep_refs] + [send_ref[...]], axis=0)
        ffn_grad = mm(slots_t_ref[...], back)
        middle = middle_ref[...]
        scale = lax.rsqrt(jnp.mean(middle * middle, axis=-1, keepdims=True) + EPSILON)
        gain_grad_ref[...] = jnp.sum(ffn_grad * middle * scale, axis=0, keepdims=True)
        scaled = ffn_grad * gain_ref[...]
        along = jnp.mean(scaled * middle, axis=-1, keepdims=True)
        middle_grad = dy_ref[...].astype(F32) + scale * scaled - middle * (scale * scale * scale * along)
        middle_grad_ref[...] = middle_grad
        attn_grad = middle_grad.astype(BF)
        grads_ref[rows : 2 * rows, :] = attn_grad
        grads_ref[2 * rows :, : model // 2] = other_ref[: rows // 2, :]
        grads_ref[2 * rows :, model // 2 :] = other_ref[rows // 2 :, :]
        in_order = mm_nt(attn_grad, wo[...]).astype(BF)
        every = mm_nt(in_order, perm_ref[...]).astype(BF)
        mixed_grad_ref[...] = every
        for g in range(mixed_grad.shape[0]):
            mixed_grad[g] = every[:, g * GROUP : (g + 1) * GROUP]

    grads = mixed_grad[step]
    parts = [
        mm_tn(probs_ref[h].astype(BF), grads[:, h * head : (h + 1) * head]) for h in range(GROUP // head)
    ]
    value_grad = jnp.concatenate(parts, axis=1).astype(BF)
    at = pl.ds(pl.multiple_of(step * GROUP, GROUP), GROUP)
    grads_ref[:rows, at] = value_grad


def weight_grad_kernel(normed_ref, side_ref, mixed_ref, vo_ref, vo_side_ref, qk_ref, qk_side_ref, *outs):
    a_ref, a_low_ref, b_ref, b_low_ref = outs
    rows = normed_ref.shape[0]
    width = side_ref.shape[1] // 2
    model = normed_ref.shape[1]
    half, part = width // 2, width // 4

    def unpack(v):
        return [v[:, :width], v[:, width:]]

    normed = jnp.concatenate([normed_ref[:, :width], *unpack(side_ref[...])], axis=0)
    mixed = jnp.concatenate([mixed_ref[...], *unpack(vo_side_ref[2 * rows :, :])], axis=0)
    for number, (left, own, side) in enumerate(
        ((normed, vo_ref, vo_side_ref), (normed, qk_ref, qk_side_ref), (mixed, vo_ref, vo_side_ref), (normed, qk_ref, qk_side_ref))
    ):
        here = slice(0, rows) if number < 2 else slice(rows, 2 * rows)
        total = mm_tn(left, jnp.concatenate([own[here, :], side[here, :]], axis=0))
        at = slice(number % 2 * model, (number % 2 + 1) * model)
        if number < 2:
            a_ref[:, at] = total[:half]
            a_low_ref[:, at] = total[half:].astype(BF)
        else:
            b_ref[:part, at] = total[:part]
            b_ref[part:, at] = total[half : half + part]
            b_low_ref[:part, at] = total[part:half].astype(BF)
            b_low_ref[part:, at] = total[half + part :].astype(BF)


def fold_near_kernel(a_ref, a_got_ref, b_ref, b_got_ref, small_ref, small_got_ref, a2_ref, a2_low_ref, b2_ref, b2_low_ref):
    a = a_ref[...] + a_got_ref[...].astype(F32)
    b = b_ref[...] + b_got_ref[...].astype(F32)
    small = small_ref[...] + small_got_ref[...]
    half = a.shape[0] // 2
    a2_ref[...] = a[:half]
    a2_low_ref[:half, :] = a[half:].astype(BF)
    a2_low_ref[half:, :] = jnp.concatenate([small, jnp.zeros_like(small)], axis=1).astype(BF)
    b2_ref[...] = b[:half]
    b2_low_ref[...] = b[half:].astype(BF)


def fold_sums(a_ref, a_low_ref, a_got_ref, b_ref, b_got_ref):
    rows = a_ref.shape[0]
    a = a_ref[...] + a_got_ref[:rows, :].astype(F32)
    b = b_ref[...] + b_got_ref[...].astype(F32)
    model = a.shape[1] // 2
    return a, b, a_low_ref[rows:, :model].astype(F32) + a_got_ref[rows:, :model].astype(F32)


def fold_far_kernel(a_ref, a_low_ref, a_got_ref, b_ref, b_got_ref, keep_ref, *low_refs):
    a, b, small = fold_sums(a_ref, a_low_ref, a_got_ref, b_ref, b_got_ref)
    model = a.shape[1] // 2
    shard = a.shape[0] // 4
    for k in range(4):
        rows = slice(k * shard, (k + 1) * shard)
        blocks = [v[rows, half * model : (half + 1) * model] for v in (a, b) for half in range(2)]
        if k:
            low_refs[k - 1][...] = jnp.concatenate([small, *blocks], axis=0).astype(BF)
        else:
            keep_ref[...] = jnp.concatenate(blocks, axis=0)


def fold_last_kernel(heads, device_ref, keep_ref, own_ref, *refs):
    got, outs = [ref[...].astype(F32) for ref in refs[:3]], refs[3:]
    shard = outs[0].shape[0]
    experts = outs[7].shape[0]
    first = got[0].shape[0] - 4 * shard
    total = keep_ref[...] + ((got[0][first:] + got[1][first:]) + got[2][first:])
    for number in range(4):
        outs[number][...] = total[number * shard : (number + 1) * shard]
    small = (own_ref[...][:first].astype(F32) + got[0][:first]) + (got[1][:first] + got[2][:first])
    outs[4][...] = small[experts]
    outs[5][...] = small[experts + 1]
    every = outs[6].shape[1]
    line = small[experts + 2 : experts + 3]
    outs[6][...] = jnp.concatenate([line[:, h * every : (h + 1) * every] for h in range(heads)], axis=0)
    spots = (small.shape[1], shard)
    mine = lax.broadcasted_iota(jnp.int32, spots, 0) == lax.broadcasted_iota(jnp.int32, spots, 1) + device_ref[0] * shard
    outs[7][...] = lax.dot_general(
        small[:experts], mine.astype(F32), (((1,), (0,)), ((), ())), precision=PRECISE, preferred_element_type=F32
    )


def score_grad_kernel(head, mixed_grad_ref, v_ref, q_ref, k_ref, probs_ref, grads_ref, along_ref):
    rows = q_ref.shape[0]
    flip = (
        lax.broadcasted_iota(jnp.int32, (rows, rows), 0) + lax.broadcasted_iota(jnp.int32, (rows, rows), 1)
        == rows - 1
    ).astype(F32).astype(BF)
    q_parts, k_parts = [], []
    for h in range(GROUP // head):
        part = slice(h * head, (h + 1) * head)
        probs = probs_ref[h]
        prob_grad = mm_nt(mixed_grad_ref[:, part], v_ref[:, part])
        inner = jnp.sum(probs * prob_grad, axis=-1, keepdims=True)
        score_grad = (probs * (prob_grad - inner)).astype(BF)
        q_parts.append(mm(score_grad, k_ref[:, part]))
        k_parts.append(mm_tn(score_grad, q_ref[:, part]))
        flipped = mm(flip, score_grad)
        half = rows // 2
        upper, lower = flipped[:half], flipped[half:]
        wide = jnp.concatenate(
            [upper[:, :half], upper[:, half:] + lower[:, :half], lower[:, half:], jnp.zeros_like(upper[:, :half])], axis=1
        )
        along_ref[h] = jnp.sum(pltpu.roll(wide, 0, 1, stride=1, stride_axis=0), axis=0, keepdims=True)
    grads_ref[:rows, :] = jnp.concatenate(q_parts, axis=1).astype(BF)
    grads_ref[rows:, :] = jnp.concatenate(k_parts, axis=1).astype(BF)


def input_kernel(table_rows, *refs):
    qk_ref, vo_ref, x_ref, gain_ref, perm_ref, middle_grad_ref = refs[:6]
    along_ref, buckets_ref, gain_next_ref, router_a_ref, router_b_ref = refs[6:11]
    qv_refs, wk_refs = refs[11:15], refs[15:19]
    input_grad_ref, small_ref, weight, wide = refs[19:]
    rows = x_ref.shape[0]
    experts, heads = router_a_ref.shape[0], along_ref.shape[0]
    every = table_rows
    onehot = (
        lax.broadcasted_iota(jnp.int32, (every, buckets_ref.shape[1]), 0) == buckets_ref[...]
    ).astype(F32)
    model = x_ref.shape[1]
    small_ref[...] = jnp.zeros_like(small_ref)
    small_ref[:experts, :] = router_a_ref[...] + router_b_ref[...]
    small_ref[experts + 1 : experts + 2, :] = gain_next_ref[...]
    along = jnp.concatenate([along_ref[h] for h in range(heads)], axis=0)
    table = lax.dot_general(
        along, onehot, (((1,), (1,)), ((), ())), precision=PRECISE, preferred_element_type=F32
    )
    small_ref[experts + 2 : experts + 3, : heads * every] = jnp.concatenate(
        [table[h : h + 1] for h in range(heads)], axis=1
    )
    fill_x_first(qv_refs, wide)
    total = mm_nt(jnp.concatenate([qk_ref[:rows, :], vo_ref[:rows, :]], axis=1), wide[...])
    fill_y_first(wk_refs, weight)
    total += mm_nt(qk_ref[rows:, :], weight[...])
    perm = perm_ref[...]
    high = total.astype(BF)
    low = (total - high.astype(F32)).astype(BF)
    normed_grad = mm_nt(high, perm) + mm_nt(low, perm)
    x = x_ref[...].astype(F32)
    scale = lax.rsqrt(jnp.mean(x * x, axis=-1, keepdims=True) + EPSILON)
    small_ref[experts : experts + 1, :] = jnp.sum(normed_grad * x * scale, axis=0, keepdims=True)
    scaled = normed_grad * gain_ref[...]
    along = jnp.mean(scaled * x, axis=-1, keepdims=True)
    input_grad_ref[...] = middle_grad_ref[...] + scale * scaled - x * (scale * scale * scale * along)


class Places:
    def __init__(self):
        self.experts = lax.axis_size("expert")
        self.nz = self.experts // 2
        self.dp = lax.axis_size("dp")
        self.near = self.nz == 4
        me = lax.axis_index("expert")
        self.z, self.c = me // 2, me % 2
        self.row = lax.axis_index("dp")
        self.columns = [[2 * z + c for z in range(self.nz)] for c in range(2)]

    def core(self, v):
        return lax.ppermute(v, "expert", [(i, i ^ 1) for i in range(self.experts)])

    def x(self, v):
        return lax.ppermute(v, "dp", [(i, i ^ 1) for i in range(self.dp)])

    def y(self, v):
        return lax.ppermute(v, "dp", [(i, i ^ 2) for i in range(self.dp)])

    def far(self, v, k):
        return lax.ppermute(v, "expert", [(i, i ^ (2 * k)) for i in range(self.experts)])

    def apart(self, v):
        return lax.all_to_all(
            v, "expert", split_axis=0, concat_axis=0, tiled=True, axis_index_groups=self.columns
        )

    def gather_z(self, v):
        if self.near:
            got = {k: self.far(v, k) for k in FAR_FIRST}
            return jnp.concatenate([v, got[1], got[2], got[3]], axis=0)
        return lax.all_gather(v, "expert", axis=0, tiled=True, axis_index_groups=self.columns)

    def z_order(self):
        steps = jnp.arange(self.nz, dtype=jnp.int32)
        return self.z ^ steps if self.near else steps

    def scatter_z(self, v):
        size = v.shape[0] // self.nz
        if self.near:
            total = v[:size]
            low = v.astype(BF)
            for k in FAR_FIRST:
                total = total + self.far(low[k * size : (k + 1) * size], k).astype(F32)
            return total
        got = self.apart(v.astype(BF).reshape(self.nz, size, v.shape[1]))
        mine = lax.dynamic_slice_in_dim(v, self.z * size, size, axis=0)
        steps = jnp.arange(self.nz, dtype=jnp.int32)[:, None, None]
        return mine + jnp.sum(jnp.where(steps == self.z, 0.0, got.astype(F32)), axis=0)

    def swap(self, blocks):
        got = {k: self.far(blocks[k], k) for k in FAR_FIRST}
        return [blocks[0], got[1], got[2], got[3]]

    def swap_relay(self, blocks, hold):
        size = blocks[0].shape[0]
        first = self.far(jnp.concatenate([blocks[2], blocks[3]], axis=0), 2)
        onward = after(jnp.concatenate([blocks[1], first[size:]], axis=0), *hold)
        second = self.far(onward, 1)
        return [blocks[0], second[:size], first[:size], second[size:]], onward

    def by_z(self, keep, got):
        room = keep.shape[0] // self.nz
        both = jnp.concatenate([v.reshape(self.nz, room, keep.shape[1]) for v in (keep, got)], axis=1)
        return [both[k] for k in range(4)] if self.near else both

    def halves(self, moved):
        moved = moved.reshape(-1, moved.shape[-1])
        half = moved.shape[0] // 2
        return [moved[:half]], [moved[half:]]

    def to_owners(self, keep, got, hold):
        blocks = self.by_z(keep, got)
        if self.near:
            blocks = all_after([blocks[k] for k in range(4)], *hold)
            two, one = self.far(blocks[2], 2), self.far(blocks[1], 1)
            three = self.far(after(blocks[3], two), 3)
            return [blocks[0], two], [one, three]
        return self.halves(self.apart(blocks))

    def send_more(self, blocks, k, hold):
        return self.far(after(blocks[k], *hold), k) if self.near else blocks

    def from_owners(self, first, second):
        width = first[0].shape[1]
        both = self.apart(jnp.concatenate([*first, *second], axis=0).reshape(self.nz, -1, width))
        room = both.shape[1] // 2
        return [both[:, :room].reshape(-1, width)], both[:, room:].reshape(-1, width)

    def to_senders(self, first, second):
        if self.near:
            two = self.far(first[1], 2)
            one, three = all_after(second, two)
            three, one = self.far(three, 3), self.far(one, 1)
            moved = [first[0], one, two, three]
            room = one.shape[0] // 2
            return moved, self.core(jnp.concatenate([v[room:] for v in moved], axis=0))
        keep, other = self.from_owners(first, second)
        return keep, self.core(other)

    def gather_far(self, a, b):
        return self.y(a), self.x(b)


def per_device(
    tokens,
    cotangent,
    routes,
    buckets,
    norm_attn,
    norm_ffn,
    rel_table,
    query_weight,
    key_weight,
    value_weight,
    out_weight,
    router_weight,
    expert_in,
    expert_out,
):
    at = Places()
    rows, model = tokens.shape
    head_count = rel_table.shape[1]
    head = model // head_count
    bucket_count = rel_table.shape[0]
    experts = router_weight.shape[1]
    shard = query_weight.shape[0]
    nz = at.nz
    room = max(2, 2 * rows // at.experts)
    slots = experts * room
    half = slots // 2
    groups = model // GROUP
    per_group = GROUP // head
    hidden = expert_in.shape[2]

    def in_hbm(*values):
        return [pltpu.with_memory_space_constraint(v, pltpu.HBM) for v in values]

    expert_in, expert_out = in_hbm(expert_in, expert_out)
    own = lax.axis_index("expert").astype(jnp.int32).reshape(1)
    smem = pl.BlockSpec(memory_space=pltpu.SMEM)

    core_of = at.c ^ jnp.arange(2, dtype=jnp.int32)
    row_of = at.row ^ jnp.arange(4, dtype=jnp.int32)
    device_of = (
        row_of[None, :, None] * at.experts + at.z_order()[None, None, :] * 2 + core_of[:, None, None]
    )
    order = (
        device_of[..., None] * shard + jnp.arange(shard, dtype=jnp.int32)
    ).reshape(1, model).astype(jnp.int32)

    shards = (query_weight, value_weight, key_weight, out_weight, router_weight.T)
    packed = pl.pallas_call(
        pack_kernel,
        out_shape=shape_of((shard, 4 * model + 128), BF),
        in_specs=[pl.BlockSpec(memory_space=pltpu.VMEM)] * 5,
        out_specs=pl.BlockSpec(memory_space=pltpu.VMEM),
        name="pack",
    )(*shards)
    line = at.gather_z(packed)
    span = 2 * rows
    bucket_line = jnp.pad(buckets, (0, 1), constant_values=-1).reshape(1, span)
    slots_map, slots_t, dy_keep, dy_send, perm, normed, picked, gain_attn, gain_ffn = pl.pallas_call(
        functools.partial(route_kernel, room, nz, at.near),
        out_shape=(
            shape_of((slots, rows), BF),
            shape_of((rows, slots), BF),
            shape_of((half, model), BF),
            shape_of((half + rows // 2, model), BF),
            shape_of((model, model), BF),
            shape_of((rows, model), BF),
            shape_of((rows, experts), F32),
            shape_of((1, model), F32),
            shape_of((1, model), F32),
        ),
        in_specs=[smem] + [pl.BlockSpec(memory_space=pltpu.VMEM)] * 6,
        compiler_params=params(),
        cost_estimate=cost(2 * rows * slots * model, 4 * rows * model),
        name="route",
    )(
        jnp.stack([at.z, at.c]).astype(jnp.int32),
        routes.reshape(1, rows),
        cotangent,
        order,
        tokens,
        norm_attn.reshape(1, model),
        norm_ffn.reshape(1, model),
    )
    dy_got = at.core(dy_send)
    normed_side = dy_got[half:]
    dy_got = dy_got[:half]
    qv, ko = line[:, : 2 * model], line[:, 2 * model :]
    qv, ko = all_after([qv, ko], slots_t)
    dy_keep, dy_got = all_after([dy_keep, dy_got], qv, ko)
    part_rows = qv.shape[0]
    dy_blocks = at.by_z(dy_keep, dy_got)
    dy_one = at.send_more(dy_blocks, 1, (dy_blocks,))
    bias = pl.pallas_call(
        bias_kernel,
        grid=(groups,),
        out_shape=shape_of((head_count, rows, rows), F32),
        in_specs=[full((1, span)), full((bucket_count, head_count))],
        out_specs=pl.BlockSpec((per_group, rows, rows), lambda g: (g, 0, 0)),
        scratch_shapes=[pltpu.VMEM((head_count, 1, span), F32)],
        compiler_params=params(),
        cost_estimate=cost(1 << 20, 4 * head_count * rows * rows),
        name="bias",
    )(after(bucket_line, slots_t), rel_table)
    qv_near, ko_near, both_near, qv_kept, ko_kept = pl.pallas_call(
        near_kernel,
        out_shape=tuple(pltpu.HBM((2 * part_rows, width), BF) for width in (2 * model, 2 * model + 128, 4 * model + 128))
        + tuple(shape_of((2 * part_rows, width), BF) for width in (2 * model, 2 * model + 128)),
        in_specs=[pl.BlockSpec(memory_space=pltpu.VMEM)] * 4,
        out_specs=tuple(pl.BlockSpec((2 * part_rows, width), lambda: (0, 0)) for width in (2 * model, 2 * model + 128, 4 * model + 128))
        + (pl.BlockSpec(memory_space=pltpu.VMEM),) * 2,
        compiler_params=params(),
        name="near",
    )(after(qv, dy_one, bias), at.x(qv), ko, at.y(ko))
    qv_far, ko_far = at.gather_far(qv_near, ko_near)
    w_first, w_second, loaded = pl.pallas_call(
        load_kernel,
        out_shape=(pltpu.VMEM((model, hidden), BF), pltpu.VMEM((hidden, model), BF), shape_of((8, 128), F32)),
        in_specs=[pl.BlockSpec(memory_space=pltpu.VMEM)] + [pl.BlockSpec(memory_space=pl.ANY)] * 2,
        out_specs=(pl.BlockSpec(memory_space=pltpu.VMEM),) * 3,
        scratch_shapes=[pltpu.SemaphoreType.DMA((8,))],
        compiler_params=params(),
        name="load",
    )(bias[0, :8, :128], expert_in, expert_out)
    both_side = at.core(both_near)
    dy_two = at.send_more(dy_blocks, 2, (qv_near, dy_one))
    qv_far, ko_far, dy_two = all_after([qv_far, ko_far, dy_two], both_side)
    dy_three = at.send_more(dy_blocks, 3, (qv_far, ko_far, dy_two))
    qv_pieces = (qv_kept, qv_far, both_side, at.core(qv_far))
    ko_pieces = (ko_kept, ko_far, both_side, at.core(ko_far))
    if at.near:
        dy_a = jnp.concatenate([dy_blocks[0], dy_two], axis=0)
    else:
        (dy_a,), (dy_b,) = at.halves(at.apart(dy_blocks))
    dy_a_later = after(dy_a, qv_far, ko_far)
    dy_ax, dy_ay = at.x(dy_a_later), at.y(dy_a_later)

    quarter = qv_near.shape[0]
    wide = ko_near.shape[1]
    side_wide = both_side.shape[1]
    head_block = pl.BlockSpec((per_group, rows, rows), lambda g: (g, 0, 0))
    in_vmem = pl.BlockSpec(memory_space=pltpu.VMEM)
    ko_full = [full((quarter, wide)), full((quarter, wide)), full((quarter, side_wide)), full((quarter, wide))]
    attend_shapes = [((rows, model), BF)] * 3 + [
        ((head_count, rows, rows), F32),
        ((rows, model // 2), BF),
        ((rows, model // 2), BF),
        ((rows, model), F32),
        ((model, experts), BF),
        ((rows, 1), F32),
        ((half, model), BF),
        ((half, model), BF),
    ]
    q, k, v, probs, mixed, mixed_other, middle, router, gate, keep, send = pl.pallas_call(
        functools.partial(attend_kernel, head),
        out_shape=tuple(pltpu.HBM(*v) if v[0] == (rows, 1) else shape_of(*v) for v in attend_shapes),
        in_specs=[in_vmem] * 3
        + [pl.BlockSpec((rows, model), lambda: (0, 0)), in_vmem]
        + [pl.BlockSpec((slots, rows), lambda: (0, 0)), pl.BlockSpec((rows, experts), lambda: (0, 0))]
        + [in_vmem] * 8,
        out_specs=(in_vmem,) * 8 + (pl.BlockSpec((rows, 1), lambda: (0, 0)),) + (in_vmem,) * 2,
        scratch_shapes=[
            pltpu.VMEM((model, 2 * model), BF),
            pltpu.VMEM((model, model), BF),
            pltpu.VMEM((model, wide - model), BF),
        ],
        compiler_params=params(),
        name="attend",
    )(
        normed,
        bias,
        perm,
        *in_hbm(tokens),
        after(gain_ffn, loaded),
        *in_hbm(slots_map, picked),
        *qv_pieces,
        *ko_pieces,
    )

    got = at.core(after(send, dy_three))
    first, second = at.to_owners(keep, got, (dy_ax, dy_ay))
    if at.near:
        dy_b = jnp.concatenate([dy_one, dy_three], axis=0)
    dy_b_later = after(dy_b, got, dy_ax, dy_ay)
    dy_by, dy_bx = at.y(dy_b_later), at.x(dy_b_later)
    hidden_grads = pl.pallas_call(
        hidden_grad_kernel,
        out_shape=(shape_of((half, hidden), F32),) * 2,
        in_specs=[in_vmem] * 3,
        out_specs=(in_vmem,) * 2,
        compiler_params=params(),
        name="hidden_grads",
    )(dy_a, dy_b, w_second)

    def expert(rows_list, dy_rows, hidden_grad, router_in):
        sizes = [v.shape[0] for v in rows_list]
        count = sum(sizes)
        shapes = [((n, model), BF) for n in sizes * 2] + [((experts, model), F32), ((count, model), BF)]
        outs = pl.pallas_call(
            functools.partial(expert_kernel, len(sizes)),
            out_shape=tuple(shape_of(*v) for v in shapes),
            in_specs=[smem] + [in_vmem] * (len(sizes) + 5),
            out_specs=(in_vmem,) * len(shapes),
            compiler_params=params(),
            name="expert",
        )(own, *rows_list, dy_rows, router_in, w_first, w_second, hidden_grad)
        n = len(sizes)
        return list(outs[:n]), list(outs[n : 2 * n]), outs[2 * n], outs[2 * n + 1]

    dy_ax_later, dy_by_later = all_after([dy_ax, dy_by], first[-1], dy_bx, hidden_grads[1])
    dy_axy, dy_byx = at.y(dy_ax_later), at.x(dy_by_later)
    back_a, returned_a, router_grad_a, rows_a = expert(first, dy_a, hidden_grads[0], after(router, dy_by, dy_bx))
    rows_ax, rows_ay = at.x(rows_a), at.y(rows_a)
    back_b, returned_b, router_grad_b, rows_b = expert(
        second, dy_b, hidden_grads[1], after(router, router_grad_a, dy_axy, dy_byx)
    )
    rows_b_later = after(rows_b, rows_ax, rows_ay)
    rows_by, rows_bx = at.y(rows_b_later), at.x(rows_b_later)
    back_keep, back_send = at.to_senders(back_a, back_b)

    slice_width = hidden // at.dp
    place = at.row.astype(jnp.int32).reshape(1)

    steps = slice_width // GROUP

    def expert_grads(rows_list, dy_list, router_in, before):
        sizes = [v.shape[0] for v in rows_list]
        count = sum(sizes)
        outs = (
            pl.BlockSpec((1, model, GROUP), lambda g, place: (0, 0, g)),
            pl.BlockSpec((1, GROUP, model), lambda g, place: (0, g, 0)),
        )
        return pl.pallas_call(
            functools.partial(expert_grad_kernel, len(sizes), bool(before)),
            grid_spec=pltpu.PrefetchScalarGridSpec(
                num_scalar_prefetch=1,
                grid=(steps,),
                in_specs=[full((n, model)) for n in sizes * 2]
                + [
                    smem,
                    full((model, experts)),
                    pl.BlockSpec((1, model, GROUP), lambda g, place: (0, 0, place[0] * steps + g)),
                    pl.BlockSpec((1, GROUP, model), lambda g, place: (0, place[0] * steps + g, 0)),
                ]
                + list(outs if before else ()),
                out_specs=outs,
                scratch_shapes=[pltpu.VMEM((count, model), BF), pltpu.VMEM((count, model), BF)],
            ),
            out_shape=(pltpu.HBM((1, model, slice_width), F32), pltpu.HBM((1, slice_width, model), F32)),
            compiler_params=params(),
            cost_estimate=cost(8 * count * model * slice_width, 20 * model * slice_width),
            name="expert_grads",
        )(place, *in_hbm(*rows_list, *dy_list), own, router_in, expert_in, expert_out, *in_hbm(*before))

    whole_vmem = pl.BlockSpec(memory_space=pltpu.VMEM)

    def first_expert_grads(rows_list, dy_list, router_in):
        count = sum(v.shape[0] for v in rows_list)
        ins = [*rows_list, *dy_list, router_in, w_first, w_second]
        return pl.pallas_call(
            functools.partial(first_expert_grad_kernel, len(rows_list)),
            out_shape=(shape_of((model, slice_width), F32), shape_of((slice_width, model), F32)),
            in_specs=[smem] * 2 + [whole_vmem] * len(ins),
            out_specs=(whole_vmem,) * 2,
            scratch_shapes=[pltpu.VMEM((count, model), BF)] * 2,
            compiler_params=params(24),
            name="expert_grads",
        )(own, place, *ins)

    def next_expert_grads(rows_list, dy_list, router_in, before):
        count = sum(v.shape[0] for v in rows_list)
        pieces = [*rows_list, *dy_list]
        return pl.pallas_call(
            functools.partial(next_expert_grad_kernel, len(rows_list)),
            grid=(slice_width // GROUP,),
            out_shape=(pltpu.HBM((1, model, slice_width), F32), pltpu.HBM((1, slice_width, model), F32)),
            in_specs=[smem] * 2 + [full(v.shape) for v in pieces] + [whole_vmem] * 5,
            out_specs=(
                pl.BlockSpec((1, model, GROUP), lambda g: (0, 0, g)),
                pl.BlockSpec((1, GROUP, model), lambda g: (0, g, 0)),
            ),
            scratch_shapes=[pltpu.VMEM((count, model), BF)] * 2,
            compiler_params=params(24),
            name="expert_grads",
        )(own, place, *in_hbm(*pieces), router_in, w_first, w_second, *before)

    rows_axy, rows_byx = at.y(after(rows_ax, rows_by, rows_bx, back_send)), at.x(after(rows_by, rows_bx, back_send))

    middle_grad, gain_ffn_grad, mixed_grad, vo_grads = pl.pallas_call(
        functools.partial(middle_kernel, head, len(back_keep)),
        grid=(groups,),
        out_shape=(
            shape_of((rows, model), F32),
            shape_of((1, model), F32),
            shape_of((rows, model), BF),
            shape_of((2 * rows + rows // 2, model), BF),
        ),
        in_specs=[full(v.shape) for v in back_keep]
        + [
            full((half, model)),
            full((rows, slots)),
            full((rows, model)),
            full((rows, model)),
            full((1, model)),
            full((model, model)),
            head_block,
            full((rows, model // 2)),
        ]
        + ko_full,
        out_specs=(
            full((rows, model)),
            full((1, model)),
            full((rows, model)),
            full((2 * rows + rows // 2, model)),
        ),
        scratch_shapes=[pltpu.VMEM((model, model), BF), pltpu.VMEM((groups, rows, GROUP), BF)],
        compiler_params=params(),
        cost_estimate=cost(10 * rows * model * model, 12 * model * model),
        name="middle",
    )(*back_keep, back_send, slots_t, cotangent, middle, after(gain_ffn, rows_by, rows_bx), perm, probs, mixed_other, *ko_pieces)
    vo_side = at.core(vo_grads)
    qk_grads, along_grad = pl.pallas_call(
        functools.partial(score_grad_kernel, head),
        grid=(groups,),
        out_shape=(shape_of((2 * rows, model), BF), shape_of((head_count, 1, span), F32)),
        in_specs=[cols(rows, GROUP)] * 4 + [head_block],
        out_specs=(cols(2 * rows, GROUP), pl.BlockSpec((per_group, 1, span), lambda g: (g, 0, 0))),
        compiler_params=params(),
        cost_estimate=cost(8 * rows * model * model, 12 * model * model),
        name="score_grads",
    )(mixed_grad, v, q, k, probs)
    qk_side = at.core(after(qk_grads, vo_side, rows_axy, rows_byx))
    small_rows = -(-(experts + 3) // 16) * 16
    input_grad, small = pl.pallas_call(
        functools.partial(input_kernel, bucket_count),
        grid=(1,),
        out_shape=(shape_of((rows, model), F32), shape_of((small_rows, model), F32)),
        in_specs=[full((2 * rows, model)), full((2 * rows + rows // 2, model))]
        + [full((rows, model)), full((1, model)), full((model, model)), full((rows, model))]
        + [full((head_count, 1, span)), full((1, span)), full((1, model))]
        + [full((experts, model))] * 2
        + [full((quarter, 2 * model))] * 4
        + [pl.BlockSpec((quarter, model), lambda g, at=at_k: (0, at)) for at_k in (0, 0, 2, 0)],
        out_specs=(full((rows, model)), full((small_rows, model))),
        scratch_shapes=[pltpu.VMEM((model, model), BF), pltpu.VMEM((model, 2 * model), BF)],
        compiler_params=params(),
        cost_estimate=cost(10 * rows * model * model, 12 * model * model),
        name="inputs",
    )(
        qk_grads,
        vo_grads,
        tokens,
        gain_attn,
        perm,
        middle_grad,
        along_grad,
        bucket_line,
        gain_ffn_grad,
        router_grad_a,
        router_grad_b,
        *qv_pieces,
        *ko_pieces,
    )
    quarter_rows = model // 4

    def vmem_call(kernel, name, shapes, *ins):
        return pl.pallas_call(
            kernel,
            out_shape=tuple(shape_of(*v) for v in shapes),
            in_specs=[pl.BlockSpec(v.shape, lambda: (0, 0)) for v in ins],
            out_specs=tuple(pl.BlockSpec(v[0], lambda: (0, 0)) for v in shapes),
            compiler_params=params(),
            name=name,
        )(*ins)

    pair = 2 * model
    a, a_low, b, b_low = vmem_call(
        weight_grad_kernel,
        "weight_grads",
        [((quarter_rows, pair), F32), ((quarter_rows, pair), BF)] * 2,
        normed,
        normed_side,
        mixed,
        vo_grads,
        vo_side,
        qk_grads,
        qk_side,
    )
    small = small + after(at.core(small), a_low)
    a_got, b_got = at.y(a_low), at.x(b_low)
    small_got = at.y(small)
    if at.near:
        home_two = at.far(after(returned_a[1], a_low, b_low), 2)
    else:
        home_two = at.apart(jnp.concatenate([*returned_a, *returned_b], axis=0).reshape(nz, -1, model))
    near_sums = first_expert_grads(
        [rows_a, rows_b, rows_ax, rows_by], [dy_a, dy_b, dy_ax, dy_by], after(router, a_low, b_low)
    )
    eighth = quarter_rows // 2
    a, a_low, b, b_low = vmem_call(
        fold_near_kernel,
        "fold_near",
        [((eighth, pair), F32), ((eighth + small_rows, pair), BF), ((eighth, pair), F32), ((eighth, pair), BF)],
        a,
        after(a_got, near_sums[0], home_two),
        b,
        b_got,
        small,
        small_got,
    )
    a_got, b_got = at.x(a_low), at.y(b_low)
    mid_sums = next_expert_grads([rows_ay, rows_bx], [dy_ay, dy_bx], after(router, a_low, b_low), near_sums)
    if at.near:
        home = [at.far(v, k) for v, k in zip(all_after([returned_b[1], returned_b[0]], a_low, b_low), (3, 1))]
        home_blocks = [returned_a[0], home[1], home_two, home[0]]
        room = half // nz
        returned_keep = home_blocks
        returned_other = jnp.concatenate([v[room:] for v in home_blocks], axis=0)
    else:
        room = home_two.shape[1] // 2
        returned_keep = [home_two[:, :room].reshape(half, model)]
        returned_other = home_two[:, room:].reshape(half, model)
    if at.near:
        keep_sum, *low = vmem_call(
            fold_far_kernel,
            "fold_far",
            [((4 * shard, model), F32)] + [((small_rows + 4 * shard, model), BF)] * 3,
            a,
            a_low,
            after(a_got, mid_sums[0], *home),
            b,
            b_got,
        )
        hold = keep_sum
        got_z = {k: at.far(low[k - 1], k) for k in FAR_FIRST}
    else:
        a = a + a_got[:eighth].astype(F32)
        b = b + b_got.astype(F32)
        summed = (a_low[eighth:].astype(F32) + a_got[eighth:].astype(F32))[:, :model]
        hold = jnp.concatenate([a, b], axis=1)
        sums = at.scatter_z(hold)
        grad_value, grad_query, grad_proj, grad_key = [sums[:, n * model : (n + 1) * model] for n in range(4)]
        summed = lax.psum(summed, "expert", axis_index_groups=at.columns)
    returned_send = at.core(after(returned_other, hold))
    grad_in, grad_out_w = expert_grads([rows_axy, rows_byx], [dy_axy, dy_byx], after(router, hold), mid_sums)
    keep_rows = half // len(returned_keep)
    expert_result = mm(
        slots_t,
        jnp.concatenate([v[:keep_rows] for v in returned_keep] + [returned_send], axis=0),
    )
    output = (middle + gate * expert_result).astype(BF)
    device = (at.row * at.experts + lax.axis_index("expert")).astype(jnp.int32)
    if at.near:
        last_ins = [after(keep_sum, output, grad_in), low[0], *[got_z[k] for k in (1, 2, 3)]]
        last_shapes = [(shard, model)] * 4 + [(model,)] * 2 + [(head_count, bucket_count), (experts, shard)]
        grad_value, grad_query, grad_proj, grad_key, gain_1, gain_2, table, router_t = pl.pallas_call(
            functools.partial(fold_last_kernel, head_count),
            out_shape=tuple(shape_of(v, F32) for v in last_shapes),
            in_specs=[smem] + [pl.BlockSpec(v.shape, lambda: (0, 0)) for v in last_ins],
            out_specs=tuple(pl.BlockSpec(v, (lambda: (0, 0)) if len(v) > 1 else (lambda: (0,))) for v in last_shapes),
            compiler_params=params(),
            name="fold_last",
        )(device.reshape(1), *last_ins)
    else:
        gain_1, gain_2 = summed[experts], summed[experts + 1]
        table = summed[experts + 2, : head_count * bucket_count].reshape(head_count, bucket_count)
        router_t = lax.dynamic_slice_in_dim(summed[:experts], device * shard, shard, axis=1)
    return (
        output,
        input_grad,
        gain_1.reshape(model),
        gain_2.reshape(model),
        table.T,
        grad_query,
        grad_key,
        grad_value,
        grad_proj,
        router_t.T,
        grad_in,
        grad_out_w,
    )


def solution(mesh):
    in_specs = (
        P(("dp", "expert"), None),
        P(("dp", "expert"), None),
        P(("dp", "expert"), None),
        P(),
        P(),
        P(),
        P(),
        P(("dp", "expert"), None),
        P(("dp", "expert"), None),
        P(("dp", "expert"), None),
        P(("dp", "expert"), None),
        P(("dp", "expert"), None),
        P("expert", None, None),
        P("expert", None, None),
    )
    out_specs = (
        P(("dp", "expert"), None),
        P(("dp", "expert"), None),
        P(),
        P(),
        P(),
        P(("dp", "expert"), None),
        P(("dp", "expert"), None),
        P(("dp", "expert"), None),
        P(("dp", "expert"), None),
        P(("dp", "expert"), None),
        P("expert", None, "dp"),
        P("expert", "dp", None),
    )
    return jax.shard_map(
        per_device, mesh=mesh, in_specs=in_specs, out_specs=out_specs, check_vma=False
    )
```

```python
import functools

import jax
import jax.numpy as jnp
from jax import lax
from jax.experimental import pallas as pl
from jax.experimental.pallas import tpu as pltpu
from jax.sharding import PartitionSpec as P

PRECISE = lax.Precision.HIGHEST
EPSILON = 1e-06
BF = jnp.bfloat16
F32 = jnp.float32
GROUP = 256
FAR_FIRST = (2, 3, 1)


def mm(a, b):
    return jnp.dot(a, b, preferred_element_type=F32)


def mm_nt(a, b):
    return lax.dot_general(a, b, (((1,), (1,)), ((), ())), preferred_element_type=F32)


def mm_tn(a, b):
    return lax.dot_general(a, b, (((0,), (0,)), ((), ())), preferred_element_type=F32)


def full(shape):
    return pl.BlockSpec(shape, lambda *_: (0,) * len(shape))


def cols(rows, width):
    return pl.BlockSpec((rows, width), lambda g, *_: (0, g))


def shape_of(shape, dtype):
    return jax.ShapeDtypeStruct(shape, dtype)


def params(megabytes=20):
    return pltpu.CompilerParams(vmem_limit_bytes=megabytes * 1024 * 1024)


def cost(flops, nbytes):
    return pl.CostEstimate(flops=1024, bytes_accessed=1024, transcendentals=0)


def after(v, *others):
    return lax.optimization_barrier((v, *others))[0]


def all_after(values, *others):
    return list(lax.optimization_barrier((*values, *others))[: len(values)])


def gelu_parts(v):
    c = 0.7978845608
    square = v * v
    half = 0.5 + 0.5 * jnp.tanh(v * (c + (c * 0.044715) * square))
    value = v * half
    return value, half + value * (1.0 - half) * (2.0 * c + (2.0 * c * 0.134145) * square)


def gate_of(rows, router, picked):
    logits = mm(rows, router)
    exponent = jnp.exp(logits - jnp.max(logits, axis=-1, keepdims=True))
    router_probs = exponent / jnp.sum(exponent, axis=-1, keepdims=True)
    return router_probs, jnp.sum(router_probs * picked, axis=-1, keepdims=True)


def one_lane(shape, lane):
    return (lax.broadcasted_iota(jnp.int32, shape, 1) == lane).astype(F32)


def pack_kernel(*refs):
    out_ref = refs[-1]
    base = 0
    for ref in refs[:-2]:
        out_ref[:, base : base + ref.shape[1]] = ref[...]
        base += ref.shape[1]
    router = refs[-2][...].astype(F32).T.astype(BF)
    out_ref[:, base:] = jnp.concatenate(
        [router, jnp.zeros((router.shape[0], out_ref.shape[1] - base - router.shape[1]), router.dtype)], axis=1
    )


def route_kernel(
    room,
    nz,
    near,
    where_ref,
    routes_ref,
    dy_ref,
    order_ref,
    x_ref,
    gain_ref,
    next_gain_ref,
    slots_ref,
    slots_t_ref,
    keep_ref,
    send_ref,
    perm_ref,
    normed_ref,
    picked_ref,
    gain_out_ref,
    gain_next_ref,
):
    slots, tokens = slots_ref.shape
    experts = picked_ref.shape[1]
    z, c = where_ref[0], where_ref[1]
    expert = routes_ref[...]
    lanes = lax.broadcasted_iota(jnp.int32, (128, tokens), 0)
    picked = (lanes == expert).astype(F32)
    upper = (
        lax.broadcasted_iota(jnp.int32, (tokens, tokens), 0)
        <= lax.broadcasted_iota(jnp.int32, (tokens, tokens), 1)
    ).astype(BF)
    counts = mm(picked.astype(BF), upper)
    rank = jnp.sum(picked * (counts - 1.0), axis=0, keepdims=True).astype(jnp.int32)
    to_z, to_c = expert >> 1, expert & 1
    ahead = to_z ^ z if near else to_z
    other = jnp.where(to_c == c, 0, 1)
    slot = (other * nz + ahead) * room + rank
    chosen = (lax.broadcasted_iota(jnp.int32, (slots, tokens), 0) == slot).astype(F32)
    slots_ref[...] = chosen.astype(BF)
    slots_t_ref[...] = chosen.T.astype(BF)
    dy_rows = mm(slots_ref[...], dy_ref[...]).astype(BF)
    keep_ref[...] = dy_rows[: slots // 2]
    send_ref[: slots // 2, :] = dy_rows[slots // 2 :]
    picked_ref[...] = picked.T[:, :experts]
    width = perm_ref.shape[0]
    perm = (lax.broadcasted_iota(jnp.int32, (width, width), 0) == order_ref[...]).astype(F32).astype(BF)
    perm_ref[...] = perm
    x = x_ref[...].astype(F32)
    scale = lax.rsqrt(jnp.mean(x * x, axis=-1, keepdims=True) + EPSILON)
    normed = mm((x * scale * gain_ref[...]).astype(BF), perm).astype(BF)
    normed_ref[...] = normed
    send_ref[slots // 2 :, : width // 2] = normed[: tokens // 2, width // 2 :]
    send_ref[slots // 2 :, width // 2 :] = normed[tokens // 2 :, width // 2 :]
    gain_out_ref[...] = gain_ref[...]
    gain_next_ref[...] = next_gain_ref[...]


def bias_kernel(buckets_ref, table_ref, bias_ref, along):
    heads, rows = bias_ref.shape[0], bias_ref.shape[1]
    half, span = rows // 2, buckets_ref.shape[1]
    step = pl.program_id(0)

    @pl.when(step == 0)
    def _():
        every = table_ref.shape[0]
        onehot = (lax.broadcasted_iota(jnp.int32, (every, span), 0) == buckets_ref[...]).astype(F32)
        values = lax.dot_general(
            table_ref[...], onehot, (((0,), (0,)), ((), ())), precision=PRECISE, preferred_element_type=F32
        )
        for h in range(along.shape[0]):
            along[h] = values[h : h + 1]

    for h in range(heads):
        line = jnp.broadcast_to(along[step * heads + h], (half, span))
        turned = pltpu.roll(line, span - rows + 1, 1, stride=1, stride_axis=0)
        bias_ref[h, :half, :] = turned[:, :rows]
        bias_ref[h, half:, :half] = turned[:, span - half :]
        bias_ref[h, half:, half:] = turned[:, :half]


def fill_x_first(pieces, out_ref):
    half = pieces[0].shape[0]
    for number, piece in enumerate(pieces):
        out_ref[number * half : (number + 1) * half, :] = piece[:, : out_ref.shape[1]]


def fill_y_first(pieces, out_ref, starts=(0, 0, 0, 0)):
    half = pieces[0].shape[0]
    part = half // 2
    width = out_ref.shape[1]
    for side in range(2):
        own, other = pieces[2 * side], pieces[2 * side + 1]
        at, at_other = [slice(start, start + width) for start in starts[2 * side : 2 * side + 2]]
        base = side * 2 * half
        out_ref[base : base + part, :] = own[:part, at]
        out_ref[base + part : base + half, :] = other[:part, at_other]
        out_ref[base + half : base + half + part, :] = own[part:, at]
        out_ref[base + half + part : base + 2 * half, :] = other[part:, at_other]


def near_kernel(qv_ref, qv_x_ref, ko_ref, ko_y_ref, qv_near_ref, ko_near_ref, both_ref, qv_kept_ref, ko_kept_ref):
    part, width = qv_ref.shape
    for number, (left, right) in enumerate(((qv_ref, ko_ref), (qv_x_ref, ko_y_ref))):
        at = slice(number * part, (number + 1) * part)
        qv_near_ref[at, :] = left[...]
        ko_near_ref[at, :] = right[...]
        qv_kept_ref[at, :] = left[...]
        ko_kept_ref[at, :] = right[...]
        both_ref[at, :width] = left[...]
        both_ref[at, width:] = right[...]


def attend_kernel(head, *refs):
    normed_ref, bias_ref, perm_ref, x_ref, gain_ref, slots_ref, picked_ref = refs[:7]
    qv_refs, ko_refs = refs[7:11], refs[11:15]
    q_ref, k_ref, v_ref, probs_ref, mixed_ref, mixed_other_ref = refs[15:21]
    middle_ref, router_ref, gate_ref, keep_ref, send_ref = refs[21:26]
    wqv, wk, wo = refs[26:]
    experts = router_ref.shape[1]
    model = x_ref.shape[1]

    fill_x_first(qv_refs, wqv)
    fill_y_first(ko_refs, wk, (0, 0, 2 * model, 0))
    fill_y_first(ko_refs, wo, (model, model, 3 * model, model))
    normed = normed_ref[...]
    mixed = []
    for group in range(model // GROUP):
        at = slice(group * GROUP, (group + 1) * GROUP)
        q = mm(normed, wqv[:, at]).astype(BF)
        k = mm(normed, wk[:, at]).astype(BF)
        v = mm(normed, wqv[:, model + group * GROUP : model + (group + 1) * GROUP]).astype(BF)
        q_ref[:, at] = q
        k_ref[:, at] = k
        v_ref[:, at] = v
        for h in range(GROUP // head):
            part = slice(h * head, (h + 1) * head)
            number = group * (GROUP // head) + h
            scores = mm_nt(q[:, part], k[:, part]) + bias_ref[number]
            exponent = jnp.exp(scores - jnp.max(scores, axis=-1, keepdims=True))
            probs = exponent / jnp.sum(exponent, axis=-1, keepdims=True)
            probs_ref[number] = probs
            mixed.append(mm(probs.astype(BF), v[:, part]))
    perm = perm_ref[...]
    mixed_in_order = mm(jnp.concatenate(mixed, axis=1).astype(BF), perm).astype(BF)
    mixed_ref[...] = mixed_in_order[:, : model // 2]
    mixed_other_ref[...] = mixed_in_order[:, model // 2 :]
    middle = x_ref[...].astype(F32) + mm(mixed_in_order, wo[:, :model])
    middle_ref[...] = middle
    scale = lax.rsqrt(jnp.mean(middle * middle, axis=-1, keepdims=True) + EPSILON)
    ffn_in = (middle * scale * gain_ref[...]).astype(BF)
    router = mm(perm, wo[:, model:]).astype(BF)[:, :experts]
    router_ref[...] = router
    rows = mm(slots_ref[...], ffn_in).astype(BF)
    gate_ref[...] = gate_of(ffn_in, router, picked_ref[...])[1]
    half = rows.shape[0] // 2
    keep_ref[...] = rows[:half]
    send_ref[...] = rows[half:]


def join(refs, out_ref):
    base = 0
    for ref in refs:
        size = ref.shape[0]
        out_ref[base : base + size, :] = ref[...]
        base += size


def part_out(v, refs):
    base = 0
    for ref in refs:
        size = ref.shape[0]
        ref[...] = v[base : base + size]
        base += size


def load_kernel(after_ref, w1_ref, w2_ref, w1_out, w2_out, token_ref, sems):
    copies = []
    for ref, out_ref in ((w1_ref, w1_out), (w2_ref, w2_out)):
        rows = ref.shape[1] // 4
        for part in range(4):
            at = pl.ds(part * rows, rows)
            copies.append(pltpu.make_async_copy(ref.at[0, at], out_ref.at[at], sems.at[len(copies)]))
    for copy in copies:
        copy.start()
    token_ref[...] = jnp.zeros_like(token_ref)
    for copy in copies:
        copy.wait()


def hidden_grad_kernel(first_ref, second_ref, w2_ref, first_out, second_out):
    rows = first_ref.shape[0]
    dy = jnp.concatenate([first_ref[...], second_ref[...]], axis=0)
    width = first_out.shape[1] // 3
    for part in range(3):
        at = slice(part * width, (part + 1) * width)
        both = mm_nt(dy, w2_ref[at, :])
        first_out[:, at] = both[:rows]
        second_out[:, at] = both[rows:]


def expert_kernel(pieces, own_ref, *refs):
    rows_refs, dy = refs[:pieces], refs[pieces]
    router_ref, w1_ref, w2_ref, hidden_grad_ref = refs[pieces + 1 : pieces + 5]
    refs = refs[pieces + 5 :]
    back_refs, result_refs = refs[:pieces], refs[pieces : 2 * pieces]
    router_grad_ref, rows = refs[2 * pieces :]
    own = own_ref[0]
    join(rows_refs, rows)
    picked = one_lane((rows.shape[0], router_ref.shape[1]), own)
    router_probs, gate = gate_of(rows[...], router_ref[...], picked)
    result, back = 0.0, 0.0
    width = w1_ref.shape[1] // 2
    for part in range(2):
        at = slice(part * width, (part + 1) * width)
        hidden, slope = gelu_parts(mm(rows[...], w1_ref[:, at]))
        result += mm(hidden.astype(BF), w2_ref[at, :])
        pre_grad = (hidden_grad_ref[:, at] * gate * slope).astype(BF)
        back += mm_nt(pre_grad, w1_ref[:, at])
    returned = result.astype(BF)
    part_out(returned, result_refs)
    gate_grad = jnp.sum(dy[...].astype(F32) * returned.astype(F32), axis=-1, keepdims=True)
    logit_grad = (router_probs * (picked - gate) * gate_grad).astype(BF)
    router_grad_ref[...] = mm_tn(logit_grad, rows[...])
    part_out((back + mm_nt(logit_grad, router_ref[...])).astype(BF), back_refs)


def expert_grad_rows(pieces, refs, own_ref, router_ref, rows_all, branch_all):
    join(refs[:pieces], rows_all)
    join(refs[pieces:], branch_all)
    picked = one_lane((rows_all.shape[0], router_ref.shape[1]), own_ref[0])
    gate = gate_of(rows_all[...], router_ref[...], picked)[1]
    branch_all[...] = (branch_all[...].astype(F32) * gate).astype(BF)


def expert_grad_part(rows, branch, w1, w2):
    hidden, slope = gelu_parts(mm(rows, w1))
    pre_grad = (mm_nt(branch, w2) * slope).astype(BF)
    return mm_tn(rows, pre_grad), mm_tn(hidden.astype(BF), branch)


def first_expert_grad_kernel(pieces, own_ref, place_ref, *refs):
    router_ref, w1_ref, w2_ref, g1_ref, g2_ref, rows_all, branch_all = refs[2 * pieces :]
    expert_grad_rows(pieces, refs[: 2 * pieces], own_ref, router_ref, rows_all, branch_all)
    width = g1_ref.shape[1]
    for part in range(width // GROUP):
        at = pl.ds(pl.multiple_of(place_ref[0] * width + part * GROUP, GROUP), GROUP)
        here = slice(part * GROUP, (part + 1) * GROUP)
        g1, g2 = expert_grad_part(rows_all[...], branch_all[...], w1_ref[:, at], w2_ref[at, :])
        g1_ref[:, here] = g1
        g2_ref[here, :] = g2


def next_expert_grad_kernel(pieces, own_ref, place_ref, *refs):
    router_ref, w1_ref, w2_ref, before1_ref, before2_ref, g1_ref, g2_ref, rows_all, branch_all = refs[2 * pieces :]
    step = pl.program_id(0)

    @pl.when(step == 0)
    def _():
        expert_grad_rows(pieces, refs[: 2 * pieces], own_ref, router_ref, rows_all, branch_all)

    width = before1_ref.shape[1]
    at = pl.ds(pl.multiple_of(place_ref[0] * width + step * GROUP, GROUP), GROUP)
    here = pl.ds(pl.multiple_of(step * GROUP, GROUP), GROUP)
    g1, g2 = expert_grad_part(rows_all[...], branch_all[...], w1_ref[:, at], w2_ref[at, :])
    g1_ref[0] = g1 + before1_ref[:, here]
    g2_ref[0] = g2 + before2_ref[here, :]


def expert_grad_kernel(pieces, more, place_ref, *refs):
    del place_ref
    rows_refs, dy_refs, refs = refs[:pieces], refs[pieces : 2 * pieces], refs[2 * pieces :]
    own_ref, router_ref, w1_ref, w2_ref = refs[:4]
    g1_ref, g2_ref, rows_all, branch_all = refs[-4:]

    @pl.when(pl.program_id(0) == 0)
    def _():
        join(rows_refs, rows_all)
        join(dy_refs, branch_all)
        picked = one_lane((rows_all.shape[0], router_ref.shape[1]), own_ref[0])
        gate = gate_of(rows_all[...], router_ref[...], picked)[1]
        branch_all[...] = (branch_all[...].astype(F32) * gate).astype(BF)

    rows, branch = rows_all[...], branch_all[...]
    hidden, slope = gelu_parts(mm(rows, w1_ref[0]))
    pre_grad = (mm_nt(branch, w2_ref[0]) * slope).astype(BF)
    g1, g2 = mm_tn(rows, pre_grad), mm_tn(hidden.astype(BF), branch)
    if more:
        g1, g2 = g1 + refs[4][0], g2 + refs[5][0]
    g1_ref[0] = g1
    g2_ref[0] = g2


def middle_kernel(head, pieces, *refs):
    keep_refs, refs = refs[:pieces], refs[pieces:]
    (send_ref, slots_t_ref, dy_ref, middle_ref, gain_ref, perm_ref, probs_ref, other_ref) = refs[:8]
    ko_refs = refs[8:12]
    (middle_grad_ref, gain_grad_ref, mixed_grad_ref, grads_ref, wo, mixed_grad) = refs[12:]
    rows, model = dy_ref.shape
    step = pl.program_id(0)
    keep_rows = send_ref.shape[0] // pieces

    @pl.when(step == 0)
    def _():
        fill_y_first(ko_refs, wo, (model, model, 3 * model, model))
        back = jnp.concatenate([ref[:keep_rows, :] for ref in keep_refs] + [send_ref[...]], axis=0)
        ffn_grad = mm(slots_t_ref[...], back)
        middle = middle_ref[...]
        scale = lax.rsqrt(jnp.mean(middle * middle, axis=-1, keepdims=True) + EPSILON)
        gain_grad_ref[...] = jnp.sum(ffn_grad * middle * scale, axis=0, keepdims=True)
        scaled = ffn_grad * gain_ref[...]
        along = jnp.mean(scaled * middle, axis=-1, keepdims=True)
        middle_grad = dy_ref[...].astype(F32) + scale * scaled - middle * (scale * scale * scale * along)
        middle_grad_ref[...] = middle_grad
        attn_grad = middle_grad.astype(BF)
        grads_ref[rows : 2 * rows, :] = attn_grad
        grads_ref[2 * rows :, : model // 2] = other_ref[: rows // 2, :]
        grads_ref[2 * rows :, model // 2 :] = other_ref[rows // 2 :, :]
        in_order = mm_nt(attn_grad, wo[...]).astype(BF)
        every = mm_nt(in_order, perm_ref[...]).astype(BF)
        mixed_grad_ref[...] = every
        for g in range(mixed_grad.shape[0]):
            mixed_grad[g] = every[:, g * GROUP : (g + 1) * GROUP]

    grads = mixed_grad[step]
    parts = [
        mm_tn(probs_ref[h].astype(BF), grads[:, h * head : (h + 1) * head]) for h in range(GROUP // head)
    ]
    value_grad = jnp.concatenate(parts, axis=1).astype(BF)
    at = pl.ds(pl.multiple_of(step * GROUP, GROUP), GROUP)
    grads_ref[:rows, at] = value_grad


def weight_grad_kernel(normed_ref, side_ref, mixed_ref, vo_ref, vo_side_ref, qk_ref, qk_side_ref, *outs):
    a_ref, a_low_ref, b_ref, b_low_ref = outs
    rows = normed_ref.shape[0]
    width = side_ref.shape[1] // 2
    model = normed_ref.shape[1]
    half, part = width // 2, width // 4

    def unpack(v):
        return [v[:, :width], v[:, width:]]

    normed = jnp.concatenate([normed_ref[:, :width], *unpack(side_ref[...])], axis=0)
    mixed = jnp.concatenate([mixed_ref[...], *unpack(vo_side_ref[2 * rows :, :])], axis=0)
    for number, (left, own, side) in enumerate(
        ((normed, vo_ref, vo_side_ref), (normed, qk_ref, qk_side_ref), (mixed, vo_ref, vo_side_ref), (normed, qk_ref, qk_side_ref))
    ):
        here = slice(0, rows) if number < 2 else slice(rows, 2 * rows)
        total = mm_tn(left, jnp.concatenate([own[here, :], side[here, :]], axis=0))
        at = slice(number % 2 * model, (number % 2 + 1) * model)
        if number < 2:
            a_ref[:, at] = total[:half]
            a_low_ref[:, at] = total[half:].astype(BF)
        else:
            b_ref[:part, at] = total[:part]
            b_ref[part:, at] = total[half : half + part]
            b_low_ref[:part, at] = total[part:half].astype(BF)
            b_low_ref[part:, at] = total[half + part :].astype(BF)


def fold_near_kernel(a_ref, a_got_ref, b_ref, b_got_ref, small_ref, small_got_ref, a2_ref, a2_low_ref, b2_ref, b2_low_ref):
    a = a_ref[...] + a_got_ref[...].astype(F32)
    b = b_ref[...] + b_got_ref[...].astype(F32)
    small = small_ref[...] + small_got_ref[...]
    half = a.shape[0] // 2
    a2_ref[...] = a[:half]
    a2_low_ref[:half, :] = a[half:].astype(BF)
    a2_low_ref[half:, :] = jnp.concatenate([small, jnp.zeros_like(small)], axis=1).astype(BF)
    b2_ref[...] = b[:half]
    b2_low_ref[...] = b[half:].astype(BF)


def fold_sums(a_ref, a_low_ref, a_got_ref, b_ref, b_got_ref):
    rows = a_ref.shape[0]
    a = a_ref[...] + a_got_ref[:rows, :].astype(F32)
    b = b_ref[...] + b_got_ref[...].astype(F32)
    model = a.shape[1] // 2
    return a, b, a_low_ref[rows:, :model].astype(F32) + a_got_ref[rows:, :model].astype(F32)


def fold_far_kernel(a_ref, a_low_ref, a_got_ref, b_ref, b_got_ref, keep_ref, *low_refs):
    a, b, small = fold_sums(a_ref, a_low_ref, a_got_ref, b_ref, b_got_ref)
    model = a.shape[1] // 2
    shard = a.shape[0] // 4
    for k in range(4):
        rows = slice(k * shard, (k + 1) * shard)
        blocks = [v[rows, half * model : (half + 1) * model] for v in (a, b) for half in range(2)]
        if k:
            low_refs[k - 1][...] = jnp.concatenate([small, *blocks], axis=0).astype(BF)
        else:
            keep_ref[...] = jnp.concatenate(blocks, axis=0)


def fold_last_kernel(heads, device_ref, keep_ref, own_ref, *refs):
    got, outs = [ref[...].astype(F32) for ref in refs[:3]], refs[3:]
    shard = outs[0].shape[0]
    experts = outs[7].shape[0]
    first = got[0].shape[0] - 4 * shard
    total = keep_ref[...] + ((got[0][first:] + got[1][first:]) + got[2][first:])
    for number in range(4):
        outs[number][...] = total[number * shard : (number + 1) * shard]
    small = (own_ref[...][:first].astype(F32) + got[0][:first]) + (got[1][:first] + got[2][:first])
    outs[4][...] = small[experts]
    outs[5][...] = small[experts + 1]
    every = outs[6].shape[1]
    line = small[experts + 2 : experts + 3]
    outs[6][...] = jnp.concatenate([line[:, h * every : (h + 1) * every] for h in range(heads)], axis=0)
    spots = (small.shape[1], shard)
    mine = lax.broadcasted_iota(jnp.int32, spots, 0) == lax.broadcasted_iota(jnp.int32, spots, 1) + device_ref[0] * shard
    outs[7][...] = lax.dot_general(
        small[:experts], mine.astype(F32), (((1,), (0,)), ((), ())), precision=PRECISE, preferred_element_type=F32
    )


def score_grad_kernel(head, mixed_grad_ref, v_ref, q_ref, k_ref, probs_ref, grads_ref, along_ref):
    rows = q_ref.shape[0]
    flip = (
        lax.broadcasted_iota(jnp.int32, (rows, rows), 0) + lax.broadcasted_iota(jnp.int32, (rows, rows), 1)
        == rows - 1
    ).astype(F32).astype(BF)
    q_parts, k_parts = [], []
    for h in range(GROUP // head):
        part = slice(h * head, (h + 1) * head)
        probs = probs_ref[h]
        prob_grad = mm_nt(mixed_grad_ref[:, part], v_ref[:, part])
        inner = jnp.sum(probs * prob_grad, axis=-1, keepdims=True)
        score_grad = (probs * (prob_grad - inner)).astype(BF)
        q_parts.append(mm(score_grad, k_ref[:, part]))
        k_parts.append(mm_tn(score_grad, q_ref[:, part]))
        flipped = mm(flip, score_grad)
        half = rows // 2
        upper, lower = flipped[:half], flipped[half:]
        wide = jnp.concatenate(
            [upper[:, :half], upper[:, half:] + lower[:, :half], lower[:, half:], jnp.zeros_like(upper[:, :half])], axis=1
        )
        along_ref[h] = jnp.sum(pltpu.roll(wide, 0, 1, stride=1, stride_axis=0), axis=0, keepdims=True)
    grads_ref[:rows, :] = jnp.concatenate(q_parts, axis=1).astype(BF)
    grads_ref[rows:, :] = jnp.concatenate(k_parts, axis=1).astype(BF)


def input_kernel(table_rows, *refs):
    qk_ref, vo_ref, x_ref, gain_ref, perm_ref, middle_grad_ref = refs[:6]
    along_ref, buckets_ref, gain_next_ref, router_a_ref, router_b_ref = refs[6:11]
    qv_refs, wk_refs = refs[11:15], refs[15:19]
    input_grad_ref, small_ref, weight, wide = refs[19:]
    rows = x_ref.shape[0]
    experts, heads = router_a_ref.shape[0], along_ref.shape[0]
    every = table_rows
    onehot = (
        lax.broadcasted_iota(jnp.int32, (every, buckets_ref.shape[1]), 0) == buckets_ref[...]
    ).astype(F32)
    model = x_ref.shape[1]
    small_ref[...] = jnp.zeros_like(small_ref)
    small_ref[:experts, :] = router_a_ref[...] + router_b_ref[...]
    small_ref[experts + 1 : experts + 2, :] = gain_next_ref[...]
    along = jnp.concatenate([along_ref[h] for h in range(heads)], axis=0)
    table = lax.dot_general(
        along, onehot, (((1,), (1,)), ((), ())), precision=PRECISE, preferred_element_type=F32
    )
    small_ref[experts + 2 : experts + 3, : heads * every] = jnp.concatenate(
        [table[h : h + 1] for h in range(heads)], axis=1
    )
    fill_x_first(qv_refs, wide)
    total = mm_nt(jnp.concatenate([qk_ref[:rows, :], vo_ref[:rows, :]], axis=1), wide[...])
    fill_y_first(wk_refs, weight)
    total += mm_nt(qk_ref[rows:, :], weight[...])
    perm = perm_ref[...]
    high = total.astype(BF)
    low = (total - high.astype(F32)).astype(BF)
    normed_grad = mm_nt(high, perm) + mm_nt(low, perm)
    x = x_ref[...].astype(F32)
    scale = lax.rsqrt(jnp.mean(x * x, axis=-1, keepdims=True) + EPSILON)
    small_ref[experts : experts + 1, :] = jnp.sum(normed_grad * x * scale, axis=0, keepdims=True)
    scaled = normed_grad * gain_ref[...]
    along = jnp.mean(scaled * x, axis=-1, keepdims=True)
    input_grad_ref[...] = middle_grad_ref[...] + scale * scaled - x * (scale * scale * scale * along)


class Places:
    def __init__(self):
        self.experts = lax.axis_size("expert")
        self.nz = self.experts // 2
        self.dp = lax.axis_size("dp")
        self.near = self.nz == 4
        me = lax.axis_index("expert")
        self.z, self.c = me // 2, me % 2
        self.row = lax.axis_index("dp")
        self.columns = [[2 * z + c for z in range(self.nz)] for c in range(2)]

    def core(self, v):
        return lax.ppermute(v, "expert", [(i, i ^ 1) for i in range(self.experts)])

    def x(self, v):
        return lax.ppermute(v, "dp", [(i, i ^ 1) for i in range(self.dp)])

    def y(self, v):
        return lax.ppermute(v, "dp", [(i, i ^ 2) for i in range(self.dp)])

    def far(self, v, k):
        return lax.ppermute(v, "expert", [(i, i ^ (2 * k)) for i in range(self.experts)])

    def apart(self, v):
        return lax.all_to_all(
            v, "expert", split_axis=0, concat_axis=0, tiled=True, axis_index_groups=self.columns
        )

    def gather_z(self, v):
        if self.near:
            got = {k: self.far(v, k) for k in FAR_FIRST}
            return jnp.concatenate([v, got[1], got[2], got[3]], axis=0)
        return lax.all_gather(v, "expert", axis=0, tiled=True, axis_index_groups=self.columns)

    def z_order(self):
        steps = jnp.arange(self.nz, dtype=jnp.int32)
        return self.z ^ steps if self.near else steps

    def scatter_z(self, v):
        size = v.shape[0] // self.nz
        if self.near:
            total = v[:size]
            low = v.astype(BF)
            for k in FAR_FIRST:
                total = total + self.far(low[k * size : (k + 1) * size], k).astype(F32)
            return total
        got = self.apart(v.astype(BF).reshape(self.nz, size, v.shape[1]))
        mine = lax.dynamic_slice_in_dim(v, self.z * size, size, axis=0)
        steps = jnp.arange(self.nz, dtype=jnp.int32)[:, None, None]
        return mine + jnp.sum(jnp.where(steps == self.z, 0.0, got.astype(F32)), axis=0)

    def swap(self, blocks):
        got = {k: self.far(blocks[k], k) for k in FAR_FIRST}
        return [blocks[0], got[1], got[2], got[3]]

    def swap_relay(self, blocks, hold):
        size = blocks[0].shape[0]
        first = self.far(jnp.concatenate([blocks[2], blocks[3]], axis=0), 2)
        onward = after(jnp.concatenate([blocks[1], first[size:]], axis=0), *hold)
        second = self.far(onward, 1)
        return [blocks[0], second[:size], first[:size], second[size:]], onward

    def by_z(self, keep, got):
        room = keep.shape[0] // self.nz
        both = jnp.concatenate([v.reshape(self.nz, room, keep.shape[1]) for v in (keep, got)], axis=1)
        return [both[k] for k in range(4)] if self.near else both

    def halves(self, moved):
        moved = moved.reshape(-1, moved.shape[-1])
        half = moved.shape[0] // 2
        return [moved[:half]], [moved[half:]]

    def to_owners(self, keep, got, hold):
        blocks = self.by_z(keep, got)
        if self.near:
            blocks = all_after([blocks[k] for k in range(4)], *hold)
            two, one = self.far(blocks[2], 2), self.far(blocks[1], 1)
            three = self.far(after(blocks[3], two), 3)
            return [blocks[0], two], [one, three]
        return self.halves(self.apart(blocks))

    def send_more(self, blocks, k, hold):
        return self.far(after(blocks[k], *hold), k) if self.near else blocks

    def from_owners(self, first, second):
        width = first[0].shape[1]
        both = self.apart(jnp.concatenate([*first, *second], axis=0).reshape(self.nz, -1, width))
        room = both.shape[1] // 2
        return [both[:, :room].reshape(-1, width)], both[:, room:].reshape(-1, width)

    def to_senders(self, first, second):
        if self.near:
            two = self.far(first[1], 2)
            one, three = all_after(second, two)
            three, one = self.far(three, 3), self.far(one, 1)
            moved = [first[0], one, two, three]
            room = one.shape[0] // 2
            return moved, self.core(jnp.concatenate([v[room:] for v in moved], axis=0))
        keep, other = self.from_owners(first, second)
        return keep, self.core(other)

    def gather_far(self, a, b):
        return self.y(a), self.x(b)


def per_device(
    tokens,
    cotangent,
    routes,
    buckets,
    norm_attn,
    norm_ffn,
    rel_table,
    query_weight,
    key_weight,
    value_weight,
    out_weight,
    router_weight,
    expert_in,
    expert_out,
):
    at = Places()
    rows, model = tokens.shape
    head_count = rel_table.shape[1]
    head = model // head_count
    bucket_count = rel_table.shape[0]
    experts = router_weight.shape[1]
    shard = query_weight.shape[0]
    nz = at.nz
    room = max(2, 2 * rows // at.experts)
    slots = experts * room
    half = slots // 2
    groups = model // GROUP
    per_group = GROUP // head
    hidden = expert_in.shape[2]

    def in_hbm(*values):
        return [pltpu.with_memory_space_constraint(v, pltpu.HBM) for v in values]

    expert_in, expert_out = in_hbm(expert_in, expert_out)
    own = lax.axis_index("expert").astype(jnp.int32).reshape(1)
    smem = pl.BlockSpec(memory_space=pltpu.SMEM)

    core_of = at.c ^ jnp.arange(2, dtype=jnp.int32)
    row_of = at.row ^ jnp.arange(4, dtype=jnp.int32)
    device_of = (
        row_of[None, :, None] * at.experts + at.z_order()[None, None, :] * 2 + core_of[:, None, None]
    )
    order = (
        device_of[..., None] * shard + jnp.arange(shard, dtype=jnp.int32)
    ).reshape(1, model).astype(jnp.int32)

    shards = (query_weight, value_weight, key_weight, out_weight, router_weight.T)
    packed = pl.pallas_call(
        pack_kernel,
        out_shape=shape_of((shard, 4 * model + 128), BF),
        in_specs=[pl.BlockSpec(memory_space=pltpu.VMEM)] * 5,
        out_specs=pl.BlockSpec(memory_space=pltpu.VMEM),
        name="pack",
    )(*shards)
    line = at.gather_z(packed)
    span = 2 * rows
    bucket_line = jnp.pad(buckets, (0, 1), constant_values=-1).reshape(1, span)
    slots_map, slots_t, dy_keep, dy_send, perm, normed, picked, gain_attn, gain_ffn = pl.pallas_call(
        functools.partial(route_kernel, room, nz, at.near),
        out_shape=(
            shape_of((slots, rows), BF),
            shape_of((rows, slots), BF),
            shape_of((half, model), BF),
            shape_of((half + rows // 2, model), BF),
            shape_of((model, model), BF),
            shape_of((rows, model), BF),
            shape_of((rows, experts), F32),
            shape_of((1, model), F32),
            shape_of((1, model), F32),
        ),
        in_specs=[smem] + [pl.BlockSpec(memory_space=pltpu.VMEM)] * 6,
        compiler_params=params(),
        cost_estimate=cost(2 * rows * slots * model, 4 * rows * model),
        name="route",
    )(
        jnp.stack([at.z, at.c]).astype(jnp.int32),
        routes.reshape(1, rows),
        cotangent,
        order,
        tokens,
        norm_attn.reshape(1, model),
        norm_ffn.reshape(1, model),
    )
    dy_got = at.core(dy_send)
    normed_side = dy_got[half:]
    dy_got = dy_got[:half]
    qv, ko = line[:, : 2 * model], line[:, 2 * model :]
    qv, ko = all_after([qv, ko], slots_t)
    dy_keep, dy_got = all_after([dy_keep, dy_got], qv, ko)
    part_rows = qv.shape[0]
    dy_blocks = at.by_z(dy_keep, dy_got)
    dy_one = at.send_more(dy_blocks, 1, (dy_blocks,))
    bias = pl.pallas_call(
        bias_kernel,
        grid=(groups,),
        out_shape=shape_of((head_count, rows, rows), F32),
        in_specs=[full((1, span)), full((bucket_count, head_count))],
        out_specs=pl.BlockSpec((per_group, rows, rows), lambda g: (g, 0, 0)),
        scratch_shapes=[pltpu.VMEM((head_count, 1, span), F32)],
        compiler_params=params(),
        cost_estimate=cost(1 << 20, 4 * head_count * rows * rows),
        name="bias",
    )(after(bucket_line, slots_t), rel_table)
    qv_near, ko_near, both_near, qv_kept, ko_kept = pl.pallas_call(
        near_kernel,
        out_shape=tuple(pltpu.HBM((2 * part_rows, width), BF) for width in (2 * model, 2 * model + 128, 4 * model + 128))
        + tuple(shape_of((2 * part_rows, width), BF) for width in (2 * model, 2 * model + 128)),
        in_specs=[pl.BlockSpec(memory_space=pltpu.VMEM)] * 4,
        out_specs=tuple(pl.BlockSpec((2 * part_rows, width), lambda: (0, 0)) for width in (2 * model, 2 * model + 128, 4 * model + 128))
        + (pl.BlockSpec(memory_space=pltpu.VMEM),) * 2,
        compiler_params=params(),
        name="near",
    )(after(qv, dy_one, bias), at.x(qv), ko, at.y(ko))
    qv_far, ko_far = at.gather_far(qv_near, ko_near)
    w_first, w_second, loaded = pl.pallas_call(
        load_kernel,
        out_shape=(pltpu.VMEM((model, hidden), BF), pltpu.VMEM((hidden, model), BF), shape_of((8, 128), F32)),
        in_specs=[pl.BlockSpec(memory_space=pltpu.VMEM)] + [pl.BlockSpec(memory_space=pl.ANY)] * 2,
        out_specs=(pl.BlockSpec(memory_space=pltpu.VMEM),) * 3,
        scratch_shapes=[pltpu.SemaphoreType.DMA((8,))],
        compiler_params=params(),
        name="load",
    )(bias[0, :8, :128], expert_in, expert_out)
    both_side = at.core(both_near)
    dy_two = at.send_more(dy_blocks, 2, (qv_near, dy_one))
    qv_far, ko_far, dy_two = all_after([qv_far, ko_far, dy_two], both_side)
    dy_three = at.send_more(dy_blocks, 3, (qv_far, ko_far, dy_two))
    qv_pieces = (qv_kept, qv_far, both_side, at.core(qv_far))
    ko_pieces = (ko_kept, ko_far, both_side, at.core(ko_far))
    if at.near:
        dy_a = jnp.concatenate([dy_blocks[0], dy_two], axis=0)
    else:
        (dy_a,), (dy_b,) = at.halves(at.apart(dy_blocks))
    dy_a_later = after(dy_a, qv_far, ko_far)
    dy_ax, dy_ay = at.x(dy_a_later), at.y(dy_a_later)

    quarter = qv_near.shape[0]
    wide = ko_near.shape[1]
    side_wide = both_side.shape[1]
    head_block = pl.BlockSpec((per_group, rows, rows), lambda g: (g, 0, 0))
    in_vmem = pl.BlockSpec(memory_space=pltpu.VMEM)
    ko_full = [full((quarter, wide)), full((quarter, wide)), full((quarter, side_wide)), full((quarter, wide))]
    attend_shapes = [((rows, model), BF)] * 3 + [
        ((head_count, rows, rows), F32),
        ((rows, model // 2), BF),
        ((rows, model // 2), BF),
        ((rows, model), F32),
        ((model, experts), BF),
        ((rows, 1), F32),
        ((half, model), BF),
        ((half, model), BF),
    ]
    q, k, v, probs, mixed, mixed_other, middle, router, gate, keep, send = pl.pallas_call(
        functools.partial(attend_kernel, head),
        out_shape=tuple(pltpu.HBM(*v) if v[0] == (rows, 1) else shape_of(*v) for v in attend_shapes),
        in_specs=[in_vmem] * 3
        + [pl.BlockSpec((rows, model), lambda: (0, 0)), in_vmem]
        + [pl.BlockSpec((slots, rows), lambda: (0, 0)), pl.BlockSpec((rows, experts), lambda: (0, 0))]
        + [in_vmem] * 8,
        out_specs=(in_vmem,) * 8 + (pl.BlockSpec((rows, 1), lambda: (0, 0)),) + (in_vmem,) * 2,
        scratch_shapes=[
            pltpu.VMEM((model, 2 * model), BF),
            pltpu.VMEM((model, model), BF),
            pltpu.VMEM((model, wide - model), BF),
        ],
        compiler_params=params(),
        name="attend",
    )(
        normed,
        bias,
        perm,
        *in_hbm(tokens),
        after(gain_ffn, loaded),
        *in_hbm(slots_map, picked),
        *qv_pieces,
        *ko_pieces,
    )

    got = at.core(after(send, dy_three))
    first, second = at.to_owners(keep, got, (dy_ax, dy_ay))
    if at.near:
        dy_b = jnp.concatenate([dy_one, dy_three], axis=0)
    dy_b_later = after(dy_b, got, dy_ax, dy_ay)
    dy_by, dy_bx = at.y(dy_b_later), at.x(dy_b_later)
    hidden_grads = pl.pallas_call(
        hidden_grad_kernel,
        out_shape=(shape_of((half, hidden), F32),) * 2,
        in_specs=[in_vmem] * 3,
        out_specs=(in_vmem,) * 2,
        compiler_params=params(),
        name="hidden_grads",
    )(dy_a, dy_b, w_second)

    def expert(rows_list, dy_rows, hidden_grad, router_in):
        sizes = [v.shape[0] for v in rows_list]
        count = sum(sizes)
        shapes = [((n, model), BF) for n in sizes * 2] + [((experts, model), F32), ((count, model), BF)]
        outs = pl.pallas_call(
            functools.partial(expert_kernel, len(sizes)),
            out_shape=tuple(shape_of(*v) for v in shapes),
            in_specs=[smem] + [in_vmem] * (len(sizes) + 5),
            out_specs=(in_vmem,) * len(shapes),
            compiler_params=params(),
            name="expert",
        )(own, *rows_list, dy_rows, router_in, w_first, w_second, hidden_grad)
        n = len(sizes)
        return list(outs[:n]), list(outs[n : 2 * n]), outs[2 * n], outs[2 * n + 1]

    dy_ax_later, dy_by_later = all_after([dy_ax, dy_by], first[-1], dy_bx, hidden_grads[1])
    dy_axy, dy_byx = at.y(dy_ax_later), at.x(dy_by_later)
    back_a, returned_a, router_grad_a, rows_a = expert(first, dy_a, hidden_grads[0], after(router, dy_by, dy_bx))
    rows_ax, rows_ay = at.x(rows_a), at.y(rows_a)
    back_b, returned_b, router_grad_b, rows_b = expert(
        second, dy_b, hidden_grads[1], after(router, router_grad_a, dy_axy, dy_byx)
    )
    rows_b_later = after(rows_b, rows_ax, rows_ay)
    rows_by, rows_bx = at.y(rows_b_later), at.x(rows_b_later)
    back_keep, back_send = at.to_senders(back_a, back_b)

    slice_width = hidden // at.dp
    place = at.row.astype(jnp.int32).reshape(1)

    steps = slice_width // GROUP

    def expert_grads(rows_list, dy_list, router_in, before):
        sizes = [v.shape[0] for v in rows_list]
        count = sum(sizes)
        outs = (
            pl.BlockSpec((1, model, GROUP), lambda g, place: (0, 0, g)),
            pl.BlockSpec((1, GROUP, model), lambda g, place: (0, g, 0)),
        )
        return pl.pallas_call(
            functools.partial(expert_grad_kernel, len(sizes), bool(before)),
            grid_spec=pltpu.PrefetchScalarGridSpec(
                num_scalar_prefetch=1,
                grid=(steps,),
                in_specs=[full((n, model)) for n in sizes * 2]
                + [
                    smem,
                    full((model, experts)),
                    pl.BlockSpec((1, model, GROUP), lambda g, place: (0, 0, place[0] * steps + g)),
                    pl.BlockSpec((1, GROUP, model), lambda g, place: (0, place[0] * steps + g, 0)),
                ]
                + list(outs if before else ()),
                out_specs=outs,
                scratch_shapes=[pltpu.VMEM((count, model), BF), pltpu.VMEM((count, model), BF)],
            ),
            out_shape=(pltpu.HBM((1, model, slice_width), F32), pltpu.HBM((1, slice_width, model), F32)),
            compiler_params=params(),
            cost_estimate=cost(8 * count * model * slice_width, 20 * model * slice_width),
            name="expert_grads",
        )(place, *in_hbm(*rows_list, *dy_list), own, router_in, expert_in, expert_out, *in_hbm(*before))

    whole_vmem = pl.BlockSpec(memory_space=pltpu.VMEM)

    def first_expert_grads(rows_list, dy_list, router_in):
        count = sum(v.shape[0] for v in rows_list)
        ins = [*rows_list, *dy_list, router_in, w_first, w_second]
        return pl.pallas_call(
            functools.partial(first_expert_grad_kernel, len(rows_list)),
            out_shape=(shape_of((model, slice_width), F32), shape_of((slice_width, model), F32)),
            in_specs=[smem] * 2 + [whole_vmem] * len(ins),
            out_specs=(whole_vmem,) * 2,
            scratch_shapes=[pltpu.VMEM((count, model), BF)] * 2,
            compiler_params=params(24),
            name="expert_grads",
        )(own, place, *ins)

    def next_expert_grads(rows_list, dy_list, router_in, before):
        count = sum(v.shape[0] for v in rows_list)
        pieces = [*rows_list, *dy_list]
        return pl.pallas_call(
            functools.partial(next_expert_grad_kernel, len(rows_list)),
            grid=(slice_width // GROUP,),
            out_shape=(pltpu.HBM((1, model, slice_width), F32), pltpu.HBM((1, slice_width, model), F32)),
            in_specs=[smem] * 2 + [full(v.shape) for v in pieces] + [whole_vmem] * 5,
            out_specs=(
                pl.BlockSpec((1, model, GROUP), lambda g: (0, 0, g)),
                pl.BlockSpec((1, GROUP, model), lambda g: (0, g, 0)),
            ),
            scratch_shapes=[pltpu.VMEM((count, model), BF)] * 2,
            compiler_params=params(24),
            name="expert_grads",
        )(own, place, *in_hbm(*pieces), router_in, w_first, w_second, *before)

    rows_axy, rows_byx = at.y(after(rows_ax, rows_by, rows_bx, back_send)), at.x(after(rows_by, rows_bx, back_send))

    middle_grad, gain_ffn_grad, mixed_grad, vo_grads = pl.pallas_call(
        functools.partial(middle_kernel, head, len(back_keep)),
        grid=(groups,),
        out_shape=(
            shape_of((rows, model), F32),
            shape_of((1, model), F32),
            shape_of((rows, model), BF),
            shape_of((2 * rows + rows // 2, model), BF),
        ),
        in_specs=[full(v.shape) for v in back_keep]
        + [
            full((half, model)),
            full((rows, slots)),
            full((rows, model)),
            full((rows, model)),
            full((1, model)),
            full((model, model)),
            head_block,
            full((rows, model // 2)),
        ]
        + ko_full,
        out_specs=(
            full((rows, model)),
            full((1, model)),
            full((rows, model)),
            full((2 * rows + rows // 2, model)),
        ),
        scratch_shapes=[pltpu.VMEM((model, model), BF), pltpu.VMEM((groups, rows, GROUP), BF)],
        compiler_params=params(),
        cost_estimate=cost(10 * rows * model * model, 12 * model * model),
        name="middle",
    )(*back_keep, back_send, slots_t, cotangent, middle, after(gain_ffn, rows_by, rows_bx), perm, probs, mixed_other, *ko_pieces)
    vo_side = at.core(vo_grads)
    qk_grads, along_grad = pl.pallas_call(
        functools.partial(score_grad_kernel, head),
        grid=(groups,),
        out_shape=(shape_of((2 * rows, model), BF), shape_of((head_count, 1, span), F32)),
        in_specs=[cols(rows, GROUP)] * 4 + [head_block],
        out_specs=(cols(2 * rows, GROUP), pl.BlockSpec((per_group, 1, span), lambda g: (g, 0, 0))),
        compiler_params=params(),
        cost_estimate=cost(8 * rows * model * model, 12 * model * model),
        name="score_grads",
    )(mixed_grad, v, q, k, probs)
    qk_side = at.core(after(qk_grads, vo_side, rows_axy, rows_byx))
    small_rows = -(-(experts + 3) // 16) * 16
    input_grad, small = pl.pallas_call(
        functools.partial(input_kernel, bucket_count),
        grid=(1,),
        out_shape=(shape_of((rows, model), F32), shape_of((small_rows, model), F32)),
        in_specs=[full((2 * rows, model)), full((2 * rows + rows // 2, model))]
        + [full((rows, model)), full((1, model)), full((model, model)), full((rows, model))]
        + [full((head_count, 1, span)), full((1, span)), full((1, model))]
        + [full((experts, model))] * 2
        + [full((quarter, 2 * model))] * 4
        + [pl.BlockSpec((quarter, model), lambda g, at=at_k: (0, at)) for at_k in (0, 0, 2, 0)],
        out_specs=(full((rows, model)), full((small_rows, model))),
        scratch_shapes=[pltpu.VMEM((model, model), BF), pltpu.VMEM((model, 2 * model), BF)],
        compiler_params=params(),
        cost_estimate=cost(10 * rows * model * model, 12 * model * model),
        name="inputs",
    )(
        qk_grads,
        vo_grads,
        tokens,
        gain_attn,
        perm,
        middle_grad,
        along_grad,
        bucket_line,
        gain_ffn_grad,
        router_grad_a,
        router_grad_b,
        *qv_pieces,
        *ko_pieces,
    )
    quarter_rows = model // 4

    def vmem_call(kernel, name, shapes, *ins):
        return pl.pallas_call(
            kernel,
            out_shape=tuple(shape_of(*v) for v in shapes),
            in_specs=[pl.BlockSpec(v.shape, lambda: (0, 0)) for v in ins],
            out_specs=tuple(pl.BlockSpec(v[0], lambda: (0, 0)) for v in shapes),
            compiler_params=params(),
            name=name,
        )(*ins)

    pair = 2 * model
    a, a_low, b, b_low = vmem_call(
        weight_grad_kernel,
        "weight_grads",
        [((quarter_rows, pair), F32), ((quarter_rows, pair), BF)] * 2,
        normed,
        normed_side,
        mixed,
        vo_grads,
        vo_side,
        qk_grads,
        qk_side,
    )
    small = small + after(at.core(small), a_low)
    a_got, b_got = at.y(a_low), at.x(b_low)
    small_got = at.y(small)
    if at.near:
        home_two = at.far(after(returned_a[1], a_low, b_low), 2)
    else:
        home_two = at.apart(jnp.concatenate([*returned_a, *returned_b], axis=0).reshape(nz, -1, model))
    near_sums = first_expert_grads(
        [rows_a, rows_b, rows_ax, rows_by], [dy_a, dy_b, dy_ax, dy_by], after(router, a_low, b_low)
    )
    eighth = quarter_rows // 2
    a, a_low, b, b_low = vmem_call(
        fold_near_kernel,
        "fold_near",
        [((eighth, pair), F32), ((eighth + small_rows, pair), BF), ((eighth, pair), F32), ((eighth, pair), BF)],
        a,
        after(a_got, near_sums[0], home_two),
        b,
        b_got,
        small,
        small_got,
    )
    a_got, b_got = at.x(a_low), at.y(b_low)
    mid_sums = next_expert_grads([rows_ay, rows_bx], [dy_ay, dy_bx], after(router, a_low, b_low), near_sums)
    if at.near:
        home = [at.far(v, k) for v, k in zip(all_after([returned_b[1], returned_b[0]], a_low, b_low), (3, 1))]
        home_blocks = [returned_a[0], home[1], home_two, home[0]]
        room = half // nz
        returned_keep = home_blocks
        returned_other = jnp.concatenate([v[room:] for v in home_blocks], axis=0)
    else:
        room = home_two.shape[1] // 2
        returned_keep = [home_two[:, :room].reshape(half, model)]
        returned_other = home_two[:, room:].reshape(half, model)
    if at.near:
        keep_sum, *low = vmem_call(
            fold_far_kernel,
            "fold_far",
            [((4 * shard, model), F32)] + [((small_rows + 4 * shard, model), BF)] * 3,
            a,
            a_low,
            after(a_got, mid_sums[0], *home),
            b,
            b_got,
        )
        hold = keep_sum
        got_z = {k: at.far(low[k - 1], k) for k in FAR_FIRST}
    else:
        a = a + a_got[:eighth].astype(F32)
        b = b + b_got.astype(F32)
        summed = (a_low[eighth:].astype(F32) + a_got[eighth:].astype(F32))[:, :model]
        hold = jnp.concatenate([a, b], axis=1)
        sums = at.scatter_z(hold)
        grad_value, grad_query, grad_proj, grad_key = [sums[:, n * model : (n + 1) * model] for n in range(4)]
        summed = lax.psum(summed, "expert", axis_index_groups=at.columns)
    returned_send = at.core(after(returned_other, hold))
    grad_in, grad_out_w = expert_grads([rows_axy, rows_byx], [dy_axy, dy_byx], after(router, hold), mid_sums)
    keep_rows = half // len(returned_keep)
    expert_result = mm(
        slots_t,
        jnp.concatenate([v[:keep_rows] for v in returned_keep] + [returned_send], axis=0),
    )
    output = (middle + gate * expert_result).astype(BF)
    device = (at.row * at.experts + lax.axis_index("expert")).astype(jnp.int32)
    if at.near:
        last_ins = [after(keep_sum, output, grad_in), low[0], *[got_z[k] for k in (1, 2, 3)]]
        last_shapes = [(shard, model)] * 4 + [(model,)] * 2 + [(head_count, bucket_count), (experts, shard)]
        grad_value, grad_query, grad_proj, grad_key, gain_1, gain_2, table, router_t = pl.pallas_call(
            functools.partial(fold_last_kernel, head_count),
            out_shape=tuple(shape_of(v, F32) for v in last_shapes),
            in_specs=[smem] + [pl.BlockSpec(v.shape, lambda: (0, 0)) for v in last_ins],
            out_specs=tuple(pl.BlockSpec(v, (lambda: (0, 0)) if len(v) > 1 else (lambda: (0,))) for v in last_shapes),
            compiler_params=params(),
            name="fold_last",
        )(device.reshape(1), *last_ins)
    else:
        gain_1, gain_2 = summed[experts], summed[experts + 1]
        table = summed[experts + 2, : head_count * bucket_count].reshape(head_count, bucket_count)
        router_t = lax.dynamic_slice_in_dim(summed[:experts], device * shard, shard, axis=1)
    return (
        output,
        input_grad,
        gain_1.reshape(model),
        gain_2.reshape(model),
        table.T,
        grad_query,
        grad_key,
        grad_value,
        grad_proj,
        router_t.T,
        grad_in,
        grad_out_w,
    )


def solution(mesh):
    in_specs = (
        P(("dp", "expert"), None),
        P(("dp", "expert"), None),
        P(("dp", "expert"), None),
        P(),
        P(),
        P(),
        P(),
        P(("dp", "expert"), None),
        P(("dp", "expert"), None),
        P(("dp", "expert"), None),
        P(("dp", "expert"), None),
        P(("dp", "expert"), None),
        P("expert", None, None),
        P("expert", None, None),
    )
    out_specs = (
        P(("dp", "expert"), None),
        P(("dp", "expert"), None),
        P(),
        P(),
        P(),
        P(("dp", "expert"), None),
        P(("dp", "expert"), None),
        P(("dp", "expert"), None),
        P(("dp", "expert"), None),
        P(("dp", "expert"), None),
        P("expert", None, "dp"),
        P("expert", "dp", None),
    )
    return jax.shard_map(
        per_device, mesh=mesh, in_specs=in_specs, out_specs=out_specs, check_vma=False
    )
```
